128 devices in a mesh: dp: 2 (over core), node: 16 (over z, x), local: 4 (over y).
Axes of the slice: x: 4, y: 4, z: 4, core: 2. Of those that a mesh axis runs over, the one named last changes fastest.
Arguments:
- tokens: bfloat16 [16384, 3584], P(('dp', 'node', 'local')), parts along dimension 0, may hold values from -6 to 6
- gate_scores: float32 [16384, 4], P(('dp', 'node', 'local')), parts along dimension 0, may hold values from 0.1 to 1
- expert_ids: int32 [16384, 4], P(('dp', 'node', 'local')), parts along dimension 0, may hold values from 0 to 63, as said below
- w_gate: bfloat16 [64, 3584, 1024], P(('node', 'local')), may hold values from -0.09375 to 0.09375
- w_up: bfloat16 [64, 3584, 1024], P(('node', 'local')), may hold values from -0.09375 to 0.09375
- w_down: bfloat16 [64, 1024, 3584], P(('node', 'local')), may hold values from -0.1875 to 0.1875
Outputs:
- mixed: bfloat16 [16384, 3584], P(('dp', 'node', 'local')), parts along dimension 0
The draws below stay inside these ranges and needn't reach their ends.
There are 2 independent parts, one for each index of `dp`. The reference program is written for one: setup_inputs(seed, part) draws one part's arguments, and reference() takes and returns one part's arrays. A program takes and returns all parts, laid end to end along the dimension named above; an argument that names none is the same for every part. Nothing has to cross between parts.
Inputs may be any that keep to these rules, and one draw needn't show every extreme that they name: `expert_ids`: expert e belongs to node group e // 4 and lives on the device of index e along node and local together. Each token names 4 different experts in exactly 2 different node groups, at least one in each. The 128 tokens of one device name every node group exactly 16 times, and in every node group one expert is named by all 16 of them, so no expert is named more than 16 times by the tokens of one device.
All inputs are finite; a program needn't handle non-finite values.
Results may differ from the reference program's by a relative error of at most 0.0075.
Values may be sent and summed in bfloat16 or wider, within the bound.
No kernel may reach another device: no remote copies, remote signals or barrier semaphores. Data moves between devices by JAX's collectives and lax.ppermute only.
A program may use at most 192 MiB of HBM per device.

```python
import jax
import jax.numpy as jnp
from jax import lax

D = 3584
FF = 1024
TOP = 4
MAXNODES = 2
TOK_DEV = 128
EXPERTS = 64
CAP = 16
TOKENS = 8192
N_NODE = 16
N_LOCAL = 4


def draw_expert_ids(key, part):
    blocks = N_NODE * N_LOCAL
    key_nodes = jax.random.fold_in(key, 11)
    key_order = jax.random.fold_in(key, 12)
    key_hot_one = jax.random.fold_in(key, 13)
    key_hot_two = jax.random.fold_in(key, 14)
    key_pick = jax.random.fold_in(key, 15)
    node_keys = jax.random.randint(key_nodes, (blocks, N_NODE), 0, 1 << 20) * N_NODE + jnp.arange(N_NODE, dtype=jnp.int32)
    node_order = jnp.argsort(node_keys, axis=1).astype(jnp.int32)
    order_keys = jax.random.randint(key_order, (blocks, TOK_DEV), 0, 1 << 20) * TOK_DEV + jnp.arange(TOK_DEV, dtype=jnp.int32)
    token_order = jnp.argsort(order_keys, axis=1).astype(jnp.int32)
    node_slot = (token_order[:, :, None] * MAXNODES + jnp.arange(MAXNODES, dtype=jnp.int32)) % N_NODE
    node_table = jnp.broadcast_to(node_order[:, None, :], (blocks, TOK_DEV, N_NODE))
    chosen_nodes = jnp.take_along_axis(node_table, node_slot, axis=2)
    hot_local = jnp.minimum(jax.random.randint(key_hot_one, (blocks, N_NODE), 0, N_LOCAL), jax.random.randint(key_hot_two, (blocks, N_NODE), 0, N_LOCAL))
    hot_table = jnp.broadcast_to(hot_local[:, None, :], (blocks, TOK_DEV, N_NODE))
    hot_chosen = jnp.take_along_axis(hot_table, chosen_nodes, axis=2)
    local_range = jnp.arange(N_LOCAL, dtype=jnp.int32)
    candidates = (chosen_nodes[..., None] * N_LOCAL + local_range).reshape(blocks, TOK_DEV, MAXNODES * N_LOCAL)
    is_hot = (local_range == hot_chosen[..., None]).astype(jnp.int32).reshape(blocks, TOK_DEV, MAXNODES * N_LOCAL)
    scores = jax.random.randint(key_pick, (blocks, TOK_DEV, MAXNODES * N_LOCAL), 0, 1 << 20) * (MAXNODES * N_LOCAL)
    scores = scores + jnp.arange(MAXNODES * N_LOCAL, dtype=jnp.int32) + is_hot * (1 << 28)
    picked = lax.top_k(scores, TOP)[1]
    chosen_ids = jnp.take_along_axis(candidates, picked, axis=2)
    return chosen_ids.reshape(TOKENS, TOP).astype(jnp.int32)


def steps_of(stream_key, dims, cuts, smallest, top_value):
    def one(position, parts):
        steps = jax.random.uniform(jax.random.fold_in(jax.random.fold_in(stream_key, 6), position), (parts,), jnp.float32, smallest / len(cuts), top_value / len(cuts))
        return jnp.repeat(jnp.exp(steps), dims[position] // parts).reshape((-1,) + (1,) * (len(dims) - position - 1))

    loudness = one(*cuts[0])
    for cut in cuts[1:]:
        loudness = loudness * one(*cut)
    return loudness


def gaussian(key, shape, deviation, bound, pieces=(), kind=jnp.bfloat16):
    factor_of = steps_of(key, shape, pieces, -0.22, 0.18) if pieces else 1.0
    values = jax.random.normal(key, shape, jnp.float32) * deviation * factor_of
    return jnp.minimum(jnp.maximum(values, -bound), bound).astype(kind)


def setup_inputs(seed: int = 0, part: int = 0) -> dict:
    arg_keys = jax.random.split(jax.random.key(seed), 7)
    own_keys = jax.random.split(jax.random.fold_in(arg_keys[6], part), 7)
    return {
        "tokens": gaussian(own_keys[0], (TOKENS, D), 1.0, 6.0, ((0, 64),)),
        "gate_scores": jnp.clip(0.1 + 0.9 * jax.random.uniform(own_keys[1], (TOKENS, TOP), jnp.float32) ** steps_of(own_keys[1], (TOKENS, TOP), ((0, 64),), -0.2, 0.2), 0.1, 1.0),
        "expert_ids": draw_expert_ids(jax.random.fold_in(jax.random.fold_in(arg_keys[6], part), 71), part),
        "w_gate": gaussian(arg_keys[3], (EXPERTS, D, FF), D ** -0.5, 0.09375, ((0, 64),)),
        "w_up": gaussian(arg_keys[4], (EXPERTS, D, FF), D ** -0.5, 0.09375, ((0, 64),)),
        "w_down": gaussian(arg_keys[5], (EXPERTS, FF, D), FF ** -0.5, 0.1875, ((0, 64),)),
    }


def quantize(tokens):
    count_rows, width = tokens.shape
    tiles = tokens.astype(jnp.float32).reshape(count_rows, width // 128, 128)
    largest = jnp.max(jnp.abs(tiles), axis=-1)
    tile_scale = ((largest + 1e-6) / 448.0).astype(jnp.bfloat16)
    scale_wide = lax.optimization_barrier(tile_scale).astype(jnp.float32)
    quantized = (tiles / scale_wide[..., None]).astype(jnp.bfloat16)
    return quantized.reshape(count_rows, width), tile_scale


def restore(quantized, tile_scale):
    dims_all = quantized.shape
    tiles = quantized.reshape(dims_all[:-1] + (dims_all[-1] // 128, 128)).astype(jnp.float32)
    return (tiles * tile_scale.astype(jnp.float32)[..., None]).reshape(dims_all).astype(jnp.bfloat16)


def expert_rows(row_block, gate_matrix, up_matrix, down_matrix):
    gate_act = jnp.dot(row_block, gate_matrix, preferred_element_type=jnp.float32)
    up_act = jnp.dot(row_block, up_matrix, preferred_element_type=jnp.float32)
    hidden = (jax.nn.silu(gate_act) * up_act).astype(jnp.bfloat16)
    return jnp.dot(hidden, down_matrix, preferred_element_type=jnp.float32).astype(jnp.bfloat16)


def reference(tokens, gate_scores, expert_ids, w_gate, w_up, w_down):
    quantized, tile_scale = quantize(tokens)
    restored = restore(quantized, tile_scale)
    gates = (2.5 * gate_scores / jnp.sum(gate_scores, axis=-1, keepdims=True)).astype(jnp.bfloat16)
    gate_flat = lax.optimization_barrier(gates).astype(jnp.float32).reshape(-1)
    flat_ids = expert_ids.reshape(-1).astype(jnp.int32)
    sorted_pos = jnp.argsort(flat_ids, stable=True).astype(jnp.int32)
    expert_load = jnp.sum((flat_ids[None, :] == jnp.arange(EXPERTS, dtype=jnp.int32)[:, None]).astype(jnp.int32), axis=1).astype(jnp.int32)
    expert_start = (jnp.cumsum(expert_load) - expert_load).astype(jnp.int32)
    most_rows = EXPERTS * CAP
    padded_pos = jnp.concatenate([sorted_pos, jnp.zeros((most_rows,), jnp.int32)])

    def one_expert(total, expert):
        flat_pos = lax.dynamic_slice(padded_pos, (expert_start[expert],), (most_rows,)).astype(jnp.int32)
        is_live = jnp.arange(most_rows, dtype=jnp.int32) < expert_load[expert]
        token_pos = (flat_pos // TOP).astype(jnp.int32)
        result = expert_rows(restored[token_pos], w_gate[expert], w_up[expert], w_down[expert])
        weight = jnp.where(is_live, gate_flat[flat_pos], jnp.zeros_like(gate_flat[flat_pos]))
        return total.at[token_pos].add(result.astype(jnp.float32) * weight[:, None]), None

    mixed, unused = lax.scan(one_expert, jnp.zeros((TOKENS, D), jnp.float32), jnp.arange(EXPERTS, dtype=jnp.int32))
    return mixed.astype(jnp.bfloat16)
```

```python
import functools

import jax
import jax.numpy as jnp
from jax import lax
from jax.experimental import pallas as pl
from jax.experimental.pallas import tpu as pltpu
from jax.sharding import PartitionSpec as P

LANES = 128
PIECE = 128
VMEM = 60 * 1024 * 1024


def slot_maps(ids_t, groups, per_group):
    slots, tokens = groups * per_group, ids_t.shape[1]
    slot = lax.broadcasted_iota(jnp.int32, (slots, tokens), 0)
    half_rows = per_group // 2
    half = slots // 2
    group = (slot % half) // half_rows
    rank = (slot // half) * half_rows + slot % half_rows
    named = jnp.zeros((slots, tokens), jnp.bool_)
    for k in range(ids_t.shape[0]):
        named = named | (ids_t[k : k + 1, :] // 4 == group)
    before = lax.broadcasted_iota(jnp.int32, (tokens, tokens), 0) < lax.broadcasted_iota(
        jnp.int32, (tokens, tokens), 1
    )
    earlier = jnp.dot(
        named.astype(jnp.bfloat16), before.astype(jnp.bfloat16), preferred_element_type=jnp.float32
    )
    mine = named & (earlier == rank.astype(jnp.float32))
    return mine, group


def prepare_kernel(locals_, groups, per_group, tok, scores_t, ids_t, out_a, out_b, pick):
    ids = ids_t[...]
    mine, group = slot_maps(ids, groups, per_group)
    onehot = mine.astype(jnp.bfloat16)
    pick[...] = onehot
    score = scores_t[...]
    total = score[0:1, :]
    for k in range(1, score.shape[0]):
        total = total + score[k : k + 1, :]
    gates = (2.5 * score / total).astype(jnp.bfloat16).astype(jnp.float32)
    width = tok.shape[1]
    lane = lax.broadcasted_iota(jnp.int32, (mine.shape[0], LANES), 1)
    meta = jnp.zeros((mine.shape[0], LANES), jnp.float32)
    for j in range(locals_):
        value = jnp.zeros(mine.shape, jnp.float32)
        for k in range(ids.shape[0]):
            value = value + jnp.where(
                mine & (ids[k : k + 1, :] == group * locals_ + j), gates[k : k + 1, :], 0.0
            )
        meta = jnp.where(lane == j, jnp.sum(value, axis=1, keepdims=True), meta)
    meta = meta.astype(jnp.bfloat16)
    half = mine.shape[0] // 2
    out_a[:, width : width + LANES] = meta[:half]
    out_b[:, width : width + LANES] = meta[half:]
    for j in range(width // LANES):
        cols = slice(j * LANES, (j + 1) * LANES)
        x = tok[:, cols].astype(jnp.float32)
        largest = jnp.max(jnp.abs(x), axis=1, keepdims=True)
        scale = ((largest + 1e-06) / 448.0).astype(jnp.bfloat16).astype(jnp.float32)
        quantized = (x / scale).astype(jnp.bfloat16).astype(jnp.float32)
        restored = (quantized * scale).astype(jnp.bfloat16)
        rows = jnp.dot(onehot, restored, preferred_element_type=jnp.float32).astype(jnp.bfloat16)
        out_a[:, cols] = rows[:half]
        out_b[:, cols] = rows[half:]


def prepare(tokens, gate_scores, expert_ids, groups, locals_):
    count, width = tokens.shape
    per_group = 2 * count // groups
    half = groups * per_group // 2
    return pl.pallas_call(
        functools.partial(prepare_kernel, locals_, groups, per_group),
        out_shape=[
            jax.ShapeDtypeStruct((half, width + LANES), jnp.bfloat16),
            jax.ShapeDtypeStruct((half, width + LANES), jnp.bfloat16),
            jax.ShapeDtypeStruct((2 * half, count), jnp.bfloat16),
        ],
        compiler_params=pltpu.CompilerParams(vmem_limit_bytes=VMEM),
        cost_estimate=pl.CostEstimate(flops=10**9, bytes_accessed=3 * 10**6, transcendentals=0),
    )(tokens, gate_scores.T, expert_ids.T)


def expert_kernel(blocks, local_ref, *refs):
    xs, (wg, wu, wd), outs = refs[:blocks], refs[blocks : blocks + 3], refs[blocks + 3 : 2 * blocks + 3]
    rows, acc = refs[2 * blocks + 3 :]
    step, steps = pl.program_id(0), pl.num_programs(0)
    width = rows.shape[1]
    piece = xs[0].shape[0]

    @pl.when(step == 0)
    def _():
        for b in range(blocks):
            rows[b * piece : (b + 1) * piece, :] = xs[b][:, :width]

    x = rows[...]
    gate = jnp.dot(x, wg[0], preferred_element_type=jnp.float32)
    up = jnp.dot(x, wu[0], preferred_element_type=jnp.float32)
    hidden = (gate / (1.0 + jnp.exp(-gate)) * up).astype(jnp.bfloat16)
    part = jnp.dot(hidden, wd[0], preferred_element_type=jnp.float32)

    @pl.when(step == 0)
    def _():
        acc[...] = part

    @pl.when((step > 0) & (step < steps - 1))
    def _():
        acc[...] += part

    @pl.when(step == steps - 1)
    def _():
        for b in range(blocks):
            meta = xs[b][:, width : width + LANES].astype(jnp.float32)
            lane = lax.broadcasted_iota(jnp.int32, meta.shape, 1)
            weight = jnp.sum(jnp.where(lane == local_ref[0], meta, 0.0), axis=1, keepdims=True)
            own = slice(b * piece, (b + 1) * piece)
            outs[b][...] = ((acc[own, :] + part[own, :]) * weight).astype(jnp.bfloat16)


def experts(xs, local, w_gate, w_up, w_down, tile=256):
    blocks = len(xs)
    piece, wide = xs[0].shape
    width, hidden = w_gate.shape[1:]
    return pl.pallas_call(
        functools.partial(expert_kernel, blocks),
        grid=(hidden // tile,),
        in_specs=[pl.BlockSpec(memory_space=pltpu.SMEM)]
        + [pl.BlockSpec((piece, wide), lambda i: (0, 0))] * blocks
        + [
            pl.BlockSpec((1, width, tile), lambda i: (0, 0, i)),
            pl.BlockSpec((1, width, tile), lambda i: (0, 0, i)),
            pl.BlockSpec((1, tile, width), lambda i: (0, i, 0)),
        ],
        out_specs=[pl.BlockSpec((piece, width), lambda i: (0, 0))] * blocks,
        out_shape=[jax.ShapeDtypeStruct((piece, width), jnp.bfloat16)] * blocks,
        scratch_shapes=[
            pltpu.VMEM((blocks * piece, width), jnp.bfloat16),
            pltpu.VMEM((blocks * piece, width), jnp.float32),
        ],
        compiler_params=pltpu.CompilerParams(
            vmem_limit_bytes=VMEM, dimension_semantics=("arbitrary",)
        ),
        cost_estimate=pl.CostEstimate(
            flops=6 * blocks * piece * width * hidden,
            bytes_accessed=6 * width * hidden,
            transcendentals=blocks * piece * hidden,
        ),
    )(local, *xs, w_gate, w_up, w_down)


def collect_kernel(pick, first, second, out):
    half = first.shape[0]
    dims = (((0,), (0,)), ((), ()))
    total = lax.dot_general(pick[:half, :], first[...], dims, preferred_element_type=jnp.float32)
    total = total + lax.dot_general(
        pick[half:, :], second[...], dims, preferred_element_type=jnp.float32
    )
    out[...] = total.astype(jnp.bfloat16)


def collect(pick, first, second):
    return pl.pallas_call(
        collect_kernel,
        out_shape=jax.ShapeDtypeStruct((pick.shape[1], first.shape[1]), jnp.bfloat16),
        compiler_params=pltpu.CompilerParams(vmem_limit_bytes=VMEM),
        cost_estimate=pl.CostEstimate(flops=3 * 10**8, bytes_accessed=3 * 10**6, transcendentals=0),
    )(pick, first, second)


def per_device(tokens, gate_scores, expert_ids, w_gate, w_up, w_down):
    groups, locals_ = lax.axis_size("node"), lax.axis_size("local")
    local = lax.axis_index("local").astype(jnp.int32).reshape(1)

    def across(block):
        parts = block.reshape(groups, block.shape[0] // groups, block.shape[1])
        return lax.all_to_all(parts, "node", 0, 0, tiled=True).reshape(block.shape)

    def up(block):
        return lax.ppermute(block, "local", [(i, (i + 1) % locals_) for i in range(locals_)])

    def down(block):
        return lax.ppermute(block, "local", [(i, (i - 1) % locals_) for i in range(locals_)])

    def add(*blocks):
        total = blocks[0].astype(jnp.float32)
        for block in blocks[1:]:
            total = total + block.astype(jnp.float32)
        return total.astype(jnp.bfloat16)

    run = functools.partial(experts, local=local, w_gate=w_gate, w_up=w_up, w_down=w_down)

    send_a, send_b, pick = prepare(tokens, gate_scores, expert_ids, groups, locals_)
    own_a = across(send_a)
    below_a, above_a = up(own_a), down(own_a)
    own_b = across(send_b)
    far_a, above_b = up(below_a), down(own_b)
    below_b, far_b = up(own_b), down(above_b)

    own_pa, below_pa, above_pa = run([own_a, below_a, above_a])
    far_pa, own_pb, above_pb = run([far_a, own_b, above_b])
    below_pb, far_pb = run([below_b, far_b])

    back_far_a, back_above_a = down(far_pa), up(above_pa)
    back_near_a, back_far_b = down(add(back_far_a, below_pa)), up(far_pb)
    total_a = add(own_pa, back_above_a, back_near_a)
    back_below_b, back_near_b = down(below_pb), up(add(back_far_b, above_pb))
    final_a = across(total_a)
    final_b = across(add(own_pb, back_below_b, back_near_b))
    return collect(pick, final_a, final_b)


def solution(mesh):
    in_specs = (
        P(("dp", "node", "local"), None),
        P(("dp", "node", "local"), None),
        P(("dp", "node", "local"), None),
        P(("node", "local"), None, None),
        P(("node", "local"), None, None),
        P(("node", "local"), None, None),
    )
    out_specs = P(("dp", "node", "local"), None)
    return jax.shard_map(
        per_device, mesh=mesh, in_specs=in_specs, out_specs=out_specs, check_vma=False
    )
```

```python
import functools

import jax
import jax.numpy as jnp
from jax import lax
from jax.experimental import pallas as pl
from jax.experimental.pallas import tpu as pltpu
from jax.sharding import PartitionSpec as P

LANES = 128
PIECE = 128
VMEM = 60 * 1024 * 1024
NEAR_TILES = 14


def slot_maps(ids_t, groups, per_group):
    slots, tokens = groups * per_group, ids_t.shape[1]
    slot = lax.broadcasted_iota(jnp.int32, (slots, tokens), 0)
    half_rows = per_group // 2
    half = slots // 2
    group = (slot % half) // half_rows
    rank = (slot // half) * half_rows + slot % half_rows
    named = jnp.zeros((slots, tokens), jnp.bool_)
    for k in range(ids_t.shape[0]):
        named = named | (ids_t[k : k + 1, :] // 4 == group)
    before = lax.broadcasted_iota(jnp.int32, (tokens, tokens), 0) < lax.broadcasted_iota(
        jnp.int32, (tokens, tokens), 1
    )
    earlier = jnp.dot(
        named.astype(jnp.bfloat16), before.astype(jnp.bfloat16), preferred_element_type=jnp.float32
    )
    mine = named & (earlier == rank.astype(jnp.float32))
    return mine, group


def prepare_kernel(locals_, groups, per_group, tok, scores_t, ids_t, out_a, out_b, pick):
    ids = ids_t[...]
    mine, group = slot_maps(ids, groups, per_group)
    onehot = mine.astype(jnp.bfloat16)
    pick[...] = onehot
    score = scores_t[...]
    total = score[0:1, :]
    for k in range(1, score.shape[0]):
        total = total + score[k : k + 1, :]
    gates = (2.5 * score / total).astype(jnp.bfloat16).astype(jnp.float32)
    width = tok.shape[1]
    lane = lax.broadcasted_iota(jnp.int32, (mine.shape[0], LANES), 1)
    meta = jnp.zeros((mine.shape[0], LANES), jnp.float32)
    for j in range(locals_):
        value = jnp.zeros(mine.shape, jnp.float32)
        for k in range(ids.shape[0]):
            value = value + jnp.where(
                mine & (ids[k : k + 1, :] == group * locals_ + j), gates[k : k + 1, :], 0.0
            )
        meta = jnp.where(lane == j, jnp.sum(value, axis=1, keepdims=True), meta)
    meta = meta.astype(jnp.bfloat16)
    half = mine.shape[0] // 2
    out_a[:, width : width + LANES] = meta[:half]
    out_b[:, width : width + LANES] = meta[half:]
    for j in range(width // LANES):
        cols = slice(j * LANES, (j + 1) * LANES)
        x = tok[:, cols].astype(jnp.float32)
        largest = jnp.max(jnp.abs(x), axis=1, keepdims=True)
        scale = ((largest + 1e-06) / 448.0).astype(jnp.bfloat16).astype(jnp.float32)
        quantized = (x / scale).astype(jnp.bfloat16).astype(jnp.float32)
        restored = (quantized * scale).astype(jnp.bfloat16)
        rows = jnp.dot(onehot, restored, preferred_element_type=jnp.float32).astype(jnp.bfloat16)
        out_a[:, cols] = rows[:half]
        out_b[:, cols] = rows[half:]


def prepare(tokens, gate_scores, expert_ids, groups, locals_):
    count, width = tokens.shape
    per_group = 2 * count // groups
    half = groups * per_group // 2
    return pl.pallas_call(
        functools.partial(prepare_kernel, locals_, groups, per_group),
        out_shape=[
            jax.ShapeDtypeStruct((half, width + LANES), jnp.bfloat16),
            jax.ShapeDtypeStruct((half, width + LANES), jnp.bfloat16),
            jax.ShapeDtypeStruct((2 * half, count), jnp.bfloat16),
        ],
        compiler_params=pltpu.CompilerParams(vmem_limit_bytes=VMEM),
        cost_estimate=pl.CostEstimate(flops=10**9, bytes_accessed=3 * 10**6, transcendentals=0),
    )(tokens, gate_scores.T, expert_ids.T)


def expert_kernel(blocks, local_ref, *refs):
    xs, (wg, wu, wd), refs = refs[:blocks], refs[blocks : blocks + 3], refs[blocks + 3 :]
    outs, direct, rows, acc = refs[:blocks], refs[blocks], refs[blocks + 1], refs[blocks + 2]
    step, steps = pl.program_id(0), pl.num_programs(0)
    width, near = rows.shape[1], outs[0].shape[1]
    piece = xs[0].shape[0]

    @pl.when(step == 0)
    def _():
        for b in range(blocks):
            rows[b * piece : (b + 1) * piece, :] = xs[b][:, :width]

    x = rows[...]
    gate = jnp.dot(x, wg[0], preferred_element_type=jnp.float32)
    up = jnp.dot(x, wu[0], preferred_element_type=jnp.float32)
    hidden = (gate / (1.0 + jnp.exp(-gate)) * up).astype(jnp.bfloat16)
    part = jnp.dot(hidden, wd[0], preferred_element_type=jnp.float32)

    @pl.when(step == 0)
    def _():
        acc[...] = part

    @pl.when((step > 0) & (step < steps - 1))
    def _():
        acc[...] += part

    @pl.when(step == steps - 1)
    def _():
        for b in range(blocks):
            meta = xs[b][:, width : width + LANES].astype(jnp.float32)
            lane = lax.broadcasted_iota(jnp.int32, meta.shape, 1)
            weight = jnp.sum(jnp.where(lane == local_ref[0], meta, 0.0), axis=1, keepdims=True)
            own = slice(b * piece, (b + 1) * piece)
            value = (acc[own, :] + part[own, :]) * weight
            outs[b][...] = value[:, :near].astype(jnp.bfloat16)
            far = value[:, near:]
            direct[:, b] = far.reshape(direct.shape[0], direct.shape[2], far.shape[1]).astype(
                jnp.bfloat16
            )


def experts(xs, local, groups, near, w_gate, w_up, w_down, tile=256):
    blocks = len(xs)
    piece, wide = xs[0].shape
    width, hidden = w_gate.shape[1:]
    direct = (groups, blocks, piece // groups, width - near)
    return pl.pallas_call(
        functools.partial(expert_kernel, blocks),
        grid=(hidden // tile,),
        in_specs=[pl.BlockSpec(memory_space=pltpu.SMEM)]
        + [pl.BlockSpec((piece, wide), lambda i: (0, 0))] * blocks
        + [
            pl.BlockSpec((1, width, tile), lambda i: (0, 0, i)),
            pl.BlockSpec((1, width, tile), lambda i: (0, 0, i)),
            pl.BlockSpec((1, tile, width), lambda i: (0, i, 0)),
        ],
        out_specs=[pl.BlockSpec((piece, near), lambda i: (0, 0))] * blocks
        + [pl.BlockSpec(direct, lambda i: (0, 0, 0, 0))],
        out_shape=[jax.ShapeDtypeStruct((piece, near), jnp.bfloat16)] * blocks
        + [jax.ShapeDtypeStruct(direct, jnp.bfloat16)],
        scratch_shapes=[
            pltpu.VMEM((blocks * piece, width), jnp.bfloat16),
            pltpu.VMEM((blocks * piece, width), jnp.float32),
        ],
        compiler_params=pltpu.CompilerParams(
            vmem_limit_bytes=VMEM, dimension_semantics=("arbitrary",)
        ),
        cost_estimate=pl.CostEstimate(
            flops=6 * blocks * piece * width * hidden,
            bytes_accessed=6 * width * hidden,
            transcendentals=blocks * piece * hidden,
        ),
    )(local, *xs, w_gate, w_up, w_down)


def whole(kernel, shapes, *arrays):
    moved = sum(x.size * x.dtype.itemsize for x in arrays)
    return pl.pallas_call(
        kernel,
        out_shape=shapes,
        compiler_params=pltpu.CompilerParams(vmem_limit_bytes=VMEM),
        cost_estimate=pl.CostEstimate(flops=10**8, bytes_accessed=3 * moved, transcendentals=0),
    )(*arrays)


def to_tokens(pick, rows):
    return lax.dot_general(pick, rows, (((0,), (0,)), ((), ())), preferred_element_type=jnp.float32)


def scatter_kernel(where, picks, first, second, third, own, below, above, far_lo, far_hi):
    groups = (first, second, third)
    width = first.shape[-1]
    for name, out in (("own", own), ("below", below), ("above", above), ("far", None)):
        pick = picks[("own", "below", "above", "far").index(name)]
        total = None
        for half in range(2):
            which, place = where[name, half]
            rows = groups[which][:, place].reshape(PIECE, width)
            part = to_tokens(pick[half * PIECE : (half + 1) * PIECE, :], rows)
            total = part if total is None else total + part
        total = total.astype(jnp.bfloat16)
        if out is not None:
            out[...] = total
        else:
            far_lo[...] = total[: far_lo.shape[0]]
            far_hi[...] = total[far_lo.shape[0] :]


def collect_kernel(pick, first, second, own, below_lo, below_hi, above_lo, above_hi, out):
    near = first.shape[1]
    half = own.shape[0] // 2
    total = to_tokens(pick[:PIECE, :], first[...]) + to_tokens(pick[PIECE:, :], second[...])
    out[:, :near] = total.astype(jnp.bfloat16)
    for place, below, above in ((0, below_lo, above_lo), (half, below_hi, above_hi)):
        rows = slice(place, place + half)
        total = own[rows, :].astype(jnp.float32) + below[...].astype(jnp.float32)
        out[rows, near:] = (total + above[...].astype(jnp.float32)).astype(jnp.bfloat16)


def per_device(tokens, gate_scores, expert_ids, w_gate, w_up, w_down):
    groups, locals_ = lax.axis_size("node"), lax.axis_size("local")
    local = lax.axis_index("local").astype(jnp.int32).reshape(1)
    count, width = tokens.shape
    near = NEAR_TILES * LANES

    def across(block):
        parts = block.reshape(groups, block.shape[0] // groups, block.shape[1])
        return lax.all_to_all(parts, "node", 0, 0, tiled=True).reshape(block.shape)

    def up(block):
        return lax.ppermute(block, "local", [(i, (i + 1) % locals_) for i in range(locals_)])

    def down(block):
        return lax.ppermute(block, "local", [(i, (i - 1) % locals_) for i in range(locals_)])

    def add(*blocks):
        total = blocks[0].astype(jnp.float32)
        for block in blocks[1:]:
            total = total + block.astype(jnp.float32)
        return total.astype(jnp.bfloat16)

    run = functools.partial(
        experts, local=local, groups=groups, near=near, w_gate=w_gate, w_up=w_up, w_down=w_down
    )

    send_a, send_b, pick = prepare(tokens, gate_scores, expert_ids, groups, locals_)
    own_a = across(send_a)
    below_a, above_a = up(own_a), down(own_a)
    own_b = across(send_b)
    far_a, above_b = up(below_a), down(own_b)
    below_b, far_b = up(own_b), down(above_b)
    pick_below, pick_above = up(pick), down(pick)
    pick_far = up(pick_below)

    own_pa, below_pa, above_pa, first = run([own_a, below_a, above_a])
    far_a, own_b, above_b, own_pa = lax.optimization_barrier((far_a, own_b, above_b, own_pa))
    far_pa, own_pb, above_pb, second = run([far_a, own_b, above_b])
    below_b, far_b, own_pb = lax.optimization_barrier((below_b, far_b, own_pb))
    below_pb, far_pb, third = run([below_b, far_b])

    home = [lax.all_to_all(x, "node", 0, 0, tiled=True) for x in (first, second, third)]

    back_far_a, back_above_a = down(far_pa), up(above_pa)
    back_near_a, back_far_b = down(add(back_far_a, below_pa)), up(far_pb)
    total_a = add(own_pa, back_above_a, back_near_a)
    back_below_b, back_near_b = down(below_pb), up(add(back_far_b, above_pb))
    final_a = across(total_a)
    final_b = across(add(own_pb, back_below_b, back_near_b))

    where = {
        ("own", 0): (0, 0), ("below", 0): (0, 1), ("above", 0): (0, 2),
        ("far", 0): (1, 0), ("own", 1): (1, 1), ("above", 1): (1, 2),
        ("below", 1): (2, 0), ("far", 1): (2, 1),
    }
    full = jax.ShapeDtypeStruct((count, width - near), jnp.bfloat16)
    part = jax.ShapeDtypeStruct((count // 2, width - near), jnp.bfloat16)

    def scatter(p0, p1, p2, p3, *refs):
        scatter_kernel(where, (p0, p1, p2, p3), *refs)

    own_t, below_t, above_t, far_lo, far_hi = whole(
        scatter, [full, full, full, part, part], pick, pick_below, pick_above, pick_far, *home
    )
    half = count // 2
    more_lo, more_hi = down(far_lo), up(far_hi)
    below_hi, above_lo = down(below_t[half:]), up(above_t[:half])
    below_lo, above_hi = down(add(below_t[:half], more_lo)), up(add(above_t[half:], more_hi))
    return whole(
        collect_kernel,
        jax.ShapeDtypeStruct((count, width), jnp.bfloat16),
        pick, final_a, final_b, own_t, below_lo, below_hi, above_lo, above_hi,
    )


def solution(mesh):
    in_specs = (
        P(("dp", "node", "local"), None),
        P(("dp", "node", "local"), None),
        P(("dp", "node", "local"), None),
        P(("node", "local"), None, None),
        P(("node", "local"), None, None),
        P(("node", "local"), None, None),
    )
    out_specs = P(("dp", "node", "local"), None)
    return jax.shard_map(
        per_device, mesh=mesh, in_specs=in_specs, out_specs=out_specs, check_vma=False
    )
```

```python
import functools

import jax
import jax.numpy as jnp
from jax import lax
from jax.experimental import pallas as pl
from jax.experimental.pallas import tpu as pltpu
from jax.sharding import PartitionSpec as P

LANES = 128
PIECE = 128
VMEM = 60 * 1024 * 1024
NEAR_TILES = 16


def slot_maps(ids_t, groups, per_group):
    slots, tokens = groups * per_group, ids_t.shape[1]
    slot = lax.broadcasted_iota(jnp.int32, (slots, tokens), 0)
    group, rank = slot // per_group, slot % per_group
    named = jnp.zeros((slots, tokens), jnp.bool_)
    for k in range(ids_t.shape[0]):
        named = named | (ids_t[k : k + 1, :] // 4 == group)
    before = lax.broadcasted_iota(jnp.int32, (tokens, tokens), 0) < lax.broadcasted_iota(
        jnp.int32, (tokens, tokens), 1
    )
    earlier = jnp.dot(
        named.astype(jnp.bfloat16), before.astype(jnp.bfloat16), preferred_element_type=jnp.float32
    )
    mine = named & (earlier == rank.astype(jnp.float32))
    return mine, group


def prepare_kernel(locals_, groups, per_group, tok, scores_t, ids_t, out, pick):
    ids = ids_t[...]
    mine, group = slot_maps(ids, groups, per_group)
    onehot = mine.astype(jnp.bfloat16)
    pick[...] = onehot
    score = scores_t[...]
    total = score[0:1, :]
    for k in range(1, score.shape[0]):
        total = total + score[k : k + 1, :]
    gates = (2.5 * score / total).astype(jnp.bfloat16).astype(jnp.float32)
    width = tok.shape[1]
    lane = lax.broadcasted_iota(jnp.int32, (mine.shape[0], LANES), 1)
    meta = jnp.zeros((mine.shape[0], LANES), jnp.float32)
    for j in range(locals_):
        value = jnp.zeros(mine.shape, jnp.float32)
        for k in range(ids.shape[0]):
            value = value + jnp.where(
                mine & (ids[k : k + 1, :] == group * locals_ + j), gates[k : k + 1, :], 0.0
            )
        meta = jnp.where(lane == j, jnp.sum(value, axis=1, keepdims=True), meta)
    token = lax.broadcasted_iota(jnp.int32, mine.shape, 1).astype(jnp.float32)
    token = jnp.sum(jnp.where(mine, token, 0.0), axis=1, keepdims=True)
    meta = jnp.where(lane == locals_, token, meta)
    out[:, width : width + LANES] = meta.astype(jnp.bfloat16)
    for j in range(width // LANES):
        cols = slice(j * LANES, (j + 1) * LANES)
        x = tok[:, cols].astype(jnp.float32)
        largest = jnp.max(jnp.abs(x), axis=1, keepdims=True)
        scale = ((largest + 1e-06) / 448.0).astype(jnp.bfloat16).astype(jnp.float32)
        quantized = (x / scale).astype(jnp.bfloat16).astype(jnp.float32)
        restored = (quantized * scale).astype(jnp.bfloat16)
        rows = jnp.dot(onehot, restored, preferred_element_type=jnp.float32)
        out[:, cols] = rows.astype(jnp.bfloat16)


def prepare(tokens, gate_scores, expert_ids, groups, locals_):
    count, width = tokens.shape
    per_group = 2 * count // groups
    slots = groups * per_group
    return pl.pallas_call(
        functools.partial(prepare_kernel, locals_, groups, per_group),
        out_shape=[
            jax.ShapeDtypeStruct((slots, width + LANES), jnp.bfloat16),
            jax.ShapeDtypeStruct((slots, count), jnp.bfloat16),
        ],
        compiler_params=pltpu.CompilerParams(vmem_limit_bytes=VMEM),
        cost_estimate=pl.CostEstimate(flops=10**9, bytes_accessed=3 * 10**6, transcendentals=0),
    )(tokens, gate_scores.T, expert_ids.T)


def expert_kernel(blocks, local_ref, *refs):
    xs, (wg, wu, wd), refs = refs[:blocks], refs[blocks : blocks + 3], refs[blocks + 3 :]
    outs, direct, rows, acc = refs[:blocks], refs[blocks], refs[blocks + 1], refs[blocks + 2]
    step, steps = pl.program_id(0), pl.num_programs(0)
    width, near = rows.shape[1], outs[0].shape[1]
    piece = xs[0].shape[0]

    @pl.when(step == 0)
    def _():
        for b in range(blocks):
            rows[b * piece : (b + 1) * piece, :] = xs[b][:, :width]

    x = rows[...]
    gate = jnp.dot(x, wg[0], preferred_element_type=jnp.float32)
    up = jnp.dot(x, wu[0], preferred_element_type=jnp.float32)
    hidden = (gate / (1.0 + jnp.exp(-gate)) * up).astype(jnp.bfloat16)
    part = jnp.dot(hidden, wd[0], preferred_element_type=jnp.float32)

    @pl.when(step == 0)
    def _():
        acc[...] = part

    @pl.when((step > 0) & (step < steps - 1))
    def _():
        acc[...] += part

    @pl.when(step == steps - 1)
    def _():
        for b in range(blocks):
            meta = xs[b][:, width : width + LANES].astype(jnp.float32)
            lane = lax.broadcasted_iota(jnp.int32, meta.shape, 1)
            weight = jnp.sum(jnp.where(lane == local_ref[0], meta, 0.0), axis=1, keepdims=True)
            own = slice(b * piece, (b + 1) * piece)
            value = (acc[own, :] + part[own, :]) * weight
            outs[b][...] = value[:, :near].astype(jnp.bfloat16)
            far = value[:, near:]
            shape = direct.shape[0], direct.shape[2]
            direct[:, b, :, : far.shape[1]] = far.reshape(*shape, far.shape[1]).astype(jnp.bfloat16)
            direct[:, b, :, far.shape[1] :] = meta.reshape(*shape, LANES).astype(jnp.bfloat16)


def experts(xs, local, groups, near, w_gate, w_up, w_down, tile=256):
    blocks = len(xs)
    piece, wide = xs[0].shape
    width, hidden = w_gate.shape[1:]
    direct = (groups, blocks, piece // groups, width - near + LANES)
    return pl.pallas_call(
        functools.partial(expert_kernel, blocks),
        grid=(hidden // tile,),
        in_specs=[pl.BlockSpec(memory_space=pltpu.SMEM)]
        + [pl.BlockSpec((piece, wide), lambda i: (0, 0))] * blocks
        + [
            pl.BlockSpec((1, width, tile), lambda i: (0, 0, i)),
            pl.BlockSpec((1, width, tile), lambda i: (0, 0, i)),
            pl.BlockSpec((1, tile, width), lambda i: (0, i, 0)),
        ],
        out_specs=[pl.BlockSpec((piece, near), lambda i: (0, 0))] * blocks
        + [pl.BlockSpec(direct, lambda i: (0, 0, 0, 0))],
        out_shape=[jax.ShapeDtypeStruct((piece, near), jnp.bfloat16)] * blocks
        + [jax.ShapeDtypeStruct(direct, jnp.bfloat16)],
        scratch_shapes=[
            pltpu.VMEM((blocks * piece, width), jnp.bfloat16),
            pltpu.VMEM((blocks * piece, width), jnp.float32),
        ],
        compiler_params=pltpu.CompilerParams(
            vmem_limit_bytes=VMEM, dimension_semantics=("arbitrary",)
        ),
        cost_estimate=pl.CostEstimate(
            flops=6 * blocks * piece * width * hidden,
            bytes_accessed=6 * width * hidden,
            transcendentals=blocks * piece * hidden,
        ),
    )(local, *xs, w_gate, w_up, w_down)


def whole(kernel, shapes, *arrays):
    moved = sum(x.size * x.dtype.itemsize for x in arrays)
    return pl.pallas_call(
        kernel,
        out_shape=shapes,
        compiler_params=pltpu.CompilerParams(vmem_limit_bytes=VMEM),
        cost_estimate=pl.CostEstimate(flops=10**8, bytes_accessed=3 * moved, transcendentals=0),
    )(*arrays)


def to_tokens(pick, rows):
    return lax.dot_general(pick, rows, (((0,), (0,)), ((), ())), preferred_element_type=jnp.float32)


def scatter_kernel(where, locals_, first, second, third, own, below, above, far_lo, far_hi):
    groups = (first, second, third)
    count, width = own.shape
    half = count // 2
    for name, out in (("own", own), ("below", below), ("above", above), ("far", None)):
        total = None
        for which, place in where[name]:
            rows = groups[which][:, place].reshape(PIECE, width + LANES)
            meta = rows[:, width:].astype(jnp.float32)
            lane = lax.broadcasted_iota(jnp.int32, meta.shape, 1)
            token = jnp.sum(jnp.where(lane == locals_, meta, 0.0), axis=1, keepdims=True)
            lane = lax.broadcasted_iota(jnp.int32, (PIECE, count), 1)
            pick = (lane.astype(jnp.float32) == token).astype(jnp.bfloat16)
            part = to_tokens(pick, rows[:, :width])
            total = part if total is None else total + part
        total = total.astype(jnp.bfloat16)
        if out is not None:
            out[...] = total
        else:
            far_lo[...] = total[:half]
            far_hi[...] = total[half:]


def pack_kernel(back_a, below_a, below_b, back_b, above_a, above_b, down, up):
    def both(x, y):
        return (x[...].astype(jnp.float32) + y[...].astype(jnp.float32)).astype(jnp.bfloat16)

    down[0] = both(back_a, below_a)
    down[1] = below_b[...]
    up[0] = above_a[...]
    up[1] = both(back_b, above_b)


def total_kernel(own_a, own_b, above, below, out):
    for half, own in enumerate((own_a, own_b)):
        total = own[...].astype(jnp.float32) + above[half].astype(jnp.float32)
        total = total + below[half].astype(jnp.float32)
        shape = out.shape[0], out.shape[2], out.shape[3]
        out[:, half] = total.reshape(shape).astype(jnp.bfloat16)


def join_kernel(below, more_lo, above, more_hi, out_down, out_up):
    half = more_lo.shape[0]

    def plus(x, y):
        return (x.astype(jnp.float32) + y.astype(jnp.float32)).astype(jnp.bfloat16)

    out_down[:half, :] = plus(below[:half, :], more_lo[...])
    out_down[half:, :] = below[half:, :]
    out_up[:half, :] = above[:half, :]
    out_up[half:, :] = plus(above[half:, :], more_hi[...])


def collect_kernel(pick, rows, own, from_above, from_below, out):
    near = rows.shape[1]
    out[:, :near] = to_tokens(pick[...], rows[...]).astype(jnp.bfloat16)
    total = own[...].astype(jnp.float32) + from_above[...].astype(jnp.float32)
    out[:, near:] = (total + from_below[...].astype(jnp.float32)).astype(jnp.bfloat16)


def per_device(tokens, gate_scores, expert_ids, w_gate, w_up, w_down):
    groups, locals_ = lax.axis_size("node"), lax.axis_size("local")
    local = lax.axis_index("local").astype(jnp.int32).reshape(1)
    count, width = tokens.shape
    near = NEAR_TILES * LANES
    tie = lax.optimization_barrier

    def across(block):
        return lax.all_to_all(block, "node", 0, 0, tiled=True)

    def up(block):
        return lax.ppermute(block, "local", [(i, (i + 1) % locals_) for i in range(locals_)])

    def down(block):
        return lax.ppermute(block, "local", [(i, (i - 1) % locals_) for i in range(locals_)])

    def like(*shape):
        return jax.ShapeDtypeStruct(shape, jnp.bfloat16)

    run = functools.partial(
        experts, local=local, groups=groups, near=near, w_gate=w_gate, w_up=w_up, w_down=w_down
    )

    send, pick = prepare(tokens, gate_scores, expert_ids, groups, locals_)
    eight = PIECE // groups
    own = across(send.reshape(groups, 2, eight, width + LANES))
    own_a = own[:, 0].reshape(PIECE, width + LANES)
    own_b = own[:, 1].reshape(PIECE, width + LANES)
    below_a, above_b = up(own_a), down(own_b)
    far_a, far_b = up(below_a), down(above_b)
    last_a, last_b, _, _ = tie((own_a, own_b, far_a, far_b))
    below_b, above_a = up(last_b), down(last_a)

    own_pa, own_pb, first = run([own_a, own_b])
    below_a, above_b, far_a, far_b, first = tie((below_a, above_b, far_a, far_b, first))
    below_pa, above_pb, far_pa, far_pb, second = run([below_a, above_b, far_a, far_b])
    below_b, above_a, second = tie((below_b, above_a, second))
    below_pb, above_pa, third = run([below_b, above_a])

    first = across(first)
    second, first = tie((second, first))
    second = across(second)
    third, second = tie((third, second))
    third = across(third)

    back_a, back_b = down(far_pa), up(far_pb)
    go_down, go_up = whole(
        pack_kernel, [like(2, PIECE, near)] * 2, back_a, below_pa, below_pb, back_b, above_pa, above_pb
    )
    from_above, from_below = down(go_down), up(go_up)
    total = whole(
        total_kernel, like(groups, 2, eight, near), own_pa, own_pb, from_above, from_below
    )
    final = across(total).reshape(2 * PIECE, near)

    where = {
        "own": ((0, 0), (0, 1)), "below": ((1, 0), (2, 0)), "above": ((2, 1), (1, 1)), "far": ((1, 2), (1, 3)),
    }
    full, part = like(count, width - near), like(count // 2, width - near)
    own_t, below_t, above_t, far_lo, far_hi = whole(
        functools.partial(scatter_kernel, where, locals_), [full, full, full, part, part], first, second, third
    )
    more_lo, more_hi = down(far_lo), up(far_hi)
    go_down, go_up = whole(join_kernel, [full, full], below_t, more_lo, above_t, more_hi)
    from_above, from_below = down(go_down), up(go_up)
    return whole(collect_kernel, like(count, width), pick, final, own_t, from_above, from_below)


def solution(mesh):
    in_specs = (
        P(("dp", "node", "local"), None),
        P(("dp", "node", "local"), None),
        P(("dp", "node", "local"), None),
        P(("node", "local"), None, None),
        P(("node", "local"), None, None),
        P(("node", "local"), None, None),
    )
    out_specs = P(("dp", "node", "local"), None)
    return jax.shard_map(
        per_device, mesh=mesh, in_specs=in_specs, out_specs=out_specs, check_vma=False
    )
```

```python
import functools

import jax
import jax.numpy as jnp
from jax import lax
from jax.experimental import pallas as pl
from jax.experimental.pallas import tpu as pltpu
from jax.sharding import PartitionSpec as P

LANES = 128
PIECE = 128
VMEM = 60 * 1024 * 1024
NEAR_TILES = 16


def slot_maps(ids_t, groups, per_group):
    slots, tokens = groups * per_group, ids_t.shape[1]
    slot = lax.broadcasted_iota(jnp.int32, (slots, tokens), 0)
    group, rank = slot // per_group, slot % per_group
    named = jnp.zeros((slots, tokens), jnp.bool_)
    for k in range(ids_t.shape[0]):
        named = named | (ids_t[k : k + 1, :] // 4 == group)
    before = lax.broadcasted_iota(jnp.int32, (tokens, tokens), 0) < lax.broadcasted_iota(
        jnp.int32, (tokens, tokens), 1
    )
    earlier = jnp.dot(
        named.astype(jnp.bfloat16), before.astype(jnp.bfloat16), preferred_element_type=jnp.float32
    )
    mine = named & (earlier == rank.astype(jnp.float32))
    return mine, group


def prepare_kernel(locals_, groups, per_group, tok, scores_t, ids_t, out, pick):
    ids = ids_t[...]
    mine, group = slot_maps(ids, groups, per_group)
    onehot = mine.astype(jnp.bfloat16)
    pick[...] = onehot
    score = scores_t[...]
    total = score[0:1, :]
    for k in range(1, score.shape[0]):
        total = total + score[k : k + 1, :]
    gates = (2.5 * score / total).astype(jnp.bfloat16).astype(jnp.float32)
    width = tok.shape[1]
    lane = lax.broadcasted_iota(jnp.int32, (mine.shape[0], LANES), 1)
    meta = jnp.zeros((mine.shape[0], LANES), jnp.float32)
    for j in range(locals_):
        value = jnp.zeros(mine.shape, jnp.float32)
        for k in range(ids.shape[0]):
            value = value + jnp.where(
                mine & (ids[k : k + 1, :] == group * locals_ + j), gates[k : k + 1, :], 0.0
            )
        meta = jnp.where(lane == j, jnp.sum(value, axis=1, keepdims=True), meta)
    token = lax.broadcasted_iota(jnp.int32, mine.shape, 1).astype(jnp.float32)
    token = jnp.sum(jnp.where(mine, token, 0.0), axis=1, keepdims=True)
    meta = jnp.where(lane == locals_, token, meta)
    out[:, width : width + LANES] = meta.astype(jnp.bfloat16)
    for j in range(width // LANES):
        cols = slice(j * LANES, (j + 1) * LANES)
        x = tok[:, cols].astype(jnp.float32)
        largest = jnp.max(jnp.abs(x), axis=1, keepdims=True)
        scale = ((largest + 1e-06) / 448.0).astype(jnp.bfloat16).astype(jnp.float32)
        quantized = (x / scale).astype(jnp.bfloat16).astype(jnp.float32)
        restored = (quantized * scale).astype(jnp.bfloat16)
        rows = jnp.dot(onehot, restored, preferred_element_type=jnp.float32)
        out[:, cols] = rows.astype(jnp.bfloat16)


def prepare(tokens, gate_scores, expert_ids, groups, locals_):
    count, width = tokens.shape
    per_group = 2 * count // groups
    slots = groups * per_group
    return pl.pallas_call(
        functools.partial(prepare_kernel, locals_, groups, per_group),
        out_shape=[
            jax.ShapeDtypeStruct((slots, width + LANES), jnp.bfloat16),
            jax.ShapeDtypeStruct((slots, count), jnp.bfloat16),
        ],
        compiler_params=pltpu.CompilerParams(vmem_limit_bytes=VMEM),
        cost_estimate=pl.CostEstimate(flops=10**9, bytes_accessed=3 * 10**6, transcendentals=0),
    )(tokens, gate_scores.T, expert_ids.T)


def expert_kernel(blocks, before, local_ref, *refs):
    xs, (wg, wu, wd), refs = refs[:blocks], refs[blocks : blocks + 3], refs[blocks + 3 + before :]
    outs, direct, rows, acc = refs[:blocks], refs[blocks], refs[blocks + 1], refs[blocks + 2]
    step, steps = pl.program_id(0), pl.num_programs(0)
    width, near = rows.shape[1], outs[0].shape[1]
    piece = xs[0].shape[0]

    @pl.when(step == 0)
    def _():
        for b in range(blocks):
            rows[b * piece : (b + 1) * piece, :] = xs[b][:, :width]

    x = rows[...]
    gate = jnp.dot(x, wg[0], preferred_element_type=jnp.float32)
    up = jnp.dot(x, wu[0], preferred_element_type=jnp.float32)
    hidden = (gate / (1.0 + jnp.exp(-gate)) * up).astype(jnp.bfloat16)
    part = jnp.dot(hidden, wd[0], preferred_element_type=jnp.float32)

    @pl.when(step == 0)
    def _():
        acc[...] = part

    @pl.when((step > 0) & (step < steps - 1))
    def _():
        acc[...] += part

    @pl.when(step == steps - 1)
    def _():
        for b in range(blocks):
            meta = xs[b][:, width : width + LANES].astype(jnp.float32)
            lane = lax.broadcasted_iota(jnp.int32, meta.shape, 1)
            weight = jnp.sum(jnp.where(lane == local_ref[0], meta, 0.0), axis=1, keepdims=True)
            own = slice(b * piece, (b + 1) * piece)
            value = (acc[own, :] + part[own, :]) * weight
            outs[b][...] = value[:, :near].astype(jnp.bfloat16)
            far = value[:, near:]
            shape = direct.shape[0], direct.shape[2]
            direct[:, b, :, : far.shape[1]] = far.reshape(*shape, far.shape[1]).astype(jnp.bfloat16)
            direct[:, b, :, far.shape[1] :] = meta.reshape(*shape, LANES).astype(jnp.bfloat16)


def experts(xs, held, local, groups, near, w_gate, w_up, w_down, tile=256):
    blocks = len(xs)
    piece, wide = xs[0].shape
    width, hidden = w_gate.shape[1:]
    before = 0 if held is None else 1
    direct = (groups, blocks, piece // groups, width - near + LANES)
    room = jax.ShapeDtypeStruct((groups, 2 * blocks) + direct[2:], jnp.bfloat16)
    return pl.pallas_call(
        functools.partial(expert_kernel, blocks, before),
        grid=(hidden // tile,),
        in_specs=[pl.BlockSpec(memory_space=pltpu.SMEM)]
        + [pl.BlockSpec((piece, wide), lambda i: (0, 0))] * blocks
        + [
            pl.BlockSpec((1, width, tile), lambda i: (0, 0, i)),
            pl.BlockSpec((1, width, tile), lambda i: (0, 0, i)),
            pl.BlockSpec((1, tile, width), lambda i: (0, i, 0)),
        ]
        + [pl.BlockSpec(memory_space=pl.ANY)] * before,
        out_specs=[pl.BlockSpec((piece, near), lambda i: (0, 0))] * blocks
        + [pl.BlockSpec(direct, lambda i: (0, before, 0, 0))],
        out_shape=[jax.ShapeDtypeStruct((piece, near), jnp.bfloat16)] * blocks
        + [room],
        input_output_aliases={blocks + 4: blocks} if before else {},
        scratch_shapes=[
            pltpu.VMEM((blocks * piece, width), jnp.bfloat16),
            pltpu.VMEM((blocks * piece, width), jnp.float32),
        ],
        compiler_params=pltpu.CompilerParams(
            vmem_limit_bytes=VMEM, dimension_semantics=("arbitrary",)
        ),
        cost_estimate=pl.CostEstimate(
            flops=6 * blocks * piece * width * hidden,
            bytes_accessed=6 * width * hidden,
            transcendentals=blocks * piece * hidden,
        ),
    )(local, *xs, w_gate, w_up, w_down, *([held] if before else []))


def whole(kernel, shapes, *arrays):
    moved = sum(x.size * x.dtype.itemsize for x in arrays)
    return pl.pallas_call(
        kernel,
        out_shape=shapes,
        compiler_params=pltpu.CompilerParams(vmem_limit_bytes=VMEM),
        cost_estimate=pl.CostEstimate(flops=10**8, bytes_accessed=3 * moved, transcendentals=0),
    )(*arrays)


def to_tokens(pick, rows):
    return lax.dot_general(pick, rows, (((0,), (0,)), ((), ())), preferred_element_type=jnp.float32)


def scatter_kernel(where, locals_, first, second, own, below, above, far_lo, far_hi):
    groups = (first, second)
    count, width = own.shape
    half = count // 2
    for name, out in (("own", own), ("below", below), ("above", above), ("far", None)):
        total = None
        for which, place in where[name]:
            rows = groups[which][:, place].reshape(PIECE, width + LANES)
            meta = rows[:, width:].astype(jnp.float32)
            lane = lax.broadcasted_iota(jnp.int32, meta.shape, 1)
            token = jnp.sum(jnp.where(lane == locals_, meta, 0.0), axis=1, keepdims=True)
            lane = lax.broadcasted_iota(jnp.int32, (PIECE, count), 1)
            pick = (lane.astype(jnp.float32) == token).astype(jnp.bfloat16)
            part = to_tokens(pick, rows[:, :width])
            total = part if total is None else total + part
        total = total.astype(jnp.bfloat16)
        if out is not None:
            out[...] = total
        else:
            far_lo[...] = total[:half]
            far_hi[...] = total[half:]


def pack_kernel(back_a, below_a, below_b, back_b, above_a, above_b, down, up):
    def both(x, y):
        return (x[...].astype(jnp.float32) + y[...].astype(jnp.float32)).astype(jnp.bfloat16)

    down[0] = both(back_a, below_a)
    down[1] = below_b[...]
    up[0] = above_a[...]
    up[1] = both(back_b, above_b)


def total_kernel(own_a, own_b, above, below, out):
    for half, own in enumerate((own_a, own_b)):
        total = own[...].astype(jnp.float32) + above[half].astype(jnp.float32)
        total = total + below[half].astype(jnp.float32)
        shape = out.shape[0], out.shape[2], out.shape[3]
        out[:, half] = total.reshape(shape).astype(jnp.bfloat16)


def join_kernel(below, more_lo, above, more_hi, out_down, out_up):
    half = more_lo.shape[0]

    def plus(x, y):
        return (x.astype(jnp.float32) + y.astype(jnp.float32)).astype(jnp.bfloat16)

    out_down[:half, :] = plus(below[:half, :], more_lo[...])
    out_down[half:, :] = below[half:, :]
    out_up[:half, :] = above[:half, :]
    out_up[half:, :] = plus(above[half:, :], more_hi[...])


def collect_kernel(pick, rows, own, from_above, from_below, out):
    near = rows.shape[1]
    out[:, :near] = to_tokens(pick[...], rows[...]).astype(jnp.bfloat16)
    total = own[...].astype(jnp.float32) + from_above[...].astype(jnp.float32)
    out[:, near:] = (total + from_below[...].astype(jnp.float32)).astype(jnp.bfloat16)


def per_device(tokens, gate_scores, expert_ids, w_gate, w_up, w_down):
    groups, locals_ = lax.axis_size("node"), lax.axis_size("local")
    local = lax.axis_index("local").astype(jnp.int32).reshape(1)
    count, width = tokens.shape
    near = NEAR_TILES * LANES
    tie = lax.optimization_barrier

    def across(block):
        return lax.all_to_all(block, "node", 0, 0, tiled=True)

    def up(block):
        return lax.ppermute(block, "local", [(i, (i + 1) % locals_) for i in range(locals_)])

    def down(block):
        return lax.ppermute(block, "local", [(i, (i - 1) % locals_) for i in range(locals_)])

    def like(*shape):
        return jax.ShapeDtypeStruct(shape, jnp.bfloat16)

    run = functools.partial(
        experts, local=local, groups=groups, near=near, w_gate=w_gate, w_up=w_up, w_down=w_down
    )

    send, pick = prepare(tokens, gate_scores, expert_ids, groups, locals_)
    eight = PIECE // groups
    own = across(send.reshape(groups, 2, eight, width + LANES))
    own_a = own[:, 0].reshape(PIECE, width + LANES)
    own_b = own[:, 1].reshape(PIECE, width + LANES)
    below_a, above_b = up(own_a), down(own_b)
    own_pa, own_pb, first = run([own_a, own_b], None)
    below_a, above_b, first = tie((below_a, above_b, first))
    far_a, far_b = up(below_a), down(above_b)
    below_pa, above_pb, first = run([below_a, above_b], first)
    last_a, last_b, far_a, far_b, first = tie((own_a, own_b, far_a, far_b, first))
    below_b, above_a = up(last_b), down(last_a)
    far_pa, far_pb, second = run([far_a, far_b], None)
    below_b, above_a, second = tie((below_b, above_a, second))
    below_pb, above_pa, second = run([below_b, above_a], second)

    first = across(first)

    back_a, back_b = down(far_pa), up(far_pb)
    go_down, go_up = whole(
        pack_kernel, [like(2, PIECE, near)] * 2, back_a, below_pa, below_pb, back_b, above_pa, above_pb
    )
    second, first, go_down, go_up = tie((second, first, go_down, go_up))
    second = across(second)
    from_above, from_below = down(go_down), up(go_up)
    total = whole(
        total_kernel, like(groups, 2, eight, near), own_pa, own_pb, from_above, from_below
    )
    final = across(total).reshape(2 * PIECE, near)

    where = {
        "own": ((0, 0), (0, 1)), "below": ((0, 2), (1, 2)), "above": ((1, 3), (0, 3)), "far": ((1, 0), (1, 1)),
    }
    full, part = like(count, width - near), like(count // 2, width - near)
    own_t, below_t, above_t, far_lo, far_hi = whole(
        functools.partial(scatter_kernel, where, locals_), [full, full, full, part, part], first, second
    )
    more_lo, more_hi = down(far_lo), up(far_hi)
    go_down, go_up = whole(join_kernel, [full, full], below_t, more_lo, above_t, more_hi)
    from_above, from_below = down(go_down), up(go_up)
    return whole(collect_kernel, like(count, width), pick, final, own_t, from_above, from_below)


def solution(mesh):
    in_specs = (
        P(("dp", "node", "local"), None),
        P(("dp", "node", "local"), None),
        P(("dp", "node", "local"), None),
        P(("node", "local"), None, None),
        P(("node", "local"), None, None),
        P(("node", "local"), None, None),
    )
    out_specs = P(("dp", "node", "local"), None)
    return jax.shard_map(
        per_device, mesh=mesh, in_specs=in_specs, out_specs=out_specs, check_vma=False
    )
```

```python
import functools

import jax
import jax.numpy as jnp
from jax import lax
from jax.experimental import pallas as pl
from jax.experimental.pallas import tpu as pltpu
from jax.sharding import PartitionSpec as P

LANES = 128
PIECE = 128
VMEM = 60 * 1024 * 1024


def slot_maps(ids_t, groups, per_group):
    slots, tokens = groups * per_group, ids_t.shape[1]
    slot = lax.broadcasted_iota(jnp.int32, (slots, tokens), 0)
    half_rows = per_group // 2
    half = slots // 2
    group = (slot % half) // half_rows
    rank = (slot // half) * half_rows + slot % half_rows
    named = jnp.zeros((slots, tokens), jnp.bool_)
    for k in range(ids_t.shape[0]):
        named = named | (ids_t[k : k + 1, :] // 4 == group)
    before = lax.broadcasted_iota(jnp.int32, (tokens, tokens), 0) < lax.broadcasted_iota(
        jnp.int32, (tokens, tokens), 1
    )
    earlier = jnp.dot(
        named.astype(jnp.bfloat16), before.astype(jnp.bfloat16), preferred_element_type=jnp.float32
    )
    mine = named & (earlier == rank.astype(jnp.float32))
    return mine, group


def prepare_kernel(locals_, groups, per_group, tok, scores_t, ids_t, out_a, out_b, pick):
    ids = ids_t[...]
    mine, group = slot_maps(ids, groups, per_group)
    onehot = mine.astype(jnp.bfloat16)
    pick[...] = onehot
    score = scores_t[...]
    total = score[0:1, :]
    for k in range(1, score.shape[0]):
        total = total + score[k : k + 1, :]
    gates = (2.5 * score / total).astype(jnp.bfloat16).astype(jnp.float32)
    width = tok.shape[1]
    lane = lax.broadcasted_iota(jnp.int32, (mine.shape[0], LANES), 1)
    meta = jnp.zeros((mine.shape[0], LANES), jnp.float32)
    for j in range(locals_):
        value = jnp.zeros(mine.shape, jnp.float32)
        for k in range(ids.shape[0]):
            value = value + jnp.where(
                mine & (ids[k : k + 1, :] == group * locals_ + j), gates[k : k + 1, :], 0.0
            )
        meta = jnp.where(lane == j, jnp.sum(value, axis=1, keepdims=True), meta)
    token = lax.broadcasted_iota(jnp.int32, mine.shape, 1).astype(jnp.float32)
    token = jnp.sum(jnp.where(mine, token, 0.0), axis=1, keepdims=True)
    meta = jnp.where(lane == locals_, token, meta)
    meta = meta.astype(jnp.bfloat16)
    half = mine.shape[0] // 2
    out_a[:, width : width + LANES] = meta[:half]
    out_b[:, width : width + LANES] = meta[half:]
    for j in range(width // LANES):
        cols = slice(j * LANES, (j + 1) * LANES)
        x = tok[:, cols].astype(jnp.float32)
        largest = jnp.max(jnp.abs(x), axis=1, keepdims=True)
        scale = ((largest + 1e-06) / 448.0).astype(jnp.bfloat16).astype(jnp.float32)
        quantized = (x / scale).astype(jnp.bfloat16).astype(jnp.float32)
        restored = (quantized * scale).astype(jnp.bfloat16)
        rows = jnp.dot(onehot, restored, preferred_element_type=jnp.float32).astype(jnp.bfloat16)
        out_a[:, cols] = rows[:half]
        out_b[:, cols] = rows[half:]


def prepare(tokens, gate_scores, expert_ids, groups, locals_):
    count, width = tokens.shape
    per_group = 2 * count // groups
    slots = groups * per_group
    return pl.pallas_call(
        functools.partial(prepare_kernel, locals_, groups, per_group),
        out_shape=[
            jax.ShapeDtypeStruct((slots // 2, width + LANES), jnp.bfloat16),
            jax.ShapeDtypeStruct((slots // 2, width + LANES), jnp.bfloat16),
            jax.ShapeDtypeStruct((slots, count), jnp.bfloat16),
        ],
        compiler_params=pltpu.CompilerParams(vmem_limit_bytes=VMEM),
        cost_estimate=pl.CostEstimate(flops=10**9, bytes_accessed=3 * 10**6, transcendentals=0),
    )(tokens, gate_scores.T, expert_ids.T)


def expert_kernel(blocks, local_ref, *refs):
    xs, (wg, wu, wd), outs = refs[:blocks], refs[blocks : blocks + 3], refs[blocks + 3 : -2]
    rows, acc = refs[-2:]
    step, steps = pl.program_id(0), pl.num_programs(0)
    width = rows.shape[1]
    piece = xs[0].shape[0]

    @pl.when(step == 0)
    def _():
        for b in range(blocks):
            rows[b * piece : (b + 1) * piece, :] = xs[b][:, :width]

    x = rows[...]
    gate = jnp.dot(x, wg[0], preferred_element_type=jnp.float32)
    up = jnp.dot(x, wu[0], preferred_element_type=jnp.float32)
    hidden = (gate / (1.0 + jnp.exp(-gate)) * up).astype(jnp.bfloat16)
    part = jnp.dot(hidden, wd[0], preferred_element_type=jnp.float32)

    @pl.when(step == 0)
    def _():
        acc[...] = part

    @pl.when((step > 0) & (step < steps - 1))
    def _():
        acc[...] += part

    @pl.when(step == steps - 1)
    def _():
        for b in range(blocks):
            meta = xs[b][:, width : width + LANES]
            lane = lax.broadcasted_iota(jnp.int32, meta.shape, 1)
            weight = jnp.where(lane == local_ref[0], meta.astype(jnp.float32), 0.0)
            weight = jnp.sum(weight, axis=1, keepdims=True)
            own = slice(b * piece, (b + 1) * piece)
            outs[b][:, :width] = ((acc[own, :] + part[own, :]) * weight).astype(jnp.bfloat16)
            if outs[b].shape[1] > width:
                outs[b][:, width:] = meta


def experts(xs, marked, local, w_gate, w_up, w_down, tile=256):
    blocks = len(xs)
    piece, wide = xs[0].shape
    width, hidden = w_gate.shape[1:]
    wides = [wide if b in marked else width for b in range(blocks)]
    return pl.pallas_call(
        functools.partial(expert_kernel, blocks),
        grid=(hidden // tile,),
        in_specs=[pl.BlockSpec(memory_space=pltpu.SMEM)]
        + [pl.BlockSpec((piece, wide), lambda i: (0, 0))] * blocks
        + [
            pl.BlockSpec((1, width, tile), lambda i: (0, 0, i)),
            pl.BlockSpec((1, width, tile), lambda i: (0, 0, i)),
            pl.BlockSpec((1, tile, width), lambda i: (0, i, 0)),
        ],
        out_specs=[pl.BlockSpec((piece, w), lambda i: (0, 0)) for w in wides],
        out_shape=[jax.ShapeDtypeStruct((piece, w), jnp.bfloat16) for w in wides],
        scratch_shapes=[
            pltpu.VMEM((blocks * piece, width), jnp.bfloat16),
            pltpu.VMEM((blocks * piece, width), jnp.float32),
        ],
        compiler_params=pltpu.CompilerParams(
            vmem_limit_bytes=VMEM, dimension_semantics=("arbitrary",)
        ),
        cost_estimate=pl.CostEstimate(
            flops=6 * blocks * piece * width * hidden,
            bytes_accessed=6 * width * hidden,
            transcendentals=blocks * piece * hidden,
        ),
    )(local, *xs, w_gate, w_up, w_down)


def whole(kernel, shapes, *arrays):
    moved = sum(x.size * x.dtype.itemsize for x in arrays)
    return pl.pallas_call(
        kernel,
        out_shape=shapes,
        compiler_params=pltpu.CompilerParams(vmem_limit_bytes=VMEM),
        cost_estimate=pl.CostEstimate(flops=10**8, bytes_accessed=3 * moved, transcendentals=0),
    )(*arrays)


def to_tokens(pick, rows):
    return lax.dot_general(pick, rows, (((0,), (0,)), ((), ())), preferred_element_type=jnp.float32)


def scatter_kernel(locals_, first, second, out):
    count, width = out.shape
    total = None
    for rows in (first, second):
        meta = rows[:, width:].astype(jnp.float32)
        lane = lax.broadcasted_iota(jnp.int32, meta.shape, 1)
        token = jnp.sum(jnp.where(lane == locals_, meta, 0.0), axis=1, keepdims=True)
        lane = lax.broadcasted_iota(jnp.int32, (rows.shape[0], count), 1)
        part = to_tokens((lane.astype(jnp.float32) == token).astype(jnp.bfloat16), rows[:, :width])
        total = part if total is None else total + part
    out[...] = total.astype(jnp.bfloat16)


def collect_kernel(pick, first, second, far, out):
    total = to_tokens(pick[:PIECE, :], first[...]) + to_tokens(pick[PIECE:, :], second[...])
    out[...] = (total + far[...].astype(jnp.float32)).astype(jnp.bfloat16)


def per_device(tokens, gate_scores, expert_ids, w_gate, w_up, w_down):
    groups, locals_ = lax.axis_size("node"), lax.axis_size("local")
    local = lax.axis_index("local").astype(jnp.int32).reshape(1)
    tie = lax.optimization_barrier

    def across(block):
        parts = block.reshape(groups, block.shape[0] // groups, block.shape[1])
        return lax.all_to_all(parts, "node", 0, 0, tiled=True).reshape(block.shape)

    def shift(block, by):
        return lax.ppermute(block, "local", [(i, (i + by) % locals_) for i in range(locals_)])

    def up(block):
        return shift(block, 1)

    def down(block):
        return shift(block, -1)

    def add(*blocks):
        total = blocks[0].astype(jnp.float32)
        for block in blocks[1:]:
            total = total + block.astype(jnp.float32)
        return total.astype(jnp.bfloat16)

    run = functools.partial(experts, local=local, w_gate=w_gate, w_up=w_up, w_down=w_down)

    send_a, send_b, pick = prepare(tokens, gate_scores, expert_ids, groups, locals_)
    own_a = across(send_a)
    below_a, above_a = up(own_a), down(own_a)
    send_b, _ = tie((send_b, own_a))
    own_b = across(send_b)
    own_pa, own_pb = run([own_a, own_b], ())
    below_a, above_a, next_b, own_pa = tie((below_a, above_a, own_b, own_pa))
    far_a, above_b = up(below_a), down(next_b)
    below_pa, above_pa = run([below_a, above_a], ())
    far_a, above_b, last_b, below_pa = tie((far_a, above_b, next_b, below_pa))
    below_b, far_b = up(last_b), down(above_b)
    far_pa, above_pb = run([far_a, above_b], (0,))
    below_b, far_b, above_pb = tie((below_b, far_b, above_pb))
    below_pb, far_pb = run([below_b, far_b], (1,))

    home_a, home_b = across(far_pa), across(far_pb)
    far = whole(
        functools.partial(scatter_kernel, locals_),
        jax.ShapeDtypeStruct(tokens.shape, jnp.bfloat16), home_a, home_b,
    )
    far = shift(far, locals_ // 2)

    final_a = across(add(own_pa, down(below_pa), up(above_pa)))
    final_b = across(add(own_pb, down(below_pb), up(above_pb)))
    return whole(
        collect_kernel, jax.ShapeDtypeStruct(tokens.shape, jnp.bfloat16), pick, final_a, final_b, far
    )


def solution(mesh):
    in_specs = (
        P(("dp", "node", "local"), None),
        P(("dp", "node", "local"), None),
        P(("dp", "node", "local"), None),
        P(("node", "local"), None, None),
        P(("node", "local"), None, None),
        P(("node", "local"), None, None),
    )
    out_specs = P(("dp", "node", "local"), None)
    return jax.shard_map(
        per_device, mesh=mesh, in_specs=in_specs, out_specs=out_specs, check_vma=False
    )
```

```python
import functools

import jax
import jax.numpy as jnp
from jax import lax
from jax.experimental import pallas as pl
from jax.experimental.pallas import tpu as pltpu
from jax.sharding import PartitionSpec as P

LANES = 128
PIECE = 128
VMEM = 60 * 1024 * 1024


def slot_maps(ids_t, groups, per_group):
    slots, tokens = groups * per_group, ids_t.shape[1]
    slot = lax.broadcasted_iota(jnp.int32, (slots, tokens), 0)
    half_rows = per_group // 2
    half = slots // 2
    group = (slot % half) // half_rows
    rank = (slot // half) * half_rows + slot % half_rows
    named = jnp.zeros((slots, tokens), jnp.bool_)
    for k in range(ids_t.shape[0]):
        named = named | (ids_t[k : k + 1, :] // 4 == group)
    before = lax.broadcasted_iota(jnp.int32, (tokens, tokens), 0) < lax.broadcasted_iota(
        jnp.int32, (tokens, tokens), 1
    )
    earlier = jnp.dot(
        named.astype(jnp.bfloat16), before.astype(jnp.bfloat16), preferred_element_type=jnp.float32
    )
    mine = named & (earlier == rank.astype(jnp.float32))
    return mine, group


def prepare_kernel(locals_, groups, per_group, tok, scores_t, ids_t, out_a, out_b, pick):
    ids = ids_t[...]
    mine, group = slot_maps(ids, groups, per_group)
    onehot = mine.astype(jnp.bfloat16)
    pick[...] = onehot
    score = scores_t[...]
    total = score[0:1, :]
    for k in range(1, score.shape[0]):
        total = total + score[k : k + 1, :]
    gates = (2.5 * score / total).astype(jnp.bfloat16).astype(jnp.float32)
    width = tok.shape[1]
    lane = lax.broadcasted_iota(jnp.int32, (mine.shape[0], LANES), 1)
    meta = jnp.zeros((mine.shape[0], LANES), jnp.float32)
    for j in range(locals_):
        value = jnp.zeros(mine.shape, jnp.float32)
        for k in range(ids.shape[0]):
            value = value + jnp.where(
                mine & (ids[k : k + 1, :] == group * locals_ + j), gates[k : k + 1, :], 0.0
            )
        meta = jnp.where(lane == j, jnp.sum(value, axis=1, keepdims=True), meta)
    token = lax.broadcasted_iota(jnp.int32, mine.shape, 1).astype(jnp.float32)
    token = jnp.sum(jnp.where(mine, token, 0.0), axis=1, keepdims=True)
    meta = jnp.where(lane == locals_, token, meta)
    meta = meta.astype(jnp.bfloat16)
    half = mine.shape[0] // 2
    out_a[:, width : width + LANES] = meta[:half]
    out_b[:, width : width + LANES] = meta[half:]
    for j in range(width // LANES):
        cols = slice(j * LANES, (j + 1) * LANES)
        x = tok[:, cols].astype(jnp.float32)
        largest = jnp.max(jnp.abs(x), axis=1, keepdims=True)
        scale = ((largest + 1e-06) / 448.0).astype(jnp.bfloat16).astype(jnp.float32)
        quantized = (x * (1.0 / scale)).astype(jnp.bfloat16).astype(jnp.float32)
        restored = (quantized * scale).astype(jnp.bfloat16)
        rows = jnp.dot(onehot, restored, preferred_element_type=jnp.float32).astype(jnp.bfloat16)
        out_a[:, cols] = rows[:half]
        out_b[:, cols] = rows[half:]


def prepare(tokens, gate_scores, expert_ids, groups, locals_):
    count, width = tokens.shape
    per_group = 2 * count // groups
    slots = groups * per_group
    return pl.pallas_call(
        functools.partial(prepare_kernel, locals_, groups, per_group),
        out_shape=[
            jax.ShapeDtypeStruct((slots // 2, width + LANES), jnp.bfloat16),
            jax.ShapeDtypeStruct((slots // 2, width + LANES), jnp.bfloat16),
            jax.ShapeDtypeStruct((slots, count), jnp.bfloat16),
        ],
        compiler_params=pltpu.CompilerParams(vmem_limit_bytes=VMEM),
        cost_estimate=pl.CostEstimate(flops=10**9, bytes_accessed=3 * 10**6, transcendentals=0),
    )(tokens, gate_scores.T, expert_ids.T)


def expert_kernel(blocks, local_ref, *refs):
    xs, (wg, wu, wd), outs = refs[:blocks], refs[blocks : blocks + 3], refs[blocks + 3 : -2]
    rows, acc = refs[-2:]
    step, steps = pl.program_id(0), pl.num_programs(0)
    width = rows.shape[1]
    piece = xs[0].shape[0]

    @pl.when(step == 0)
    def _():
        for b in range(blocks):
            rows[b * piece : (b + 1) * piece, :] = xs[b][:, :width]

    x = rows[...]
    gate = jnp.dot(x, wg[0], preferred_element_type=jnp.float32)
    up = jnp.dot(x, wu[0], preferred_element_type=jnp.float32)
    hidden = (gate / (1.0 + jnp.exp(-gate)) * up).astype(jnp.bfloat16)
    part = jnp.dot(hidden, wd[0], preferred_element_type=jnp.float32)

    @pl.when(step == 0)
    def _():
        acc[...] = part

    @pl.when((step > 0) & (step < steps - 1))
    def _():
        acc[...] += part

    @pl.when(step == steps - 1)
    def _():
        for b in range(blocks):
            meta = xs[b][:, width : width + LANES]
            lane = lax.broadcasted_iota(jnp.int32, meta.shape, 1)
            weight = jnp.where(lane == local_ref[0], meta.astype(jnp.float32), 0.0)
            weight = jnp.sum(weight, axis=1, keepdims=True)
            own = slice(b * piece, (b + 1) * piece)
            outs[b][:, :width] = ((acc[own, :] + part[own, :]) * weight).astype(jnp.bfloat16)
            if outs[b].shape[1] > width:
                outs[b][:, width:] = meta


def experts(xs, marked, local, w_gate, w_up, w_down, tile=256):
    blocks = len(xs)
    piece, wide = xs[0].shape
    width, hidden = w_gate.shape[1:]
    wides = [wide if b in marked else width for b in range(blocks)]
    return pl.pallas_call(
        functools.partial(expert_kernel, blocks),
        grid=(hidden // tile,),
        in_specs=[pl.BlockSpec(memory_space=pltpu.SMEM)]
        + [pl.BlockSpec((piece, wide), lambda i: (0, 0))] * blocks
        + [
            pl.BlockSpec((1, width, tile), lambda i: (0, 0, i)),
            pl.BlockSpec((1, width, tile), lambda i: (0, 0, i)),
            pl.BlockSpec((1, tile, width), lambda i: (0, i, 0)),
        ],
        out_specs=[pl.BlockSpec((piece, w), lambda i: (0, 0)) for w in wides],
        out_shape=[jax.ShapeDtypeStruct((piece, w), jnp.bfloat16) for w in wides],
        scratch_shapes=[
            pltpu.VMEM((blocks * piece, width), jnp.bfloat16),
            pltpu.VMEM((blocks * piece, width), jnp.float32),
        ],
        compiler_params=pltpu.CompilerParams(
            vmem_limit_bytes=VMEM, dimension_semantics=("arbitrary",)
        ),
        cost_estimate=pl.CostEstimate(
            flops=6 * blocks * piece * width * hidden,
            bytes_accessed=6 * width * hidden,
            transcendentals=blocks * piece * hidden,
        ),
    )(local, *xs, w_gate, w_up, w_down)


def whole(kernel, shapes, *arrays):
    moved = sum(x.size * x.dtype.itemsize for x in arrays)
    return pl.pallas_call(
        kernel,
        out_shape=shapes,
        compiler_params=pltpu.CompilerParams(vmem_limit_bytes=VMEM),
        cost_estimate=pl.CostEstimate(flops=10**8, bytes_accessed=3 * moved, transcendentals=0),
    )(*arrays)


def to_tokens(pick, rows):
    return lax.dot_general(pick, rows, (((0,), (0,)), ((), ())), preferred_element_type=jnp.float32)


def scatter_kernel(locals_, first, second, out):
    count, width = out.shape
    total = None
    for rows in (first, second):
        meta = rows[:, width:].astype(jnp.float32)
        lane = lax.broadcasted_iota(jnp.int32, meta.shape, 1)
        token = jnp.sum(jnp.where(lane == locals_, meta, 0.0), axis=1, keepdims=True)
        lane = lax.broadcasted_iota(jnp.int32, (rows.shape[0], count), 1)
        part = to_tokens((lane.astype(jnp.float32) == token).astype(jnp.bfloat16), rows[:, :width])
        total = part if total is None else total + part
    out[...] = total.astype(jnp.bfloat16)


def collect_kernel(pick, first, second, far, out):
    total = to_tokens(pick[:PIECE, :], first[...]) + to_tokens(pick[PIECE:, :], second[...])
    out[...] = (total + far[...].astype(jnp.float32)).astype(jnp.bfloat16)


def collect(pick, first, second, far, steps=4):
    count, width = far.shape
    cut = width // steps
    block = pl.BlockSpec((count, cut), lambda i: (0, i))
    return pl.pallas_call(
        collect_kernel,
        grid=(steps,),
        in_specs=[pl.BlockSpec(pick.shape, lambda i: (0, 0)), block, block, block],
        out_specs=block,
        out_shape=jax.ShapeDtypeStruct((count, width), jnp.bfloat16),
        compiler_params=pltpu.CompilerParams(vmem_limit_bytes=VMEM),
        cost_estimate=pl.CostEstimate(
            flops=4 * pick.size * width, bytes_accessed=8 * far.size, transcendentals=0
        ),
    )(pick, first, second, far)


def per_device(tokens, gate_scores, expert_ids, w_gate, w_up, w_down):
    groups, locals_ = lax.axis_size("node"), lax.axis_size("local")
    local = lax.axis_index("local").astype(jnp.int32).reshape(1)
    tie = lax.optimization_barrier

    def across(block):
        parts = block.reshape(groups, block.shape[0] // groups, block.shape[1])
        return lax.all_to_all(parts, "node", 0, 0, tiled=True).reshape(block.shape)

    def shift(block, by):
        return lax.ppermute(block, "local", [(i, (i + by) % locals_) for i in range(locals_)])

    def up(block):
        return shift(block, 1)

    def down(block):
        return shift(block, -1)

    def add(*blocks):
        total = blocks[0].astype(jnp.float32)
        for block in blocks[1:]:
            total = total + block.astype(jnp.float32)
        return total.astype(jnp.bfloat16)

    run = functools.partial(experts, local=local, w_gate=w_gate, w_up=w_up, w_down=w_down)

    send_a, send_b, pick = prepare(tokens, gate_scores, expert_ids, groups, locals_)
    own_a = across(send_a)
    below_a, above_a = up(own_a), down(own_a)
    send_b, _ = tie((send_b, own_a))
    own_b = across(send_b)
    [own_pa] = run([own_a], ())
    below_a, above_a, next_b, own_pa = tie((below_a, above_a, own_b, own_pa))
    far_a, above_b = up(below_a), down(next_b)
    below_pa, above_pa = run([below_a, above_a], ())
    far_a, above_b, last_b, below_pa = tie((far_a, above_b, next_b, below_pa))
    below_b, far_b = up(last_b), down(above_b)
    far_pa, above_pb = run([far_a, above_b], (0,))
    below_pa, above_pa, far_pa = tie((below_pa, above_pa, far_pa))
    below_b, far_b, above_pb = tie((below_b, far_b, above_pb))
    below_pb, far_pb = run([below_b, far_b], (1,))
    last_b, far_pb = tie((last_b, far_pb))
    [own_pb] = run([last_b], ())

    home_a, home_b = across(far_pa), across(far_pb)
    far = whole(
        functools.partial(scatter_kernel, locals_),
        jax.ShapeDtypeStruct(tokens.shape, jnp.bfloat16), home_a, home_b,
    )
    far = shift(far, locals_ // 2)

    final_a = across(add(own_pa, down(below_pa), up(above_pa)))
    final_b = across(add(own_pb, down(below_pb), up(above_pb)))
    return collect(pick, final_a, final_b, far)


def solution(mesh):
    in_specs = (
        P(("dp", "node", "local"), None),
        P(("dp", "node", "local"), None),
        P(("dp", "node", "local"), None),
        P(("node", "local"), None, None),
        P(("node", "local"), None, None),
        P(("node", "local"), None, None),
    )
    out_specs = P(("dp", "node", "local"), None)
    return jax.shard_map(
        per_device, mesh=mesh, in_specs=in_specs, out_specs=out_specs, check_vma=False
    )
```

```python
import functools

import jax
import jax.numpy as jnp
from jax import lax
from jax.experimental import pallas as pl
from jax.experimental.pallas import tpu as pltpu
from jax.sharding import PartitionSpec as P

LANES = 128
PIECE = 128
VMEM = 60 * 1024 * 1024


def slot_maps(ids_t, groups, per_group):
    slots, tokens = groups * per_group, ids_t.shape[1]
    slot = lax.broadcasted_iota(jnp.int32, (slots, tokens), 0)
    half_rows = per_group // 2
    half = slots // 2
    group = (slot % half) // half_rows
    rank = (slot // half) * half_rows + slot % half_rows
    named = jnp.zeros((slots, tokens), jnp.bool_)
    for k in range(ids_t.shape[0]):
        named = named | (ids_t[k : k + 1, :] // 4 == group)
    before = lax.broadcasted_iota(jnp.int32, (tokens, tokens), 0) < lax.broadcasted_iota(
        jnp.int32, (tokens, tokens), 1
    )
    earlier = jnp.dot(
        named.astype(jnp.bfloat16), before.astype(jnp.bfloat16), preferred_element_type=jnp.float32
    )
    mine = named & (earlier == rank.astype(jnp.float32))
    return mine, group


def prepare_kernel(locals_, groups, per_group, tok, scores_t, ids_t, out_a, out_b, pick):
    ids = ids_t[...]
    mine, group = slot_maps(ids, groups, per_group)
    onehot = mine.astype(jnp.bfloat16)
    pick[...] = onehot
    score = scores_t[...]
    total = score[0:1, :]
    for k in range(1, score.shape[0]):
        total = total + score[k : k + 1, :]
    gates = (2.5 * score / total).astype(jnp.bfloat16).astype(jnp.float32)
    width = tok.shape[1]
    lane = lax.broadcasted_iota(jnp.int32, (mine.shape[0], LANES), 1)
    meta = jnp.zeros((mine.shape[0], LANES), jnp.float32)
    for j in range(locals_):
        value = jnp.zeros(mine.shape, jnp.float32)
        for k in range(ids.shape[0]):
            value = value + jnp.where(
                mine & (ids[k : k + 1, :] == group * locals_ + j), gates[k : k + 1, :], 0.0
            )
        meta = jnp.where(lane == j, jnp.sum(value, axis=1, keepdims=True), meta)
    token = lax.broadcasted_iota(jnp.int32, mine.shape, 1).astype(jnp.float32)
    token = jnp.sum(jnp.where(mine, token, 0.0), axis=1, keepdims=True)
    meta = jnp.where(lane == locals_, token, meta)
    meta = meta.astype(jnp.bfloat16)
    half = mine.shape[0] // 2
    out_a[:, width : width + LANES] = meta[:half]
    out_b[:, width : width + LANES] = meta[half:]
    for j in range(width // LANES):
        cols = slice(j * LANES, (j + 1) * LANES)
        x = tok[:, cols].astype(jnp.float32)
        largest = jnp.max(jnp.abs(x), axis=1, keepdims=True)
        scale = ((largest + 1e-06) / 448.0).astype(jnp.bfloat16).astype(jnp.float32)
        quantized = (x * (1.0 / scale)).astype(jnp.bfloat16).astype(jnp.float32)
        restored = (quantized * scale).astype(jnp.bfloat16)
        rows = jnp.dot(onehot, restored, preferred_element_type=jnp.float32).astype(jnp.bfloat16)
        out_a[:, cols] = rows[:half]
        out_b[:, cols] = rows[half:]


def prepare(tokens, gate_scores, expert_ids, groups, locals_):
    count, width = tokens.shape
    per_group = 2 * count // groups
    slots = groups * per_group
    return pl.pallas_call(
        functools.partial(prepare_kernel, locals_, groups, per_group),
        out_shape=[
            jax.ShapeDtypeStruct((slots // 2, width + LANES), jnp.bfloat16),
            jax.ShapeDtypeStruct((slots // 2, width + LANES), jnp.bfloat16),
            jax.ShapeDtypeStruct((slots, count), jnp.bfloat16),
        ],
        compiler_params=pltpu.CompilerParams(vmem_limit_bytes=VMEM),
        cost_estimate=pl.CostEstimate(flops=10**9, bytes_accessed=3 * 10**6, transcendentals=0),
    )(tokens, gate_scores.T, expert_ids.T)


def expert_kernel(blocks, tile, local_ref, *refs):
    xs, weights, outs = refs[:blocks], refs[blocks : blocks + 3], refs[blocks + 3 : 2 * blocks + 3]
    rows, acc, done, wg, wu, wd, arrived, left, held = refs[2 * blocks + 3 :]
    width = acc.shape[1]
    piece = xs[0].shape[0]

    def own(b):
        return pl.ds(b * piece, piece)

    loads = [pltpu.make_async_copy(xs[b], rows.at[own(b)], arrived.at[b]) for b in range(blocks)]
    for load in loads:
        load.start()

    def weight_tiles(i):
        cols = pl.ds(pl.multiple_of(i * tile, tile), tile)
        places = (0, slice(None), cols), (0, slice(None), cols), (0, cols, slice(None))
        return [
            pltpu.make_async_copy(source.at[place], target.at[place[1:]], held.at[which, i])
            for which, (source, target, place) in enumerate(zip(weights, (wg, wu, wd), places))
        ]

    steps = wg.shape[1] // tile
    for i in range(steps):
        for copy in weight_tiles(i):
            copy.start()
    for load in loads:
        load.wait()

    def step(i, carry):
        cols = pl.ds(pl.multiple_of(i * tile, tile), tile)
        for copy in weight_tiles(i):
            copy.wait()
        x = rows[:, :width]
        gate = jnp.dot(x, wg[:, cols], preferred_element_type=jnp.float32)
        up = jnp.dot(x, wu[:, cols], preferred_element_type=jnp.float32)
        hidden = (gate / (1.0 + jnp.exp(-gate)) * up).astype(jnp.bfloat16)
        part = jnp.dot(hidden, wd[cols, :], preferred_element_type=jnp.float32)

        @pl.when(i == 0)
        def _():
            acc[...] = part

        @pl.when(i > 0)
        def _():
            acc[...] += part

        return carry

    lax.fori_loop(0, steps, step, 0)
    stores = []
    for b in range(blocks):
        meta = rows[own(b), width:]
        lane = lax.broadcasted_iota(jnp.int32, meta.shape, 1)
        weight = jnp.where(lane == local_ref[0], meta.astype(jnp.float32), 0.0)
        weight = jnp.sum(weight, axis=1, keepdims=True)
        done[own(b), :width] = (acc[own(b), :] * weight).astype(jnp.bfloat16)
        done[own(b), width:] = meta
        stores.append(
            pltpu.make_async_copy(done.at[own(b), pl.ds(0, outs[b].shape[1])], outs[b], left.at[b])
        )
        stores[-1].start()
    for store in stores:
        store.wait()


def experts(xs, marked, local, w_gate, w_up, w_down, tile=256):
    blocks = len(xs)
    piece, wide = xs[0].shape
    width, hidden = w_gate.shape[1:]
    wides = [wide if b in marked else width for b in range(blocks)]
    anywhere = pl.BlockSpec(memory_space=pl.ANY)
    return pl.pallas_call(
        functools.partial(expert_kernel, blocks, tile),
        in_specs=[pl.BlockSpec(memory_space=pltpu.SMEM)]
        + [anywhere] * blocks
        + [anywhere] * 3,
        out_specs=[anywhere] * blocks,
        out_shape=[jax.ShapeDtypeStruct((piece, w), jnp.bfloat16) for w in wides],
        scratch_shapes=[
            pltpu.VMEM((blocks * piece, wide), jnp.bfloat16),
            pltpu.VMEM((blocks * piece, width), jnp.float32),
            pltpu.VMEM((blocks * piece, wide), jnp.bfloat16),
            pltpu.VMEM((width, hidden), jnp.bfloat16),
            pltpu.VMEM((width, hidden), jnp.bfloat16),
            pltpu.VMEM((hidden, width), jnp.bfloat16),
            pltpu.SemaphoreType.DMA((blocks,)),
            pltpu.SemaphoreType.DMA((blocks,)),
            pltpu.SemaphoreType.DMA((3, hidden // tile)),
        ],
        compiler_params=pltpu.CompilerParams(vmem_limit_bytes=VMEM),
        cost_estimate=pl.CostEstimate(
            flops=6 * blocks * piece * width * hidden,
            bytes_accessed=6 * width * hidden,
            transcendentals=blocks * piece * hidden,
        ),
    )(local, *xs, w_gate, w_up, w_down)


def whole(kernel, shapes, *arrays):
    moved = sum(x.size * x.dtype.itemsize for x in arrays)
    return pl.pallas_call(
        kernel,
        out_shape=shapes,
        compiler_params=pltpu.CompilerParams(vmem_limit_bytes=VMEM),
        cost_estimate=pl.CostEstimate(flops=10**8, bytes_accessed=3 * moved, transcendentals=0),
    )(*arrays)


def to_tokens(pick, rows):
    return lax.dot_general(pick, rows, (((0,), (0,)), ((), ())), preferred_element_type=jnp.float32)


def scatter_kernel(locals_, first, second, out):
    count, width = out.shape
    total = None
    for rows in (first, second):
        meta = rows[:, width:].astype(jnp.float32)
        lane = lax.broadcasted_iota(jnp.int32, meta.shape, 1)
        token = jnp.sum(jnp.where(lane == locals_, meta, 0.0), axis=1, keepdims=True)
        lane = lax.broadcasted_iota(jnp.int32, (rows.shape[0], count), 1)
        part = to_tokens((lane.astype(jnp.float32) == token).astype(jnp.bfloat16), rows[:, :width])
        total = part if total is None else total + part
    out[...] = total.astype(jnp.bfloat16)


def collect_kernel(pick, first, second, far, out):
    total = to_tokens(pick[:PIECE, :], first[...]) + to_tokens(pick[PIECE:, :], second[...])
    out[...] = (total + far[...].astype(jnp.float32)).astype(jnp.bfloat16)


def per_device(tokens, gate_scores, expert_ids, w_gate, w_up, w_down):
    groups, locals_ = lax.axis_size("node"), lax.axis_size("local")
    local = lax.axis_index("local").astype(jnp.int32).reshape(1)
    tie = lax.optimization_barrier

    def across(block):
        parts = block.reshape(groups, block.shape[0] // groups, block.shape[1])
        return lax.all_to_all(parts, "node", 0, 0, tiled=True).reshape(block.shape)

    def shift(block, by):
        return lax.ppermute(block, "local", [(i, (i + by) % locals_) for i in range(locals_)])

    def up(block):
        return shift(block, 1)

    def down(block):
        return shift(block, -1)

    def add(*blocks):
        total = blocks[0].astype(jnp.float32)
        for block in blocks[1:]:
            total = total + block.astype(jnp.float32)
        return total.astype(jnp.bfloat16)

    run = functools.partial(experts, local=local, w_gate=w_gate, w_up=w_up, w_down=w_down)

    send_a, send_b, pick = prepare(tokens, gate_scores, expert_ids, groups, locals_)
    own_a = across(send_a)
    below_a, above_a = up(own_a), down(own_a)
    send_b, _ = tie((send_b, own_a))
    own_b = across(send_b)
    [own_pa] = run([own_a], ())
    below_a, above_a, next_b, own_pa = tie((below_a, above_a, own_b, own_pa))
    far_a, above_b = up(below_a), down(next_b)
    below_pa, above_pa = run([below_a, above_a], ())
    far_a, above_b, last_b, below_pa = tie((far_a, above_b, next_b, below_pa))
    below_b, far_b = up(last_b), down(above_b)
    far_pa, above_pb = run([far_a, above_b], (0,))
    below_pa, above_pa, far_pa = tie((below_pa, above_pa, far_pa))
    below_b, far_b, above_pb = tie((below_b, far_b, above_pb))
    below_pb, far_pb = run([below_b, far_b], (1,))

    home_a = across(far_pa)
    above_pb, below_pb, far_pb, home_a = tie((above_pb, below_pb, far_pb, home_a))
    home_b = across(far_pb)
    last_b, home_b = tie((last_b, home_b))
    [own_pb] = run([last_b], ())
    far = whole(
        functools.partial(scatter_kernel, locals_),
        jax.ShapeDtypeStruct(tokens.shape, jnp.bfloat16), home_a, home_b,
    )
    far = shift(far, locals_ // 2)

    final_a = across(add(own_pa, down(below_pa), up(above_pa)))
    final_b = across(add(own_pb, down(below_pb), up(above_pb)))
    near = [pltpu.with_memory_space_constraint(x, pltpu.VMEM) for x in (final_a, final_b, far)]
    return whole(collect_kernel, jax.ShapeDtypeStruct(tokens.shape, jnp.bfloat16), pick, *near)


def solution(mesh):
    in_specs = (
        P(("dp", "node", "local"), None),
        P(("dp", "node", "local"), None),
        P(("dp", "node", "local"), None),
        P(("node", "local"), None, None),
        P(("node", "local"), None, None),
        P(("node", "local"), None, None),
    )
    out_specs = P(("dp", "node", "local"), None)
    return jax.shard_map(
        per_device, mesh=mesh, in_specs=in_specs, out_specs=out_specs, check_vma=False
    )
```

```python
import functools

import jax
import jax.numpy as jnp
from jax import lax
from jax.experimental import pallas as pl
from jax.experimental.pallas import tpu as pltpu
from jax.sharding import PartitionSpec as P

LANES = 128
PIECE = 128
VMEM = 60 * 1024 * 1024


def slot_maps(ids_t, groups, per_group):
    slots, tokens = groups * per_group, ids_t.shape[1]
    slot = lax.broadcasted_iota(jnp.int32, (slots, tokens), 0)
    half_rows = per_group // 2
    half = slots // 2
    group = (slot % half) // half_rows
    rank = (slot // half) * half_rows + slot % half_rows
    named = jnp.zeros((slots, tokens), jnp.bool_)
    for k in range(ids_t.shape[0]):
        named = named | (ids_t[k : k + 1, :] // 4 == group)
    before = lax.broadcasted_iota(jnp.int32, (tokens, tokens), 0) < lax.broadcasted_iota(
        jnp.int32, (tokens, tokens), 1
    )
    earlier = jnp.dot(
        named.astype(jnp.bfloat16), before.astype(jnp.bfloat16), preferred_element_type=jnp.float32
    )
    mine = named & (earlier == rank.astype(jnp.float32))
    return mine, group


def prepare_kernel(locals_, groups, per_group, tok, scores_t, ids_t, out_a, out_b, pick):
    ids = ids_t[...]
    mine, group = slot_maps(ids, groups, per_group)
    onehot = mine.astype(jnp.bfloat16)
    pick[...] = onehot
    score = scores_t[...]
    total = score[0:1, :]
    for k in range(1, score.shape[0]):
        total = total + score[k : k + 1, :]
    gates = (2.5 * score / total).astype(jnp.bfloat16).astype(jnp.float32)
    width = tok.shape[1]
    lane = lax.broadcasted_iota(jnp.int32, (mine.shape[0], LANES), 1)
    meta = jnp.zeros((mine.shape[0], LANES), jnp.float32)
    for j in range(locals_):
        value = jnp.zeros(mine.shape, jnp.float32)
        for k in range(ids.shape[0]):
            value = value + jnp.where(
                mine & (ids[k : k + 1, :] == group * locals_ + j), gates[k : k + 1, :], 0.0
            )
        meta = jnp.where(lane == j, jnp.sum(value, axis=1, keepdims=True), meta)
    token = lax.broadcasted_iota(jnp.int32, mine.shape, 1).astype(jnp.float32)
    token = jnp.sum(jnp.where(mine, token, 0.0), axis=1, keepdims=True)
    meta = jnp.where(lane == locals_, token, meta)
    meta = meta.astype(jnp.bfloat16)
    half = mine.shape[0] // 2
    out_a[:, width : width + LANES] = meta[:half]
    out_b[:, width : width + LANES] = meta[half:]
    for start in range(0, width, 4 * LANES):
        restored = []
        for place in range(start, start + 4 * LANES, LANES):
            x = tok[:, place : place + LANES].astype(jnp.float32)
            largest = jnp.max(jnp.abs(x), axis=1, keepdims=True)
            scale = ((largest + 1e-06) / 448.0).astype(jnp.bfloat16).astype(jnp.float32)
            quantized = (x * (1.0 / scale)).astype(jnp.bfloat16).astype(jnp.float32)
            restored.append((quantized * scale).astype(jnp.bfloat16))
        cols = slice(start, start + 4 * LANES)
        restored = jnp.concatenate(restored, axis=1)
        rows = jnp.dot(onehot, restored, preferred_element_type=jnp.float32).astype(jnp.bfloat16)
        out_a[:, cols] = rows[:half]
        out_b[:, cols] = rows[half:]


def prepare(tokens, gate_scores, expert_ids, groups, locals_):
    count, width = tokens.shape
    per_group = 2 * count // groups
    slots = groups * per_group
    return pl.pallas_call(
        functools.partial(prepare_kernel, locals_, groups, per_group),
        out_shape=[
            jax.ShapeDtypeStruct((slots // 2, width + LANES), jnp.bfloat16),
            jax.ShapeDtypeStruct((slots // 2, width + LANES), jnp.bfloat16),
            jax.ShapeDtypeStruct((slots, count), jnp.bfloat16),
        ],
        compiler_params=pltpu.CompilerParams(vmem_limit_bytes=VMEM),
        cost_estimate=pl.CostEstimate(flops=10**9, bytes_accessed=3 * 10**6, transcendentals=0),
    )(tokens, gate_scores.T, expert_ids.T)


def expert_kernel(blocks, local_ref, *refs):
    xs, (wg, wu, wd), outs = refs[:blocks], refs[blocks : blocks + 3], refs[blocks + 3 : -2]
    rows, acc = refs[-2:]
    step, steps = pl.program_id(0), pl.num_programs(0)
    width = rows.shape[1]
    piece = xs[0].shape[0]

    @pl.when(step == 0)
    def _():
        for b in range(blocks):
            rows[b * piece : (b + 1) * piece, :] = xs[b][:, :width]

    x = rows[...]
    gate = jnp.dot(x, wg[0], preferred_element_type=jnp.float32)
    up = jnp.dot(x, wu[0], preferred_element_type=jnp.float32)
    hidden = (gate / (1.0 + jnp.exp(-gate)) * up).astype(jnp.bfloat16)
    part = jnp.dot(hidden, wd[0], preferred_element_type=jnp.float32)

    @pl.when(step == 0)
    def _():
        acc[...] = part

    @pl.when((step > 0) & (step < steps - 1))
    def _():
        acc[...] += part

    @pl.when(step == steps - 1)
    def _():
        for b in range(blocks):
            meta = xs[b][:, width : width + LANES]
            lane = lax.broadcasted_iota(jnp.int32, meta.shape, 1)
            weight = jnp.where(lane == local_ref[0], meta.astype(jnp.float32), 0.0)
            weight = jnp.sum(weight, axis=1, keepdims=True)
            own = slice(b * piece, (b + 1) * piece)
            outs[b][:, :width] = ((acc[own, :] + part[own, :]) * weight).astype(jnp.bfloat16)
            if outs[b].shape[1] > width:
                outs[b][:, width:] = meta


def experts(xs, marked, local, w_gate, w_up, w_down, tile=256):
    blocks = len(xs)
    piece, wide = xs[0].shape
    width, hidden = w_gate.shape[1:]
    wides = [wide if b in marked else width for b in range(blocks)]
    return pl.pallas_call(
        functools.partial(expert_kernel, blocks),
        grid=(hidden // tile,),
        in_specs=[pl.BlockSpec(memory_space=pltpu.SMEM)]
        + [pl.BlockSpec((piece, wide), lambda i: (0, 0))] * blocks
        + [
            pl.BlockSpec((1, width, tile), lambda i: (0, 0, i)),
            pl.BlockSpec((1, width, tile), lambda i: (0, 0, i)),
            pl.BlockSpec((1, tile, width), lambda i: (0, i, 0)),
        ],
        out_specs=[pl.BlockSpec((piece, w), lambda i: (0, 0)) for w in wides],
        out_shape=[jax.ShapeDtypeStruct((piece, w), jnp.bfloat16) for w in wides],
        scratch_shapes=[
            pltpu.VMEM((blocks * piece, width), jnp.bfloat16),
            pltpu.VMEM((blocks * piece, width), jnp.float32),
        ],
        compiler_params=pltpu.CompilerParams(
            vmem_limit_bytes=VMEM, dimension_semantics=("arbitrary",)
        ),
        cost_estimate=pl.CostEstimate(
            flops=6 * blocks * piece * width * hidden,
            bytes_accessed=6 * width * hidden,
            transcendentals=blocks * piece * hidden,
        ),
    )(local, *xs, w_gate, w_up, w_down)


def whole(kernel, shapes, *arrays):
    moved = sum(x.size * x.dtype.itemsize for x in arrays)
    return pl.pallas_call(
        kernel,
        out_shape=shapes,
        compiler_params=pltpu.CompilerParams(vmem_limit_bytes=VMEM),
        cost_estimate=pl.CostEstimate(flops=10**8, bytes_accessed=3 * moved, transcendentals=0),
    )(*arrays)


def to_tokens(pick, rows):
    return lax.dot_general(pick, rows, (((0,), (0,)), ((), ())), preferred_element_type=jnp.float32)


def scatter_kernel(locals_, first, second, out):
    count, width = out.shape
    total = None
    for rows in (first, second):
        meta = rows[:, width:].astype(jnp.float32)
        lane = lax.broadcasted_iota(jnp.int32, meta.shape, 1)
        token = jnp.sum(jnp.where(lane == locals_, meta, 0.0), axis=1, keepdims=True)
        lane = lax.broadcasted_iota(jnp.int32, (rows.shape[0], count), 1)
        part = to_tokens((lane.astype(jnp.float32) == token).astype(jnp.bfloat16), rows[:, :width])
        total = part if total is None else total + part
    out[...] = total.astype(jnp.bfloat16)


def collect_kernel(pick, first, second, far, out):
    total = to_tokens(pick[:PIECE, :], first[...]) + to_tokens(pick[PIECE:, :], second[...])
    out[...] = (total + far[...].astype(jnp.float32)).astype(jnp.bfloat16)


def per_device(tokens, gate_scores, expert_ids, w_gate, w_up, w_down):
    groups, locals_ = lax.axis_size("node"), lax.axis_size("local")
    local = lax.axis_index("local").astype(jnp.int32).reshape(1)
    tie = lax.optimization_barrier

    def across(block):
        parts = block.reshape(groups, block.shape[0] // groups, block.shape[1])
        return lax.all_to_all(parts, "node", 0, 0, tiled=True).reshape(block.shape)

    def shift(block, by):
        return lax.ppermute(block, "local", [(i, (i + by) % locals_) for i in range(locals_)])

    def up(block):
        return shift(block, 1)

    def down(block):
        return shift(block, -1)

    def add(*blocks):
        total = blocks[0].astype(jnp.float32)
        for block in blocks[1:]:
            total = total + block.astype(jnp.float32)
        return total.astype(jnp.bfloat16)

    run = functools.partial(experts, local=local, w_gate=w_gate, w_up=w_up, w_down=w_down)

    send_a, send_b, pick = prepare(tokens, gate_scores, expert_ids, groups, locals_)
    own_a = across(send_a)
    below_a, above_a = up(own_a), down(own_a)
    send_b, _ = tie((send_b, own_a))
    own_b = across(send_b)
    [own_pa] = run([own_a], ())
    below_a, above_a, next_b, own_pa = tie((below_a, above_a, own_b, own_pa))
    far_a, above_b = up(below_a), down(next_b)
    below_pa, above_pa, own_pb = run([below_a, above_a, next_b], ())
    far_a, above_b, last_b, below_pa = tie((far_a, above_b, next_b, below_pa))
    below_b, far_b = up(last_b), down(above_b)
    far_pa, above_pb = run([far_a, above_b], (0,))
    below_pa, above_pa, far_pa = tie((below_pa, above_pa, far_pa))
    below_b, far_b, above_pb = tie((below_b, far_b, above_pb))
    below_pb, far_pb = run([below_b, far_b], (1,))

    home_a = across(far_pa)
    above_pb, below_pb, far_pb, home_a = tie((above_pb, below_pb, far_pb, home_a))
    home_b = across(far_pb)
    far = whole(
        functools.partial(scatter_kernel, locals_),
        jax.ShapeDtypeStruct(tokens.shape, jnp.bfloat16), home_a, home_b,
    )
    far = shift(far, locals_ // 2)

    final_a = across(add(own_pa, down(below_pa), up(above_pa)))
    final_b = across(add(own_pb, down(below_pb), up(above_pb)))
    near = [pltpu.with_memory_space_constraint(x, pltpu.VMEM) for x in (final_a, final_b, far)]
    return whole(collect_kernel, jax.ShapeDtypeStruct(tokens.shape, jnp.bfloat16), pick, *near)


def solution(mesh):
    in_specs = (
        P(("dp", "node", "local"), None),
        P(("dp", "node", "local"), None),
        P(("dp", "node", "local"), None),
        P(("node", "local"), None, None),
        P(("node", "local"), None, None),
        P(("node", "local"), None, None),
    )
    out_specs = P(("dp", "node", "local"), None)
    return jax.shard_map(
        per_device, mesh=mesh, in_specs=in_specs, out_specs=out_specs, check_vma=False
    )
```

```python
import functools

import jax
import jax.numpy as jnp
from jax import lax
from jax.experimental import pallas as pl
from jax.experimental.pallas import tpu as pltpu
from jax.sharding import PartitionSpec as P

LANES = 128
PIECE = 128
VMEM = 60 * 1024 * 1024
EXPERT_VMEM = 60 * 1024 * 1024


def slot_maps(ids, groups, per_group, parts):
    slots, tokens = groups * per_group, ids.shape[1]
    slot = lax.broadcasted_iota(jnp.int32, (slots, tokens), 0)
    part_rows, part = per_group // parts, slots // parts
    group = (slot % part) // part_rows
    rank = (slot // part) * part_rows + slot % part_rows
    named = jnp.zeros((slots, tokens), jnp.bool_)
    for k in range(ids.shape[0]):
        named = named | (ids[k : k + 1, :] // 4 == group)
    before = lax.broadcasted_iota(jnp.int32, (tokens, tokens), 0) < lax.broadcasted_iota(
        jnp.int32, (tokens, tokens), 1
    )
    earlier = jnp.dot(
        named.astype(jnp.bfloat16), before.astype(jnp.bfloat16), preferred_element_type=jnp.float32
    )
    return named & (earlier == rank.astype(jnp.float32)), group


def slot_meta(ids, gates, mine, group, locals_):
    lane = lax.broadcasted_iota(jnp.int32, (mine.shape[0], LANES), 1)
    meta = jnp.zeros((mine.shape[0], LANES), jnp.float32)
    for j in range(locals_):
        value = jnp.zeros(mine.shape, jnp.float32)
        for k in range(ids.shape[0]):
            value = value + jnp.where(
                mine & (ids[k : k + 1, :] == group * locals_ + j), gates[k : k + 1, :], 0.0
            )
        meta = jnp.where(lane == j, jnp.sum(value, axis=1, keepdims=True), meta)
    token = lax.broadcasted_iota(jnp.int32, mine.shape, 1).astype(jnp.float32)
    token = jnp.sum(jnp.where(mine, token, 0.0), axis=1, keepdims=True)
    return jnp.where(lane == locals_, token, meta).astype(jnp.bfloat16)


def prepare_kernel(locals_, groups, per_group, tok, scores_t, ids_t, out_a, out_b, plain, pick):
    ids = ids_t[...]
    names = ids.shape[0]
    mine, group = slot_maps(ids, groups, per_group, 2)
    onehot = mine.astype(jnp.bfloat16)
    pick[...] = onehot
    score = scores_t[...]
    total = score[0:1, :]
    for k in range(1, names):
        total = total + score[k : k + 1, :]
    gates = (2.5 * score / total).astype(jnp.bfloat16).astype(jnp.float32)
    width, half = tok.shape[1], mine.shape[0] // 2
    meta = slot_meta(ids, gates, mine, group, locals_)
    out_a[:, width : width + LANES] = meta[:half]
    out_b[:, width : width + LANES] = meta[half:]
    row = lax.broadcasted_iota(jnp.int32, (LANES, tok.shape[0]), 0)
    routes = jnp.zeros((LANES, tok.shape[0]), jnp.float32)
    for k in range(names):
        routes = jnp.where(row == k, ids[k : k + 1, :].astype(jnp.float32), routes)
        routes = jnp.where(row == names + k, gates[k : k + 1, :], routes)
    plain[:, width : width + LANES] = routes.T.astype(jnp.bfloat16)
    for start in range(0, width, 4 * LANES):
        restored = []
        for place in range(start, start + 4 * LANES, LANES):
            x = tok[:, place : place + LANES].astype(jnp.float32)
            largest = jnp.max(jnp.abs(x), axis=1, keepdims=True)
            scale = ((largest + 1e-06) / 448.0).astype(jnp.bfloat16).astype(jnp.float32)
            quantized = (x * (1.0 / scale)).astype(jnp.bfloat16).astype(jnp.float32)
            restored.append((quantized * scale).astype(jnp.bfloat16))
        cols = slice(start, start + 4 * LANES)
        restored = jnp.concatenate(restored, axis=1)
        plain[:, cols] = restored
        rows = jnp.dot(onehot, restored, preferred_element_type=jnp.float32).astype(jnp.bfloat16)
        out_a[:, cols] = rows[:half]
        out_b[:, cols] = rows[half:]


def prepare(tokens, gate_scores, expert_ids, groups, locals_):
    count, width = tokens.shape
    per_group = 2 * count // groups
    slots = groups * per_group
    return pl.pallas_call(
        functools.partial(prepare_kernel, locals_, groups, per_group),
        out_shape=[
            jax.ShapeDtypeStruct((slots // 2, width + LANES), jnp.bfloat16),
            jax.ShapeDtypeStruct((slots // 2, width + LANES), jnp.bfloat16),
            jax.ShapeDtypeStruct((count, width + LANES), jnp.bfloat16),
            jax.ShapeDtypeStruct((slots, count), jnp.bfloat16),
        ],
        compiler_params=pltpu.CompilerParams(vmem_limit_bytes=VMEM),
        cost_estimate=pl.CostEstimate(flops=10**9, bytes_accessed=4 * 10**6, transcendentals=0),
    )(tokens, gate_scores.T, expert_ids.T)


def regroup_kernel(locals_, groups, names, plain, out):
    width = plain.shape[1] - LANES
    routes = plain[:, width:].astype(jnp.float32).T
    ids, gates = routes[:names].astype(jnp.int32), routes[names : 2 * names]
    mine, group = slot_maps(ids, groups, out.shape[0] // groups, 1)
    out[:, width:] = slot_meta(ids, gates, mine, group, locals_)
    onehot = mine.astype(jnp.bfloat16)
    for start in range(0, width, 4 * LANES):
        cols = slice(start, start + 4 * LANES)
        rows = jnp.dot(onehot, plain[:, cols], preferred_element_type=jnp.float32)
        out[:, cols] = rows.astype(jnp.bfloat16)


def expert_kernel(blocks, local_ref, *refs):
    xs, (wg, wu, wd), outs = refs[:blocks], refs[blocks : blocks + 3], refs[blocks + 3 : -2]
    rows, acc = refs[-2:]
    step, steps = pl.program_id(0), pl.num_programs(0)
    width = rows.shape[1]
    starts = [sum(x.shape[0] for x in xs[:b]) for b in range(blocks)]

    @pl.when(step == 0)
    def _():
        for b in range(blocks):
            rows[starts[b] : starts[b] + xs[b].shape[0], :] = xs[b][:, :width]

    x = rows[...]
    gate = jnp.dot(x, wg[0], preferred_element_type=jnp.float32)
    up = jnp.dot(x, wu[0], preferred_element_type=jnp.float32)
    hidden = (gate / (1.0 + jnp.exp(-gate)) * up).astype(jnp.bfloat16)
    part = jnp.dot(hidden, wd[0], preferred_element_type=jnp.float32)

    @pl.when(step == 0)
    def _():
        acc[...] = part

    @pl.when((step > 0) & (step < steps - 1))
    def _():
        acc[...] += part

    @pl.when(step == steps - 1)
    def _():
        for b in range(blocks):
            meta = xs[b][:, width : width + LANES]
            lane = lax.broadcasted_iota(jnp.int32, meta.shape, 1)
            weight = jnp.where(lane == local_ref[0], meta.astype(jnp.float32), 0.0)
            weight = jnp.sum(weight, axis=1, keepdims=True)
            own = slice(starts[b], starts[b] + xs[b].shape[0])
            outs[b][:, :width] = ((acc[own, :] + part[own, :]) * weight).astype(jnp.bfloat16)
            if outs[b].shape[1] > width:
                outs[b][:, width:] = meta


def experts(xs, marked, local, w_gate, w_up, w_down, tile=256):
    blocks, wide = len(xs), xs[0].shape[1]
    high = sum(x.shape[0] for x in xs)
    width, hidden = w_gate.shape[1:]
    outs = [(x.shape[0], wide if b in marked else width) for b, x in enumerate(xs)]
    return pl.pallas_call(
        functools.partial(expert_kernel, blocks),
        grid=(hidden // tile,),
        in_specs=[pl.BlockSpec(memory_space=pltpu.SMEM)]
        + [pl.BlockSpec(x.shape, lambda i: (0, 0)) for x in xs]
        + [
            pl.BlockSpec((1, width, tile), lambda i: (0, 0, i)),
            pl.BlockSpec((1, width, tile), lambda i: (0, 0, i)),
            pl.BlockSpec((1, tile, width), lambda i: (0, i, 0)),
        ],
        out_specs=[pl.BlockSpec(out, lambda i: (0, 0)) for out in outs],
        out_shape=[jax.ShapeDtypeStruct(out, jnp.bfloat16) for out in outs],
        scratch_shapes=[
            pltpu.VMEM((high, width), jnp.bfloat16),
            pltpu.VMEM((high, width), jnp.float32),
        ],
        compiler_params=pltpu.CompilerParams(
            vmem_limit_bytes=EXPERT_VMEM, dimension_semantics=("arbitrary",)
        ),
        cost_estimate=pl.CostEstimate(
            flops=6 * high * width * hidden,
            bytes_accessed=6 * width * hidden,
            transcendentals=high * hidden,
        ),
    )(local, *xs, w_gate, w_up, w_down)


def whole(kernel, shapes, *arrays):
    moved = sum(x.size * x.dtype.itemsize for x in arrays)
    return pl.pallas_call(
        kernel,
        out_shape=shapes,
        compiler_params=pltpu.CompilerParams(vmem_limit_bytes=VMEM),
        cost_estimate=pl.CostEstimate(flops=10**8, bytes_accessed=3 * moved, transcendentals=0),
    )(*arrays)


def to_tokens(pick, rows):
    return lax.dot_general(pick, rows, (((0,), (0,)), ((), ())), preferred_element_type=jnp.float32)


def scatter_kernel(locals_, rows, out):
    count, width = out.shape
    meta = rows[:, width:].astype(jnp.float32)
    lane = lax.broadcasted_iota(jnp.int32, meta.shape, 1)
    token = jnp.sum(jnp.where(lane == locals_, meta, 0.0), axis=1, keepdims=True)
    lane = lax.broadcasted_iota(jnp.int32, (rows.shape[0], count), 1)
    pick = (lane.astype(jnp.float32) == token).astype(jnp.bfloat16)
    out[...] = to_tokens(pick, rows[:, :width]).astype(jnp.bfloat16)


def collect_kernel(pick, first, second, far, out):
    total = to_tokens(pick[:PIECE, :], first[...]) + to_tokens(pick[PIECE:, :], second[...])
    out[...] = (total + far[...].astype(jnp.float32)).astype(jnp.bfloat16)


def per_device(tokens, gate_scores, expert_ids, w_gate, w_up, w_down):
    groups, locals_ = lax.axis_size("node"), lax.axis_size("local")
    local = lax.axis_index("local").astype(jnp.int32).reshape(1)
    tie = lax.optimization_barrier

    def across(block):
        parts = block.reshape(groups, block.shape[0] // groups, block.shape[1])
        return lax.all_to_all(parts, "node", 0, 0, tiled=True).reshape(block.shape)

    def shift(block, by):
        return lax.ppermute(block, "local", [(i, (i + by) % locals_) for i in range(locals_)])

    def up(block):
        return shift(block, 1)

    def down(block):
        return shift(block, -1)

    def add(*blocks):
        total = blocks[0].astype(jnp.float32)
        for block in blocks[1:]:
            total = total + block.astype(jnp.float32)
        return total.astype(jnp.bfloat16)

    run = functools.partial(experts, local=local, w_gate=w_gate, w_up=w_up, w_down=w_down)

    send_a, send_b, plain, pick = prepare(tokens, gate_scores, expert_ids, groups, locals_)
    across_ring = locals_ // 2
    plain = shift(plain, across_ring)
    slots = jax.ShapeDtypeStruct((pick.shape[0], plain.shape[1]), jnp.bfloat16)
    send_far = whole(
        functools.partial(regroup_kernel, locals_, groups, expert_ids.shape[1]), slots, plain
    )
    own_a = across(send_a)
    below_a, above_a = up(own_a), down(own_a)
    send_b, _ = tie((send_b, own_a))
    own_b = across(send_b)
    [own_pa] = run([own_a], ())
    send_far, own_b, own_pa, below_a, above_a = tie((send_far, own_b, own_pa, below_a, above_a))
    far = across(send_far)
    below_b, above_b = up(own_b), down(own_b)
    below_pa, above_pa, own_pb = run([below_a, above_a, own_b], ())
    far, own_pb = tie((far, own_pb))
    [far_p] = run([far], (0,))
    below_b, above_b, far_p = tie((below_b, above_b, far_p))
    below_pb, above_pb = run([below_b, above_b], ())

    far_t = jax.ShapeDtypeStruct(tokens.shape, jnp.bfloat16)
    far = shift(whole(functools.partial(scatter_kernel, locals_), far_t, across(far_p)), across_ring)

    final_a = across(add(own_pa, down(below_pa), up(above_pa)))
    final_b = across(add(own_pb, down(below_pb), up(above_pb)))
    near = [pltpu.with_memory_space_constraint(x, pltpu.VMEM) for x in (final_a, final_b, far)]
    return whole(collect_kernel, jax.ShapeDtypeStruct(tokens.shape, jnp.bfloat16), pick, *near)


def solution(mesh):
    in_specs = (
        P(("dp", "node", "local"), None),
        P(("dp", "node", "local"), None),
        P(("dp", "node", "local"), None),
        P(("node", "local"), None, None),
        P(("node", "local"), None, None),
        P(("node", "local"), None, None),
    )
    out_specs = P(("dp", "node", "local"), None)
    return jax.shard_map(
        per_device, mesh=mesh, in_specs=in_specs, out_specs=out_specs, check_vma=False
    )
```

```python
import functools

import jax
import jax.numpy as jnp
from jax import lax
from jax.experimental import pallas as pl
from jax.experimental.pallas import tpu as pltpu
from jax.sharding import PartitionSpec as P

LANES = 128
PIECE = 128
VMEM = 60 * 1024 * 1024
EXPERT_VMEM = 60 * 1024 * 1024


def slot_maps(ids, groups, per_group, parts):
    slots, tokens = groups * per_group, ids.shape[1]
    slot = lax.broadcasted_iota(jnp.int32, (slots, tokens), 0)
    part_rows, part = per_group // parts, slots // parts
    group = (slot % part) // part_rows
    rank = (slot // part) * part_rows + slot % part_rows
    named = jnp.zeros((slots, tokens), jnp.bool_)
    for k in range(ids.shape[0]):
        named = named | (ids[k : k + 1, :] // 4 == group)
    before = lax.broadcasted_iota(jnp.int32, (tokens, tokens), 0) < lax.broadcasted_iota(
        jnp.int32, (tokens, tokens), 1
    )
    earlier = jnp.dot(
        named.astype(jnp.bfloat16), before.astype(jnp.bfloat16), preferred_element_type=jnp.float32
    )
    return named & (earlier == rank.astype(jnp.float32)), group


def slot_meta(ids, gates, mine, group, locals_):
    lane = lax.broadcasted_iota(jnp.int32, (mine.shape[0], LANES), 1)
    meta = jnp.zeros((mine.shape[0], LANES), jnp.float32)
    for j in range(locals_):
        value = jnp.zeros(mine.shape, jnp.float32)
        for k in range(ids.shape[0]):
            value = value + jnp.where(
                mine & (ids[k : k + 1, :] == group * locals_ + j), gates[k : k + 1, :], 0.0
            )
        meta = jnp.where(lane == j, jnp.sum(value, axis=1, keepdims=True), meta)
    token = lax.broadcasted_iota(jnp.int32, mine.shape, 1).astype(jnp.float32)
    token = jnp.sum(jnp.where(mine, token, 0.0), axis=1, keepdims=True)
    return jnp.where(lane == locals_, token, meta).astype(jnp.bfloat16)


def prepare_kernel(locals_, groups, per_group, tok, scores_t, ids_t, out, plain, pick):
    ids = ids_t[...]
    names = ids.shape[0]
    pick[...] = slot_maps(ids, groups, per_group, 2)[0].astype(jnp.bfloat16)
    mine, group = slot_maps(ids, groups, per_group, 1)
    onehot = mine.astype(jnp.bfloat16)
    score = scores_t[...]
    total = score[0:1, :]
    for k in range(1, names):
        total = total + score[k : k + 1, :]
    gates = (2.5 * score / total).astype(jnp.bfloat16).astype(jnp.float32)
    width = tok.shape[1]
    out[:, width : width + LANES] = slot_meta(ids, gates, mine, group, locals_)
    row = lax.broadcasted_iota(jnp.int32, (LANES, tok.shape[0]), 0)
    routes = jnp.zeros((LANES, tok.shape[0]), jnp.float32)
    for k in range(names):
        routes = jnp.where(row == k, ids[k : k + 1, :].astype(jnp.float32), routes)
        routes = jnp.where(row == names + k, gates[k : k + 1, :], routes)
    plain[:, width : width + LANES] = routes.T.astype(jnp.bfloat16)
    for start in range(0, width, 4 * LANES):
        restored = []
        for place in range(start, start + 4 * LANES, LANES):
            x = tok[:, place : place + LANES].astype(jnp.float32)
            largest = jnp.max(jnp.abs(x), axis=1, keepdims=True)
            scale = ((largest + 1e-06) / 448.0).astype(jnp.bfloat16).astype(jnp.float32)
            quantized = (x * (1.0 / scale)).astype(jnp.bfloat16).astype(jnp.float32)
            restored.append((quantized * scale).astype(jnp.bfloat16))
        cols = slice(start, start + 4 * LANES)
        restored = jnp.concatenate(restored, axis=1)
        plain[:, cols] = restored
        rows = jnp.dot(onehot, restored, preferred_element_type=jnp.float32)
        out[:, cols] = rows.astype(jnp.bfloat16)


def prepare(tokens, gate_scores, expert_ids, groups, locals_):
    count, width = tokens.shape
    per_group = 2 * count // groups
    slots = groups * per_group
    return pl.pallas_call(
        functools.partial(prepare_kernel, locals_, groups, per_group),
        out_shape=[
            jax.ShapeDtypeStruct((slots, width + LANES), jnp.bfloat16),
            jax.ShapeDtypeStruct((count, width + LANES), jnp.bfloat16),
            jax.ShapeDtypeStruct((slots, count), jnp.bfloat16),
        ],
        compiler_params=pltpu.CompilerParams(vmem_limit_bytes=VMEM),
        cost_estimate=pl.CostEstimate(flops=10**9, bytes_accessed=4 * 10**6, transcendentals=0),
    )(tokens, gate_scores.T, expert_ids.T)


def regroup_kernel(locals_, groups, names, plain, out):
    width = plain.shape[1] - LANES
    routes = plain[:, width:].astype(jnp.float32).T
    ids, gates = routes[:names].astype(jnp.int32), routes[names : 2 * names]
    mine, group = slot_maps(ids, groups, out.shape[0] // groups, 1)
    out[:, width:] = slot_meta(ids, gates, mine, group, locals_)
    onehot = mine.astype(jnp.bfloat16)
    for start in range(0, width, 4 * LANES):
        cols = slice(start, start + 4 * LANES)
        rows = jnp.dot(onehot, plain[:, cols], preferred_element_type=jnp.float32)
        out[:, cols] = rows.astype(jnp.bfloat16)


def expert_kernel(blocks, local_ref, *refs):
    xs, (wg, wu, wd), outs = refs[:blocks], refs[blocks : blocks + 3], refs[blocks + 3 : -2]
    rows, acc = refs[-2:]
    step, steps = pl.program_id(0), pl.num_programs(0)
    width = rows.shape[1]
    starts = [sum(x.shape[0] for x in xs[:b]) for b in range(blocks)]

    @pl.when(step == 0)
    def _():
        for b in range(blocks):
            rows[starts[b] : starts[b] + xs[b].shape[0], :] = xs[b][:, :width]

    x = rows[...]
    gate = jnp.dot(x, wg[0], preferred_element_type=jnp.float32)
    up = jnp.dot(x, wu[0], preferred_element_type=jnp.float32)
    hidden = (gate / (1.0 + jnp.exp(-gate)) * up).astype(jnp.bfloat16)
    part = jnp.dot(hidden, wd[0], preferred_element_type=jnp.float32)

    @pl.when(step == 0)
    def _():
        acc[...] = part

    @pl.when((step > 0) & (step < steps - 1))
    def _():
        acc[...] += part

    @pl.when(step == steps - 1)
    def _():
        for b in range(blocks):
            meta = xs[b][:, width : width + LANES]
            lane = lax.broadcasted_iota(jnp.int32, meta.shape, 1)
            weight = jnp.where(lane == local_ref[0], meta.astype(jnp.float32), 0.0)
            weight = jnp.sum(weight, axis=1, keepdims=True)
            own = slice(starts[b], starts[b] + xs[b].shape[0])
            outs[b][:, :width] = ((acc[own, :] + part[own, :]) * weight).astype(jnp.bfloat16)
            if outs[b].shape[1] > width:
                outs[b][:, width:] = meta


def experts(xs, marked, local, w_gate, w_up, w_down, tile=256):
    blocks, wide = len(xs), xs[0].shape[1]
    high = sum(x.shape[0] for x in xs)
    width, hidden = w_gate.shape[1:]
    outs = [(x.shape[0], wide if b in marked else width) for b, x in enumerate(xs)]
    return pl.pallas_call(
        functools.partial(expert_kernel, blocks),
        grid=(hidden // tile,),
        in_specs=[pl.BlockSpec(memory_space=pltpu.SMEM)]
        + [pl.BlockSpec(x.shape, lambda i: (0, 0)) for x in xs]
        + [
            pl.BlockSpec((1, width, tile), lambda i: (0, 0, i)),
            pl.BlockSpec((1, width, tile), lambda i: (0, 0, i)),
            pl.BlockSpec((1, tile, width), lambda i: (0, i, 0)),
        ],
        out_specs=[pl.BlockSpec(out, lambda i: (0, 0)) for out in outs],
        out_shape=[jax.ShapeDtypeStruct(out, jnp.bfloat16) for out in outs],
        scratch_shapes=[
            pltpu.VMEM((high, width), jnp.bfloat16),
            pltpu.VMEM((high, width), jnp.float32),
        ],
        compiler_params=pltpu.CompilerParams(
            vmem_limit_bytes=EXPERT_VMEM, dimension_semantics=("arbitrary",)
        ),
        cost_estimate=pl.CostEstimate(
            flops=6 * high * width * hidden,
            bytes_accessed=6 * width * hidden,
            transcendentals=high * hidden,
        ),
    )(local, *xs, w_gate, w_up, w_down)


def whole(kernel, shapes, *arrays):
    moved = sum(x.size * x.dtype.itemsize for x in arrays)
    return pl.pallas_call(
        kernel,
        out_shape=shapes,
        compiler_params=pltpu.CompilerParams(vmem_limit_bytes=VMEM),
        cost_estimate=pl.CostEstimate(flops=10**8, bytes_accessed=3 * moved, transcendentals=0),
    )(*arrays)


def to_tokens(pick, rows):
    return lax.dot_general(pick, rows, (((0,), (0,)), ((), ())), preferred_element_type=jnp.float32)


def scatter_kernel(locals_, rows, out):
    count, width = out.shape
    meta = rows[:, width:].astype(jnp.float32)
    lane = lax.broadcasted_iota(jnp.int32, meta.shape, 1)
    token = jnp.sum(jnp.where(lane == locals_, meta, 0.0), axis=1, keepdims=True)
    lane = lax.broadcasted_iota(jnp.int32, (rows.shape[0], count), 1)
    pick = (lane.astype(jnp.float32) == token).astype(jnp.bfloat16)
    out[...] = to_tokens(pick, rows[:, :width]).astype(jnp.bfloat16)


def collect_kernel(pick, first, second, far, out):
    total = to_tokens(pick[:PIECE, :], first[...]) + to_tokens(pick[PIECE:, :], second[...])
    out[...] = (total + far[...].astype(jnp.float32)).astype(jnp.bfloat16)


def per_device(tokens, gate_scores, expert_ids, w_gate, w_up, w_down):
    groups, locals_ = lax.axis_size("node"), lax.axis_size("local")
    local = lax.axis_index("local").astype(jnp.int32).reshape(1)
    tie = lax.optimization_barrier

    def across(block):
        parts = block.reshape(groups, block.shape[0] // groups, block.shape[1])
        return lax.all_to_all(parts, "node", 0, 0, tiled=True).reshape(block.shape)

    def shift(block, by):
        return lax.ppermute(block, "local", [(i, (i + by) % locals_) for i in range(locals_)])

    def up(block):
        return shift(block, 1)

    def down(block):
        return shift(block, -1)

    def add(*blocks):
        total = blocks[0].astype(jnp.float32)
        for block in blocks[1:]:
            total = total + block.astype(jnp.float32)
        return total.astype(jnp.bfloat16)

    run = functools.partial(experts, local=local, w_gate=w_gate, w_up=w_up, w_down=w_down)

    send, plain, pick = prepare(tokens, gate_scores, expert_ids, groups, locals_)
    across_ring = locals_ // 2
    plain = shift(plain, across_ring)
    slots = jax.ShapeDtypeStruct(send.shape, jnp.bfloat16)
    send_far = whole(
        functools.partial(regroup_kernel, locals_, groups, expert_ids.shape[1]), slots, plain
    )
    own = across(send).reshape(groups, 2, PIECE // groups, send.shape[1])
    own_a, own_b = (own[:, half].reshape(PIECE, send.shape[1]) for half in range(2))
    below_a, above_a = up(own_a), down(own_a)
    send_far, own_b = tie((send_far, own_b))
    far = across(send_far)
    own_pa, own_pb = run([own_a, own_b], ())
    below_a, above_a, own_b, own_pa = tie((below_a, above_a, own_b, own_pa))
    below_b, above_b = up(own_b), down(own_b)
    below_pa, above_pa = run([below_a, above_a], ())
    far, below_pa = tie((far, below_pa))
    [far_p] = run([far], (0,))
    below_b, above_b, far_p = tie((below_b, above_b, far_p))
    below_pb, above_pb = run([below_b, above_b], ())

    far_t = jax.ShapeDtypeStruct(tokens.shape, jnp.bfloat16)
    far = shift(whole(functools.partial(scatter_kernel, locals_), far_t, across(far_p)), across_ring)

    final_a = across(add(own_pa, down(below_pa), up(above_pa)))
    final_b = across(add(own_pb, down(below_pb), up(above_pb)))
    near = [pltpu.with_memory_space_constraint(x, pltpu.VMEM) for x in (final_a, final_b, far)]
    return whole(collect_kernel, jax.ShapeDtypeStruct(tokens.shape, jnp.bfloat16), pick, *near)


def solution(mesh):
    in_specs = (
        P(("dp", "node", "local"), None),
        P(("dp", "node", "local"), None),
        P(("dp", "node", "local"), None),
        P(("node", "local"), None, None),
        P(("node", "local"), None, None),
        P(("node", "local"), None, None),
    )
    out_specs = P(("dp", "node", "local"), None)
    return jax.shard_map(
        per_device, mesh=mesh, in_specs=in_specs, out_specs=out_specs, check_vma=False
    )
```

```python
import functools

import jax
import jax.numpy as jnp
from jax import lax
from jax.experimental import pallas as pl
from jax.experimental.pallas import tpu as pltpu
from jax.sharding import PartitionSpec as P

LANES = 128
PIECE = 128
VMEM = 60 * 1024 * 1024
EXPERT_VMEM = 48 * 1024 * 1024


def slot_maps(ids_t, groups, per_group):
    slots, tokens = groups * per_group, ids_t.shape[1]
    slot = lax.broadcasted_iota(jnp.int32, (slots, tokens), 0)
    half_rows = per_group // 2
    half = slots // 2
    group = (slot % half) // half_rows
    rank = (slot // half) * half_rows + slot % half_rows
    named = jnp.zeros((slots, tokens), jnp.bool_)
    for k in range(ids_t.shape[0]):
        named = named | (ids_t[k : k + 1, :] // 4 == group)
    before = lax.broadcasted_iota(jnp.int32, (tokens, tokens), 0) < lax.broadcasted_iota(
        jnp.int32, (tokens, tokens), 1
    )
    earlier = jnp.dot(
        named.astype(jnp.bfloat16), before.astype(jnp.bfloat16), preferred_element_type=jnp.float32
    )
    mine = named & (earlier == rank.astype(jnp.float32))
    return mine, group


def prepare_kernel(locals_, groups, per_group, tok, scores_t, ids_t, out_a, out_b, pick):
    ids = ids_t[...]
    mine, group = slot_maps(ids, groups, per_group)
    onehot = mine.astype(jnp.bfloat16)
    pick[...] = onehot
    score = scores_t[...]
    total = score[0:1, :]
    for k in range(1, score.shape[0]):
        total = total + score[k : k + 1, :]
    gates = (2.5 * score / total).astype(jnp.bfloat16).astype(jnp.float32)
    width = tok.shape[1]
    lane = lax.broadcasted_iota(jnp.int32, (mine.shape[0], LANES), 1)
    meta = jnp.zeros((mine.shape[0], LANES), jnp.float32)
    for j in range(locals_):
        value = jnp.zeros(mine.shape, jnp.float32)
        for k in range(ids.shape[0]):
            value = value + jnp.where(
                mine & (ids[k : k + 1, :] == group * locals_ + j), gates[k : k + 1, :], 0.0
            )
        meta = jnp.where(lane == j, jnp.sum(value, axis=1, keepdims=True), meta)
    token = lax.broadcasted_iota(jnp.int32, mine.shape, 1).astype(jnp.float32)
    token = jnp.sum(jnp.where(mine, token, 0.0), axis=1, keepdims=True)
    meta = jnp.where(lane == locals_, token, meta)
    meta = meta.astype(jnp.bfloat16)
    half = mine.shape[0] // 2
    out_a[:, width : width + LANES] = meta[:half]
    out_b[:, width : width + LANES] = meta[half:]
    for start in range(0, width, 4 * LANES):
        restored = []
        for place in range(start, start + 4 * LANES, LANES):
            x = tok[:, place : place + LANES].astype(jnp.float32)
            largest = jnp.max(jnp.abs(x), axis=1, keepdims=True)
            scale = ((largest + 1e-06) / 448.0).astype(jnp.bfloat16).astype(jnp.float32)
            quantized = (x * (1.0 / scale)).astype(jnp.bfloat16).astype(jnp.float32)
            restored.append((quantized * scale).astype(jnp.bfloat16))
        cols = slice(start, start + 4 * LANES)
        restored = jnp.concatenate(restored, axis=1)
        rows = jnp.dot(onehot, restored, preferred_element_type=jnp.float32).astype(jnp.bfloat16)
        out_a[:, cols] = rows[:half]
        out_b[:, cols] = rows[half:]


def prepare(tokens, gate_scores, expert_ids, groups, locals_):
    count, width = tokens.shape
    per_group = 2 * count // groups
    slots = groups * per_group
    return pl.pallas_call(
        functools.partial(prepare_kernel, locals_, groups, per_group),
        out_shape=[
            jax.ShapeDtypeStruct((slots // 2, width + LANES), jnp.bfloat16),
            jax.ShapeDtypeStruct((slots // 2, width + LANES), jnp.bfloat16),
            jax.ShapeDtypeStruct((slots, count), jnp.bfloat16),
        ],
        compiler_params=pltpu.CompilerParams(vmem_limit_bytes=VMEM),
        cost_estimate=pl.CostEstimate(flops=10**9, bytes_accessed=3 * 10**6, transcendentals=0),
    )(tokens, gate_scores.T, expert_ids.T)


def expert_kernel(blocks, local_ref, *refs):
    xs, (wg, wu, wd), outs = refs[:blocks], refs[blocks : blocks + 3], refs[blocks + 3 : -2]
    rows, acc = refs[-2:]
    step, steps = pl.program_id(0), pl.num_programs(0)
    width = rows.shape[1]
    piece = xs[0].shape[0]

    @pl.when(step == 0)
    def _():
        for b in range(blocks):
            rows[b * piece : (b + 1) * piece, :] = xs[b][:, :width]

    x = rows[...]
    gate = jnp.dot(x, wg[0], preferred_element_type=jnp.float32)
    up = jnp.dot(x, wu[0], preferred_element_type=jnp.float32)
    hidden = (gate / (1.0 + jnp.exp(-gate)) * up).astype(jnp.bfloat16)
    part = jnp.dot(hidden, wd[0], preferred_element_type=jnp.float32)

    @pl.when(step == 0)
    def _():
        acc[...] = part

    @pl.when((step > 0) & (step < steps - 1))
    def _():
        acc[...] += part

    @pl.when(step == steps - 1)
    def _():
        for b in range(blocks):
            meta = xs[b][:, width : width + LANES]
            lane = lax.broadcasted_iota(jnp.int32, meta.shape, 1)
            weight = jnp.where(lane == local_ref[0], meta.astype(jnp.float32), 0.0)
            weight = jnp.sum(weight, axis=1, keepdims=True)
            own = slice(b * piece, (b + 1) * piece)
            outs[b][:, :width] = ((acc[own, :] + part[own, :]) * weight).astype(jnp.bfloat16)
            if outs[b].shape[1] > width:
                outs[b][:, width:] = meta


def experts(xs, marked, local, w_gate, w_up, w_down, tile=256):
    blocks = len(xs)
    piece, wide = xs[0].shape
    width, hidden = w_gate.shape[1:]
    wides = [wide if b in marked else width for b in range(blocks)]
    return pl.pallas_call(
        functools.partial(expert_kernel, blocks),
        grid=(hidden // tile,),
        in_specs=[pl.BlockSpec(memory_space=pltpu.SMEM)]
        + [pl.BlockSpec((piece, wide), lambda i: (0, 0))] * blocks
        + [
            pl.BlockSpec((1, width, tile), lambda i: (0, 0, i)),
            pl.BlockSpec((1, width, tile), lambda i: (0, 0, i)),
            pl.BlockSpec((1, tile, width), lambda i: (0, i, 0)),
        ],
        out_specs=[pl.BlockSpec((piece, w), lambda i: (0, 0)) for w in wides],
        out_shape=[jax.ShapeDtypeStruct((piece, w), jnp.bfloat16) for w in wides],
        scratch_shapes=[
            pltpu.VMEM((blocks * piece, width), jnp.bfloat16),
            pltpu.VMEM((blocks * piece, width), jnp.float32),
        ],
        compiler_params=pltpu.CompilerParams(
            vmem_limit_bytes=EXPERT_VMEM, dimension_semantics=("arbitrary",)
        ),
        cost_estimate=pl.CostEstimate(
            flops=6 * blocks * piece * width * hidden,
            bytes_accessed=6 * width * hidden,
            transcendentals=blocks * piece * hidden,
        ),
    )(local, *xs, w_gate, w_up, w_down)


def whole(kernel, shapes, *arrays):
    moved = sum(x.size * x.dtype.itemsize for x in arrays)
    return pl.pallas_call(
        kernel,
        out_shape=shapes,
        compiler_params=pltpu.CompilerParams(vmem_limit_bytes=VMEM),
        cost_estimate=pl.CostEstimate(flops=10**8, bytes_accessed=3 * moved, transcendentals=0),
    )(*arrays)


def to_tokens(pick, rows):
    return lax.dot_general(pick, rows, (((0,), (0,)), ((), ())), preferred_element_type=jnp.float32)


def scatter_kernel(locals_, first, second, out):
    count, width = out.shape
    total = None
    for rows in (first, second):
        meta = rows[:, width:].astype(jnp.float32)
        lane = lax.broadcasted_iota(jnp.int32, meta.shape, 1)
        token = jnp.sum(jnp.where(lane == locals_, meta, 0.0), axis=1, keepdims=True)
        lane = lax.broadcasted_iota(jnp.int32, (rows.shape[0], count), 1)
        part = to_tokens((lane.astype(jnp.float32) == token).astype(jnp.bfloat16), rows[:, :width])
        total = part if total is None else total + part
    out[...] = total.astype(jnp.bfloat16)


def collect_kernel(pick, first, second, far, out):
    total = to_tokens(pick[:PIECE, :], first[...]) + to_tokens(pick[PIECE:, :], second[...])
    out[...] = (total + far[...].astype(jnp.float32)).astype(jnp.bfloat16)


def per_device(tokens, gate_scores, expert_ids, w_gate, w_up, w_down):
    groups, locals_ = lax.axis_size("node"), lax.axis_size("local")
    local = lax.axis_index("local").astype(jnp.int32).reshape(1)
    tie = lax.optimization_barrier

    def across(block):
        parts = block.reshape(groups, block.shape[0] // groups, block.shape[1])
        return lax.all_to_all(parts, "node", 0, 0, tiled=True).reshape(block.shape)

    def shift(block, by):
        return lax.ppermute(block, "local", [(i, (i + by) % locals_) for i in range(locals_)])

    def up(block):
        return shift(block, 1)

    def down(block):
        return shift(block, -1)

    def add(*blocks):
        total = blocks[0].astype(jnp.float32)
        for block in blocks[1:]:
            total = total + block.astype(jnp.float32)
        return total.astype(jnp.bfloat16)

    run = functools.partial(experts, local=local, w_gate=w_gate, w_up=w_up, w_down=w_down)

    send_a, send_b, pick = prepare(tokens, gate_scores, expert_ids, groups, locals_)
    own_a = across(send_a)
    below_a, above_a = up(own_a), down(own_a)
    send_b, _ = tie((send_b, own_a))
    own_b = across(send_b)
    [own_pa] = run([own_a], ())
    below_a, above_a, next_b, own_pa = tie((below_a, above_a, own_b, own_pa))
    far_a, above_b = up(below_a), down(next_b)
    kept = pltpu.with_memory_space_constraint(next_b, pltpu.VMEM)
    below_pa, above_pa, own_pb = run([below_a, above_a, kept], ())
    far_a, above_b, last_b, below_pa = tie((far_a, above_b, next_b, below_pa))
    below_b, far_b = up(last_b), down(above_b)
    far_pa, above_pb = run([far_a, above_b], (0,))
    below_pa, above_pa, far_pa = tie((below_pa, above_pa, far_pa))
    below_b, far_b, above_pb = tie((below_b, far_b, above_pb))
    kept = [pltpu.with_memory_space_constraint(x, pltpu.VMEM) for x in (below_b, far_b)]
    below_pb, far_pb = run(kept, (1,))

    home_a = across(far_pa)
    from_above, from_below = down(below_pa), up(above_pa)
    far_pb, home_a = tie((far_pb, home_a))
    above_pb, below_pb, from_above, from_below, home_a = tie(
        (above_pb, below_pb, from_above, from_below, home_a)
    )
    home_b = across(far_pb)
    far = whole(
        functools.partial(scatter_kernel, locals_),
        jax.ShapeDtypeStruct(tokens.shape, jnp.bfloat16), home_a, home_b,
    )
    far = shift(far, locals_ // 2)

    final_a = across(add(own_pa, from_above, from_below))
    final_b = across(add(own_pb, down(below_pb), up(above_pb)))
    near = [pltpu.with_memory_space_constraint(x, pltpu.VMEM) for x in (final_a, final_b, far)]
    return whole(collect_kernel, jax.ShapeDtypeStruct(tokens.shape, jnp.bfloat16), pick, *near)


def solution(mesh):
    in_specs = (
        P(("dp", "node", "local"), None),
        P(("dp", "node", "local"), None),
        P(("dp", "node", "local"), None),
        P(("node", "local"), None, None),
        P(("node", "local"), None, None),
        P(("node", "local"), None, None),
    )
    out_specs = P(("dp", "node", "local"), None)
    return jax.shard_map(
        per_device, mesh=mesh, in_specs=in_specs, out_specs=out_specs, check_vma=False
    )
```

```python
import functools

import jax
import jax.numpy as jnp
from jax import lax
from jax.experimental import pallas as pl
from jax.experimental.pallas import tpu as pltpu
from jax.sharding import PartitionSpec as P

LANES = 128
PIECE = 128
VMEM = 60 * 1024 * 1024
EXPERT_VMEM = 48 * 1024 * 1024


def slot_maps(ids_t, groups, per_group):
    slots, tokens = groups * per_group, ids_t.shape[1]
    slot = lax.broadcasted_iota(jnp.int32, (slots, tokens), 0)
    half_rows = per_group // 2
    half = slots // 2
    group = (slot % half) // half_rows
    rank = (slot // half) * half_rows + slot % half_rows
    named = jnp.zeros((slots, tokens), jnp.bool_)
    for k in range(ids_t.shape[0]):
        named = named | (ids_t[k : k + 1, :] // 4 == group)
    before = lax.broadcasted_iota(jnp.int32, (tokens, tokens), 0) < lax.broadcasted_iota(
        jnp.int32, (tokens, tokens), 1
    )
    earlier = jnp.dot(
        named.astype(jnp.bfloat16), before.astype(jnp.bfloat16), preferred_element_type=jnp.float32
    )
    mine = named & (earlier == rank.astype(jnp.float32))
    return mine, group


def prepare_kernel(locals_, groups, per_group, tok, scores_t, ids_t, out_a, out_b, pick):
    ids = ids_t[...]
    mine, group = slot_maps(ids, groups, per_group)
    onehot = mine.astype(jnp.bfloat16)
    pick[...] = onehot
    score = scores_t[...]
    total = score[0:1, :]
    for k in range(1, score.shape[0]):
        total = total + score[k : k + 1, :]
    gates = (2.5 * score / total).astype(jnp.bfloat16).astype(jnp.float32)
    width = tok.shape[1]
    lane = lax.broadcasted_iota(jnp.int32, (mine.shape[0], LANES), 1)
    meta = jnp.zeros((mine.shape[0], LANES), jnp.float32)
    for j in range(locals_):
        value = jnp.zeros(mine.shape, jnp.float32)
        for k in range(ids.shape[0]):
            value = value + jnp.where(
                mine & (ids[k : k + 1, :] == group * locals_ + j), gates[k : k + 1, :], 0.0
            )
        meta = jnp.where(lane == j, jnp.sum(value, axis=1, keepdims=True), meta)
    token = lax.broadcasted_iota(jnp.int32, mine.shape, 1).astype(jnp.float32)
    token = jnp.sum(jnp.where(mine, token, 0.0), axis=1, keepdims=True)
    meta = jnp.where(lane == locals_, token, meta)
    meta = meta.astype(jnp.bfloat16)
    half = mine.shape[0] // 2
    out_a[:, width : width + LANES] = meta[:half]
    out_b[:, width : width + LANES] = meta[half:]
    for start in range(0, width, 4 * LANES):
        restored = []
        for place in range(start, start + 4 * LANES, LANES):
            x = tok[:, place : place + LANES].astype(jnp.float32)
            largest = jnp.max(jnp.abs(x), axis=1, keepdims=True)
            scale = ((largest + 1e-06) / 448.0).astype(jnp.bfloat16).astype(jnp.float32)
            quantized = (x * (1.0 / scale)).astype(jnp.bfloat16).astype(jnp.float32)
            restored.append((quantized * scale).astype(jnp.bfloat16))
        cols = slice(start, start + 4 * LANES)
        restored = jnp.concatenate(restored, axis=1)
        rows = jnp.dot(onehot, restored, preferred_element_type=jnp.float32).astype(jnp.bfloat16)
        out_a[:, cols] = rows[:half]
        out_b[:, cols] = rows[half:]


def prepare(tokens, gate_scores, expert_ids, groups, locals_):
    count, width = tokens.shape
    per_group = 2 * count // groups
    slots = groups * per_group
    return pl.pallas_call(
        functools.partial(prepare_kernel, locals_, groups, per_group),
        out_shape=[
            jax.ShapeDtypeStruct((slots // 2, width + LANES), jnp.bfloat16),
            jax.ShapeDtypeStruct((slots // 2, width + LANES), jnp.bfloat16),
            jax.ShapeDtypeStruct((slots, count), jnp.bfloat16),
        ],
        compiler_params=pltpu.CompilerParams(vmem_limit_bytes=VMEM),
        cost_estimate=pl.CostEstimate(flops=10**9, bytes_accessed=3 * 10**6, transcendentals=0),
    )(tokens, gate_scores.T, expert_ids.T)


def expert_kernel(blocks, local_ref, *refs):
    xs, (wg, wu, wd), outs = refs[:blocks], refs[blocks : blocks + 3], refs[blocks + 3 : -2]
    rows, acc = refs[-2:]
    step, steps = pl.program_id(0), pl.num_programs(0)
    width = rows.shape[1]
    piece = xs[0].shape[0]

    @pl.when(step == 0)
    def _():
        for b in range(blocks):
            rows[b * piece : (b + 1) * piece, :] = xs[b][:, :width]

    x = rows[...]
    gate = jnp.dot(x, wg[0], preferred_element_type=jnp.float32)
    up = jnp.dot(x, wu[0], preferred_element_type=jnp.float32)
    hidden = (gate / (1.0 + jnp.exp(-gate)) * up).astype(jnp.bfloat16)
    part = jnp.dot(hidden, wd[0], preferred_element_type=jnp.float32)

    @pl.when(step == 0)
    def _():
        acc[...] = part

    @pl.when((step > 0) & (step < steps - 1))
    def _():
        acc[...] += part

    @pl.when(step == steps - 1)
    def _():
        for b in range(blocks):
            meta = xs[b][:, width : width + LANES]
            lane = lax.broadcasted_iota(jnp.int32, meta.shape, 1)
            weight = jnp.where(lane == local_ref[0], meta.astype(jnp.float32), 0.0)
            weight = jnp.sum(weight, axis=1, keepdims=True)
            own = slice(b * piece, (b + 1) * piece)
            outs[b][:, :width] = ((acc[own, :] + part[own, :]) * weight).astype(jnp.bfloat16)
            if outs[b].shape[1] > width:
                outs[b][:, width:] = meta


def experts(xs, marked, local, w_gate, w_up, w_down, tile=256):
    blocks = len(xs)
    piece, wide = xs[0].shape
    width, hidden = w_gate.shape[1:]
    wides = [wide if b in marked else width for b in range(blocks)]
    return pl.pallas_call(
        functools.partial(expert_kernel, blocks),
        grid=(hidden // tile,),
        in_specs=[pl.BlockSpec(memory_space=pltpu.SMEM)]
        + [pl.BlockSpec((piece, wide), lambda i: (0, 0))] * blocks
        + [
            pl.BlockSpec((1, width, tile), lambda i: (0, 0, i)),
            pl.BlockSpec((1, width, tile), lambda i: (0, 0, i)),
            pl.BlockSpec((1, tile, width), lambda i: (0, i, 0)),
        ],
        out_specs=[pl.BlockSpec((piece, w), lambda i: (0, 0)) for w in wides],
        out_shape=[jax.ShapeDtypeStruct((piece, w), jnp.bfloat16) for w in wides],
        scratch_shapes=[
            pltpu.VMEM((blocks * piece, width), jnp.bfloat16),
            pltpu.VMEM((blocks * piece, width), jnp.float32),
        ],
        compiler_params=pltpu.CompilerParams(
            vmem_limit_bytes=EXPERT_VMEM, dimension_semantics=("arbitrary",)
        ),
        cost_estimate=pl.CostEstimate(
            flops=6 * blocks * piece * width * hidden,
            bytes_accessed=6 * width * hidden,
            transcendentals=blocks * piece * hidden,
        ),
    )(local, *xs, w_gate, w_up, w_down)


def whole(kernel, shapes, *arrays):
    moved = sum(x.size * x.dtype.itemsize for x in arrays)
    return pl.pallas_call(
        kernel,
        out_shape=shapes,
        compiler_params=pltpu.CompilerParams(vmem_limit_bytes=VMEM),
        cost_estimate=pl.CostEstimate(flops=10**8, bytes_accessed=3 * moved, transcendentals=0),
    )(*arrays)


def to_tokens(pick, rows):
    return lax.dot_general(pick, rows, (((0,), (0,)), ((), ())), preferred_element_type=jnp.float32)


def scatter_kernel(locals_, first, second, out):
    count, width = out.shape
    total = None
    for rows in (first, second):
        meta = rows[:, width:].astype(jnp.float32)
        lane = lax.broadcasted_iota(jnp.int32, meta.shape, 1)
        token = jnp.sum(jnp.where(lane == locals_, meta, 0.0), axis=1, keepdims=True)
        lane = lax.broadcasted_iota(jnp.int32, (rows.shape[0], count), 1)
        part = to_tokens((lane.astype(jnp.float32) == token).astype(jnp.bfloat16), rows[:, :width])
        total = part if total is None else total + part
    out[...] = total.astype(jnp.bfloat16)


def collect_kernel(pick, first, second, far, out):
    total = to_tokens(pick[:PIECE, :], first[...]) + to_tokens(pick[PIECE:, :], second[...])
    out[...] = (total + far[...].astype(jnp.float32)).astype(jnp.bfloat16)


def per_device(tokens, gate_scores, expert_ids, w_gate, w_up, w_down):
    groups, locals_ = lax.axis_size("node"), lax.axis_size("local")
    local = lax.axis_index("local").astype(jnp.int32).reshape(1)
    tie = lax.optimization_barrier

    def across(block):
        parts = block.reshape(groups, block.shape[0] // groups, block.shape[1])
        return lax.all_to_all(parts, "node", 0, 0, tiled=True).reshape(block.shape)

    def shift(block, by):
        return lax.ppermute(block, "local", [(i, (i + by) % locals_) for i in range(locals_)])

    def up(block):
        return shift(block, 1)

    def down(block):
        return shift(block, -1)

    def add(*blocks):
        total = blocks[0].astype(jnp.float32)
        for block in blocks[1:]:
            total = total + block.astype(jnp.float32)
        return total.astype(jnp.bfloat16)

    run = functools.partial(experts, local=local, w_gate=w_gate, w_up=w_up, w_down=w_down)

    send_a, send_b, pick = prepare(tokens, gate_scores, expert_ids, groups, locals_)
    own_a = across(send_a)
    below_a, above_a = up(own_a), down(own_a)
    send_b, _ = tie((send_b, own_a))
    own_b = across(send_b)
    [own_pa] = run([own_a], ())
    below_a, above_a, next_b, own_pa = tie((below_a, above_a, own_b, own_pa))
    far_a, above_b = up(below_a), down(next_b)
    kept = pltpu.with_memory_space_constraint(next_b, pltpu.VMEM)
    below_pa, above_pa, own_pb = run([below_a, above_a, kept], ())
    far_a, above_b, last_b, below_pa = tie((far_a, above_b, next_b, below_pa))
    below_b, far_b = up(last_b), down(above_b)
    far_pa, above_pb = run([far_a, above_b], (0,))
    below_pa, above_pa, far_pa = tie((below_pa, above_pa, far_pa))
    below_b, far_b, above_pb = tie((below_b, far_b, above_pb))
    kept = [pltpu.with_memory_space_constraint(x, pltpu.VMEM) for x in (below_b, far_b)]
    below_pb, far_pb = run(kept, (1,))

    home_a = across(far_pa)
    from_above, from_below = down(below_pa), up(above_pa)
    far_pb, home_a = tie((far_pb, home_a))
    above_pb, below_pb, from_above, from_below, home_a = tie(
        (above_pb, below_pb, from_above, from_below, home_a)
    )
    home_b = across(far_pb)
    far = whole(
        functools.partial(scatter_kernel, locals_),
        jax.ShapeDtypeStruct(tokens.shape, jnp.bfloat16), home_a, home_b,
    )
    last_above, last_below = down(below_pb), up(above_pb)
    far, last_above, last_below = tie((far, last_above, last_below))
    far = shift(far, locals_ // 2)

    final_a = across(add(own_pa, from_above, from_below))
    final_b = across(add(own_pb, last_above, last_below))
    near = [pltpu.with_memory_space_constraint(x, pltpu.VMEM) for x in (final_a, final_b, far)]
    return whole(collect_kernel, jax.ShapeDtypeStruct(tokens.shape, jnp.bfloat16), pick, *near)


def solution(mesh):
    in_specs = (
        P(("dp", "node", "local"), None),
        P(("dp", "node", "local"), None),
        P(("dp", "node", "local"), None),
        P(("node", "local"), None, None),
        P(("node", "local"), None, None),
        P(("node", "local"), None, None),
    )
    out_specs = P(("dp", "node", "local"), None)
    return jax.shard_map(
        per_device, mesh=mesh, in_specs=in_specs, out_specs=out_specs, check_vma=False
    )
```

```python
import functools

import jax
import jax.numpy as jnp
from jax import lax
from jax.experimental import pallas as pl
from jax.experimental.pallas import tpu as pltpu
from jax.sharding import PartitionSpec as P

LANES = 128
PIECE = 128
VMEM = 60 * 1024 * 1024
EXPERT_VMEM = 48 * 1024 * 1024


def slot_maps(ids_t, groups, per_group):
    slots, tokens = groups * per_group, ids_t.shape[1]
    slot = lax.broadcasted_iota(jnp.int32, (slots, tokens), 0)
    half_rows = per_group // 2
    half = slots // 2
    group = (slot % half) // half_rows
    rank = (slot // half) * half_rows + slot % half_rows
    named = jnp.zeros((slots, tokens), jnp.bool_)
    for k in range(ids_t.shape[0]):
        named = named | (ids_t[k : k + 1, :] // 4 == group)
    before = lax.broadcasted_iota(jnp.int32, (tokens, tokens), 0) < lax.broadcasted_iota(
        jnp.int32, (tokens, tokens), 1
    )
    earlier = jnp.dot(
        named.astype(jnp.bfloat16), before.astype(jnp.bfloat16), preferred_element_type=jnp.float32
    )
    mine = named & (earlier == rank.astype(jnp.float32))
    return mine, group


def prepare_kernel(locals_, groups, per_group, tok, scores_t, ids_t, out_a, out_b, pick):
    ids = ids_t[...]
    mine, group = slot_maps(ids, groups, per_group)
    onehot = mine.astype(jnp.bfloat16)
    pick[...] = onehot
    score = scores_t[...]
    total = score[0:1, :]
    for k in range(1, score.shape[0]):
        total = total + score[k : k + 1, :]
    gates = (2.5 * score / total).astype(jnp.bfloat16).astype(jnp.float32)
    width = tok.shape[1]
    lane = lax.broadcasted_iota(jnp.int32, (mine.shape[0], LANES), 1)
    meta = jnp.zeros((mine.shape[0], LANES), jnp.float32)
    for j in range(locals_):
        value = jnp.zeros(mine.shape, jnp.float32)
        for k in range(ids.shape[0]):
            value = value + jnp.where(
                mine & (ids[k : k + 1, :] == group * locals_ + j), gates[k : k + 1, :], 0.0
            )
        meta = jnp.where(lane == j, jnp.sum(value, axis=1, keepdims=True), meta)
    token = lax.broadcasted_iota(jnp.int32, mine.shape, 1).astype(jnp.float32)
    token = jnp.sum(jnp.where(mine, token, 0.0), axis=1, keepdims=True)
    meta = jnp.where(lane == locals_, token, meta)
    meta = meta.astype(jnp.bfloat16)
    half = mine.shape[0] // 2
    out_a[:, width : width + LANES] = meta[:half]
    out_b[:, width : width + LANES] = meta[half:]
    for start in range(0, width, 4 * LANES):
        restored = []
        for place in range(start, start + 4 * LANES, LANES):
            x = tok[:, place : place + LANES].astype(jnp.float32)
            largest = jnp.max(jnp.abs(x), axis=1, keepdims=True)
            scale = ((largest + 1e-06) / 448.0).astype(jnp.bfloat16).astype(jnp.float32)
            quantized = (x * (1.0 / scale)).astype(jnp.bfloat16).astype(jnp.float32)
            restored.append((quantized * scale).astype(jnp.bfloat16))
        cols = slice(start, start + 4 * LANES)
        restored = jnp.concatenate(restored, axis=1)
        rows = jnp.dot(onehot, restored, preferred_element_type=jnp.float32).astype(jnp.bfloat16)
        out_a[:, cols] = rows[:half]
        out_b[:, cols] = rows[half:]


def prepare(tokens, gate_scores, expert_ids, groups, locals_):
    count, width = tokens.shape
    per_group = 2 * count // groups
    slots = groups * per_group
    return pl.pallas_call(
        functools.partial(prepare_kernel, locals_, groups, per_group),
        out_shape=[
            jax.ShapeDtypeStruct((slots // 2, width + LANES), jnp.bfloat16),
            jax.ShapeDtypeStruct((slots // 2, width + LANES), jnp.bfloat16),
            jax.ShapeDtypeStruct((slots, count), jnp.bfloat16),
        ],
        compiler_params=pltpu.CompilerParams(vmem_limit_bytes=VMEM),
        cost_estimate=pl.CostEstimate(flops=10**9, bytes_accessed=3 * 10**6, transcendentals=0),
    )(tokens, gate_scores.T, expert_ids.T)


def expert_kernel(blocks, local_ref, *refs):
    xs, (wg, wu, wd), outs = refs[:blocks], refs[blocks : blocks + 3], refs[blocks + 3 : -2]
    rows, acc = refs[-2:]
    step, steps = pl.program_id(0), pl.num_programs(0)
    width = rows.shape[1]
    piece = xs[0].shape[0]

    @pl.when(step == 0)
    def _():
        for b in range(blocks):
            rows[b * piece : (b + 1) * piece, :] = xs[b][:, :width]

    x = rows[...]
    gate = jnp.dot(x, wg[0], preferred_element_type=jnp.float32)
    up = jnp.dot(x, wu[0], preferred_element_type=jnp.float32)
    hidden = (gate / (1.0 + jnp.exp(-gate)) * up).astype(jnp.bfloat16)
    part = jnp.dot(hidden, wd[0], preferred_element_type=jnp.float32)

    @pl.when(step == 0)
    def _():
        acc[...] = part

    @pl.when((step > 0) & (step < steps - 1))
    def _():
        acc[...] += part

    @pl.when(step == steps - 1)
    def _():
        for b in range(blocks):
            meta = xs[b][:, width : width + LANES]
            lane = lax.broadcasted_iota(jnp.int32, meta.shape, 1)
            weight = jnp.where(lane == local_ref[0], meta.astype(jnp.float32), 0.0)
            weight = jnp.sum(weight, axis=1, keepdims=True)
            own = slice(b * piece, (b + 1) * piece)
            outs[b][:, :width] = ((acc[own, :] + part[own, :]) * weight).astype(jnp.bfloat16)
            if outs[b].shape[1] > width:
                outs[b][:, width:] = meta


def experts(xs, marked, local, w_gate, w_up, w_down, tile=256):
    blocks = len(xs)
    piece, wide = xs[0].shape
    width, hidden = w_gate.shape[1:]
    wides = [wide if b in marked else width for b in range(blocks)]
    return pl.pallas_call(
        functools.partial(expert_kernel, blocks),
        grid=(hidden // tile,),
        in_specs=[pl.BlockSpec(memory_space=pltpu.SMEM)]
        + [pl.BlockSpec((piece, wide), lambda i: (0, 0))] * blocks
        + [
            pl.BlockSpec((1, width, tile), lambda i: (0, 0, i)),
            pl.BlockSpec((1, width, tile), lambda i: (0, 0, i)),
            pl.BlockSpec((1, tile, width), lambda i: (0, i, 0)),
        ],
        out_specs=[pl.BlockSpec((piece, w), lambda i: (0, 0)) for w in wides],
        out_shape=[jax.ShapeDtypeStruct((piece, w), jnp.bfloat16) for w in wides],
        scratch_shapes=[
            pltpu.VMEM((blocks * piece, width), jnp.bfloat16),
            pltpu.VMEM((blocks * piece, width), jnp.float32),
        ],
        compiler_params=pltpu.CompilerParams(
            vmem_limit_bytes=EXPERT_VMEM, dimension_semantics=("arbitrary",)
        ),
        cost_estimate=pl.CostEstimate(
            flops=6 * blocks * piece * width * hidden,
            bytes_accessed=6 * width * hidden,
            transcendentals=blocks * piece * hidden,
        ),
    )(local, *xs, w_gate, w_up, w_down)


def whole(kernel, shapes, *arrays):
    moved = sum(x.size * x.dtype.itemsize for x in arrays)
    return pl.pallas_call(
        kernel,
        out_shape=shapes,
        compiler_params=pltpu.CompilerParams(vmem_limit_bytes=VMEM),
        cost_estimate=pl.CostEstimate(flops=10**8, bytes_accessed=3 * moved, transcendentals=0),
    )(*arrays)


def to_tokens(pick, rows):
    return lax.dot_general(pick, rows, (((0,), (0,)), ((), ())), preferred_element_type=jnp.float32)


def scatter_kernel(locals_, first, second, out):
    count, width = out.shape
    total = None
    for rows in (first, second):
        meta = rows[:, width:].astype(jnp.float32)
        lane = lax.broadcasted_iota(jnp.int32, meta.shape, 1)
        token = jnp.sum(jnp.where(lane == locals_, meta, 0.0), axis=1, keepdims=True)
        lane = lax.broadcasted_iota(jnp.int32, (rows.shape[0], count), 1)
        part = to_tokens((lane.astype(jnp.float32) == token).astype(jnp.bfloat16), rows[:, :width])
        total = part if total is None else total + part
    out[...] = total.astype(jnp.bfloat16)


def collect_kernel(pick, first, second, far, out):
    total = to_tokens(pick[:PIECE, :], first[...]) + to_tokens(pick[PIECE:, :], second[...])
    out[...] = (total + far[...].astype(jnp.float32)).astype(jnp.bfloat16)


def per_device(tokens, gate_scores, expert_ids, w_gate, w_up, w_down):
    groups, locals_ = lax.axis_size("node"), lax.axis_size("local")
    local = lax.axis_index("local").astype(jnp.int32).reshape(1)
    tie = lax.optimization_barrier

    def across(block):
        parts = block.reshape(groups, block.shape[0] // groups, block.shape[1])
        return lax.all_to_all(parts, "node", 0, 0, tiled=True).reshape(block.shape)

    def shift(block, by):
        return lax.ppermute(block, "local", [(i, (i + by) % locals_) for i in range(locals_)])

    def up(block):
        return shift(block, 1)

    def down(block):
        return shift(block, -1)

    def add(*blocks):
        total = blocks[0].astype(jnp.float32)
        for block in blocks[1:]:
            total = total + block.astype(jnp.float32)
        return total.astype(jnp.bfloat16)

    run = functools.partial(experts, local=local, w_gate=w_gate, w_up=w_up, w_down=w_down)

    send_a, send_b, pick = prepare(tokens, gate_scores, expert_ids, groups, locals_)
    own_a = across(send_a)
    below_a, above_a = up(own_a), down(own_a)
    send_b, _ = tie((send_b, own_a))
    own_b = across(send_b)
    [own_pa] = run([own_a], ())
    below_a, above_a, next_b, own_pa = tie((below_a, above_a, own_b, own_pa))
    far_a, above_b = up(below_a), down(next_b)
    kept = pltpu.with_memory_space_constraint(next_b, pltpu.VMEM)
    below_pa, above_pa, own_pb = run([below_a, above_a, kept], ())
    below_b = up(next_b)
    far_a, above_b, below_pa = tie((far_a, above_b, below_pa))
    far_b = down(above_b)
    far_pa, above_pb = run([far_a, above_b], (0,))
    below_pa, above_pa, far_pa = tie((below_pa, above_pa, far_pa))
    below_b, far_b, above_pb = tie((below_b, far_b, above_pb))
    kept = [pltpu.with_memory_space_constraint(x, pltpu.VMEM) for x in (below_b, far_b)]
    below_pb, far_pb = run(kept, (1,))

    home_a = across(far_pa)
    from_above, from_below = down(below_pa), up(above_pa)
    far_pb, home_a = tie((far_pb, home_a))
    above_pb, below_pb, from_above, from_below, home_a = tie(
        (above_pb, below_pb, from_above, from_below, home_a)
    )
    home_b = across(far_pb)
    far = whole(
        functools.partial(scatter_kernel, locals_),
        jax.ShapeDtypeStruct(tokens.shape, jnp.bfloat16), home_a, home_b,
    )
    last_above, last_below = down(below_pb), up(above_pb)
    total_b, far = tie((add(own_pb, last_above, last_below), far))
    far = shift(far, locals_ // 2)

    final_a = across(add(own_pa, from_above, from_below))
    final_b = across(total_b)
    near = [pltpu.with_memory_space_constraint(x, pltpu.VMEM) for x in (final_a, final_b, far)]
    return whole(collect_kernel, jax.ShapeDtypeStruct(tokens.shape, jnp.bfloat16), pick, *near)


def solution(mesh):
    in_specs = (
        P(("dp", "node", "local"), None),
        P(("dp", "node", "local"), None),
        P(("dp", "node", "local"), None),
        P(("node", "local"), None, None),
        P(("node", "local"), None, None),
        P(("node", "local"), None, None),
    )
    out_specs = P(("dp", "node", "local"), None)
    return jax.shard_map(
        per_device, mesh=mesh, in_specs=in_specs, out_specs=out_specs, check_vma=False
    )
```

```python
import functools

import jax
import jax.numpy as jnp
from jax import lax
from jax.experimental import pallas as pl
from jax.experimental.pallas import tpu as pltpu
from jax.sharding import PartitionSpec as P

LANES = 128
PIECE = 128
VMEM = 60 * 1024 * 1024
EXPERT_VMEM = 48 * 1024 * 1024


def slot_maps(ids_t, groups, per_group):
    slots, tokens = groups * per_group, ids_t.shape[1]
    slot = lax.broadcasted_iota(jnp.int32, (slots, tokens), 0)
    half_rows = per_group // 2
    half = slots // 2
    group = (slot % half) // half_rows
    rank = (slot // half) * half_rows + slot % half_rows
    named = jnp.zeros((slots, tokens), jnp.bool_)
    for k in range(ids_t.shape[0]):
        named = named | (ids_t[k : k + 1, :] // 4 == group)
    before = lax.broadcasted_iota(jnp.int32, (tokens, tokens), 0) < lax.broadcasted_iota(
        jnp.int32, (tokens, tokens), 1
    )
    earlier = jnp.dot(
        named.astype(jnp.bfloat16), before.astype(jnp.bfloat16), preferred_element_type=jnp.float32
    )
    mine = named & (earlier == rank.astype(jnp.float32))
    return mine, group


def prepare_kernel(locals_, groups, per_group, tok, scores_t, ids_t, out_a, out_b, pick):
    ids = ids_t[...]
    mine, group = slot_maps(ids, groups, per_group)
    onehot = mine.astype(jnp.bfloat16)
    pick[...] = onehot
    score = scores_t[...]
    total = score[0:1, :]
    for k in range(1, score.shape[0]):
        total = total + score[k : k + 1, :]
    gates = (2.5 * score / total).astype(jnp.bfloat16).astype(jnp.float32)
    width = tok.shape[1]
    lane = lax.broadcasted_iota(jnp.int32, (mine.shape[0], LANES), 1)
    meta = jnp.zeros((mine.shape[0], LANES), jnp.float32)
    for j in range(locals_):
        value = jnp.zeros(mine.shape, jnp.float32)
        for k in range(ids.shape[0]):
            value = value + jnp.where(
                mine & (ids[k : k + 1, :] == group * locals_ + j), gates[k : k + 1, :], 0.0
            )
        meta = jnp.where(lane == j, jnp.sum(value, axis=1, keepdims=True), meta)
    token = lax.broadcasted_iota(jnp.int32, mine.shape, 1).astype(jnp.float32)
    token = jnp.sum(jnp.where(mine, token, 0.0), axis=1, keepdims=True)
    meta = jnp.where(lane == locals_, token, meta)
    meta = meta.astype(jnp.bfloat16)
    half = mine.shape[0] // 2
    out_a[:, width : width + LANES] = meta[:half]
    out_b[:, width : width + LANES] = meta[half:]
    for start in range(0, width, 4 * LANES):
        restored = []
        for place in range(start, start + 4 * LANES, LANES):
            x = tok[:, place : place + LANES].astype(jnp.float32)
            largest = jnp.max(jnp.abs(x), axis=1, keepdims=True)
            scale = ((largest + 1e-06) / 448.0).astype(jnp.bfloat16).astype(jnp.float32)
            quantized = (x * (1.0 / scale)).astype(jnp.bfloat16).astype(jnp.float32)
            restored.append((quantized * scale).astype(jnp.bfloat16))
        cols = slice(start, start + 4 * LANES)
        restored = jnp.concatenate(restored, axis=1)
        rows = jnp.dot(onehot, restored, preferred_element_type=jnp.float32).astype(jnp.bfloat16)
        out_a[:, cols] = rows[:half]
        out_b[:, cols] = rows[half:]


def prepare(tokens, gate_scores, expert_ids, groups, locals_):
    count, width = tokens.shape
    per_group = 2 * count // groups
    slots = groups * per_group
    return pl.pallas_call(
        functools.partial(prepare_kernel, locals_, groups, per_group),
        out_shape=[
            jax.ShapeDtypeStruct((slots // 2, width + LANES), jnp.bfloat16),
            jax.ShapeDtypeStruct((slots // 2, width + LANES), jnp.bfloat16),
            jax.ShapeDtypeStruct((slots, count), jnp.bfloat16),
        ],
        compiler_params=pltpu.CompilerParams(vmem_limit_bytes=VMEM),
        cost_estimate=pl.CostEstimate(flops=10**9, bytes_accessed=3 * 10**6, transcendentals=0),
    )(tokens, gate_scores.T, expert_ids.T)


def expert_kernel(blocks, local_ref, *refs):
    xs, (wg, wu, wd), outs = refs[:blocks], refs[blocks : blocks + 3], refs[blocks + 3 : -2]
    rows, acc = refs[-2:]
    step, steps = pl.program_id(0), pl.num_programs(0)
    width = rows.shape[1]
    piece = xs[0].shape[0]

    @pl.when(step == 0)
    def _():
        for b in range(blocks):
            rows[b * piece : (b + 1) * piece, :] = xs[b][:, :width]

    x = rows[...]
    gate = jnp.dot(x, wg[0], preferred_element_type=jnp.float32)
    up = jnp.dot(x, wu[0], preferred_element_type=jnp.float32)
    hidden = (gate / (1.0 + jnp.exp(-gate)) * up).astype(jnp.bfloat16)
    part = jnp.dot(hidden, wd[0], preferred_element_type=jnp.float32)

    @pl.when(step == 0)
    def _():
        acc[...] = part

    @pl.when((step > 0) & (step < steps - 1))
    def _():
        acc[...] += part

    @pl.when(step == steps - 1)
    def _():
        for b in range(blocks):
            meta = xs[b][:, width : width + LANES]
            lane = lax.broadcasted_iota(jnp.int32, meta.shape, 1)
            weight = jnp.where(lane == local_ref[0], meta.astype(jnp.float32), 0.0)
            weight = jnp.sum(weight, axis=1, keepdims=True)
            own = slice(b * piece, (b + 1) * piece)
            outs[b][:, :width] = ((acc[own, :] + part[own, :]) * weight).astype(jnp.bfloat16)
            if outs[b].shape[1] > width:
                outs[b][:, width:] = meta


def experts(xs, marked, local, w_gate, w_up, w_down, tile=256):
    blocks = len(xs)
    piece, wide = xs[0].shape
    width, hidden = w_gate.shape[1:]
    wides = [wide if b in marked else width for b in range(blocks)]
    return pl.pallas_call(
        functools.partial(expert_kernel, blocks),
        grid=(hidden // tile,),
        in_specs=[pl.BlockSpec(memory_space=pltpu.SMEM)]
        + [pl.BlockSpec((piece, wide), lambda i: (0, 0))] * blocks
        + [
            pl.BlockSpec((1, width, tile), lambda i: (0, 0, i)),
            pl.BlockSpec((1, width, tile), lambda i: (0, 0, i)),
            pl.BlockSpec((1, tile, width), lambda i: (0, i, 0)),
        ],
        out_specs=[pl.BlockSpec((piece, w), lambda i: (0, 0)) for w in wides],
        out_shape=[jax.ShapeDtypeStruct((piece, w), jnp.bfloat16) for w in wides],
        scratch_shapes=[
            pltpu.VMEM((blocks * piece, width), jnp.bfloat16),
            pltpu.VMEM((blocks * piece, width), jnp.float32),
        ],
        compiler_params=pltpu.CompilerParams(
            vmem_limit_bytes=EXPERT_VMEM, dimension_semantics=("arbitrary",)
        ),
        cost_estimate=pl.CostEstimate(
            flops=6 * blocks * piece * width * hidden,
            bytes_accessed=6 * width * hidden,
            transcendentals=blocks * piece * hidden,
        ),
    )(local, *xs, w_gate, w_up, w_down)


def whole(kernel, shapes, *arrays):
    moved = sum(x.size * x.dtype.itemsize for x in arrays)
    return pl.pallas_call(
        kernel,
        out_shape=shapes,
        compiler_params=pltpu.CompilerParams(vmem_limit_bytes=VMEM),
        cost_estimate=pl.CostEstimate(flops=10**8, bytes_accessed=3 * moved, transcendentals=0),
    )(*arrays)


def to_tokens(pick, rows):
    return lax.dot_general(pick, rows, (((0,), (0,)), ((), ())), preferred_element_type=jnp.float32)


def scatter_kernel(locals_, first, second, out):
    count, width = out.shape
    total = None
    for rows in (first, second):
        meta = rows[:, width:].astype(jnp.float32)
        lane = lax.broadcasted_iota(jnp.int32, meta.shape, 1)
        token = jnp.sum(jnp.where(lane == locals_, meta, 0.0), axis=1, keepdims=True)
        lane = lax.broadcasted_iota(jnp.int32, (rows.shape[0], count), 1)
        part = to_tokens((lane.astype(jnp.float32) == token).astype(jnp.bfloat16), rows[:, :width])
        total = part if total is None else total + part
    out[...] = total.astype(jnp.bfloat16)


def collect_kernel(pick, first, second, far, out):
    total = to_tokens(pick[:PIECE, :], first[...]) + to_tokens(pick[PIECE:, :], second[...])
    out[...] = (total + far[...].astype(jnp.float32)).astype(jnp.bfloat16)


def per_device(tokens, gate_scores, expert_ids, w_gate, w_up, w_down):
    groups, locals_ = lax.axis_size("node"), lax.axis_size("local")
    local = lax.axis_index("local").astype(jnp.int32).reshape(1)
    tie = lax.optimization_barrier

    def across(block):
        parts = block.reshape(groups, block.shape[0] // groups, block.shape[1])
        return lax.all_to_all(parts, "node", 0, 0, tiled=True).reshape(block.shape)

    def shift(block, by):
        return lax.ppermute(block, "local", [(i, (i + by) % locals_) for i in range(locals_)])

    def up(block):
        return shift(block, 1)

    def down(block):
        return shift(block, -1)

    def add(*blocks):
        total = blocks[0].astype(jnp.float32)
        for block in blocks[1:]:
            total = total + block.astype(jnp.float32)
        return total.astype(jnp.bfloat16)

    run = functools.partial(experts, local=local, w_gate=w_gate, w_up=w_up, w_down=w_down)

    send_a, send_b, pick = prepare(tokens, gate_scores, expert_ids, groups, locals_)
    own_a = across(send_a)
    below_a, above_a = up(own_a), down(own_a)
    send_b, _ = tie((send_b, own_a))
    own_b = across(send_b)
    [own_pa] = run([own_a], ())
    below_a, above_a, next_b, own_pa = tie((below_a, above_a, own_b, own_pa))
    far_a, above_b = up(below_a), down(next_b)
    kept = pltpu.with_memory_space_constraint(next_b, pltpu.VMEM)
    below_pa, above_pa, own_pb = run([below_a, above_a, kept], ())
    far_a, above_b, last_b, below_pa = tie((far_a, above_b, next_b, below_pa))
    below_b, far_b = up(last_b), down(above_b)
    far_pa, above_pb = run([far_a, above_b], (0,))
    below_pa, above_pa, far_pa = tie((below_pa, above_pa, far_pa))
    below_b, far_b, above_pb = tie((below_b, far_b, above_pb))
    keep = functools.partial(pltpu.with_memory_space_constraint, memory_space=pltpu.VMEM)
    [far_pb] = run([keep(far_b)], (0,))
    below_b, far_pb = tie((below_b, far_pb))
    [below_pb] = run([keep(below_b)], ())

    home_a = across(far_pa)
    from_above, from_below = down(below_pa), up(above_pa)
    far_pb, home_a = tie((far_pb, home_a))
    above_pb, below_pb, from_above, from_below, home_a = tie(
        (above_pb, below_pb, from_above, from_below, home_a)
    )
    home_b = across(far_pb)
    far = whole(
        functools.partial(scatter_kernel, locals_),
        jax.ShapeDtypeStruct(tokens.shape, jnp.bfloat16), home_a, home_b,
    )
    last_above, last_below = down(below_pb), up(above_pb)
    total_b, far = tie((add(own_pb, last_above, last_below), far))
    far = shift(far, locals_ // 2)

    final_a = across(add(own_pa, from_above, from_below))
    final_b = across(total_b)
    near = [pltpu.with_memory_space_constraint(x, pltpu.VMEM) for x in (final_a, final_b, far)]
    return whole(collect_kernel, jax.ShapeDtypeStruct(tokens.shape, jnp.bfloat16), pick, *near)


def solution(mesh):
    in_specs = (
        P(("dp", "node", "local"), None),
        P(("dp", "node", "local"), None),
        P(("dp", "node", "local"), None),
        P(("node", "local"), None, None),
        P(("node", "local"), None, None),
        P(("node", "local"), None, None),
    )
    out_specs = P(("dp", "node", "local"), None)
    return jax.shard_map(
        per_device, mesh=mesh, in_specs=in_specs, out_specs=out_specs, check_vma=False
    )
```

```python
import functools

import jax
import jax.numpy as jnp
from jax import lax
from jax.experimental import pallas as pl
from jax.experimental.pallas import tpu as pltpu
from jax.sharding import PartitionSpec as P

LANES = 128
PIECE = 128
VMEM = 60 * 1024 * 1024
EXPERT_VMEM = 48 * 1024 * 1024


def slot_maps(ids_t, groups, per_group):
    slots, tokens = groups * per_group, ids_t.shape[1]
    slot = lax.broadcasted_iota(jnp.int32, (slots, tokens), 0)
    half_rows = per_group // 2
    half = slots // 2
    group = (slot % half) // half_rows
    rank = (slot // half) * half_rows + slot % half_rows
    named = jnp.zeros((slots, tokens), jnp.bool_)
    for k in range(ids_t.shape[0]):
        named = named | (ids_t[k : k + 1, :] // 4 == group)
    before = lax.broadcasted_iota(jnp.int32, (tokens, tokens), 0) < lax.broadcasted_iota(
        jnp.int32, (tokens, tokens), 1
    )
    earlier = jnp.dot(
        named.astype(jnp.bfloat16), before.astype(jnp.bfloat16), preferred_element_type=jnp.float32
    )
    mine = named & (earlier == rank.astype(jnp.float32))
    return mine, group


def prepare_kernel(locals_, groups, per_group, tok, scores_t, ids_t, out_a, out_b, pick):
    ids = ids_t[...]
    mine, group = slot_maps(ids, groups, per_group)
    onehot = mine.astype(jnp.bfloat16)
    pick[...] = onehot
    score = scores_t[...]
    total = score[0:1, :]
    for k in range(1, score.shape[0]):
        total = total + score[k : k + 1, :]
    gates = (2.5 * score / total).astype(jnp.bfloat16).astype(jnp.float32)
    width = tok.shape[1]
    lane = lax.broadcasted_iota(jnp.int32, (mine.shape[0], LANES), 1)
    meta = jnp.zeros((mine.shape[0], LANES), jnp.float32)
    for j in range(locals_):
        value = jnp.zeros(mine.shape, jnp.float32)
        for k in range(ids.shape[0]):
            value = value + jnp.where(
                mine & (ids[k : k + 1, :] == group * locals_ + j), gates[k : k + 1, :], 0.0
            )
        meta = jnp.where(lane == j, jnp.sum(value, axis=1, keepdims=True), meta)
    token = lax.broadcasted_iota(jnp.int32, mine.shape, 1).astype(jnp.float32)
    token = jnp.sum(jnp.where(mine, token, 0.0), axis=1, keepdims=True)
    meta = jnp.where(lane == locals_, token, meta)
    meta = meta.astype(jnp.bfloat16)
    half = mine.shape[0] // 2
    out_a[:, width : width + LANES] = meta[:half]
    out_b[:, width : width + LANES] = meta[half:]
    for start in range(0, width, 4 * LANES):
        restored = []
        for place in range(start, start + 4 * LANES, LANES):
            x = tok[:, place : place + LANES].astype(jnp.float32)
            largest = jnp.max(jnp.abs(x), axis=1, keepdims=True)
            scale = ((largest + 1e-06) / 448.0).astype(jnp.bfloat16).astype(jnp.float32)
            quantized = (x * (1.0 / scale)).astype(jnp.bfloat16).astype(jnp.float32)
            restored.append((quantized * scale).astype(jnp.bfloat16))
        cols = slice(start, start + 4 * LANES)
        restored = jnp.concatenate(restored, axis=1)
        rows = jnp.dot(onehot, restored, preferred_element_type=jnp.float32).astype(jnp.bfloat16)
        out_a[:, cols] = rows[:half]
        out_b[:, cols] = rows[half:]


def prepare(tokens, gate_scores, expert_ids, groups, locals_):
    count, width = tokens.shape
    per_group = 2 * count // groups
    slots = groups * per_group
    return pl.pallas_call(
        functools.partial(prepare_kernel, locals_, groups, per_group),
        out_shape=[
            jax.ShapeDtypeStruct((slots // 2, width + LANES), jnp.bfloat16),
            jax.ShapeDtypeStruct((slots // 2, width + LANES), jnp.bfloat16),
            jax.ShapeDtypeStruct((slots, count), jnp.bfloat16),
        ],
        compiler_params=pltpu.CompilerParams(vmem_limit_bytes=VMEM),
        cost_estimate=pl.CostEstimate(flops=10**9, bytes_accessed=3 * 10**6, transcendentals=0),
    )(tokens, gate_scores.T, expert_ids.T)


def expert_kernel(blocks, local_ref, *refs):
    xs, (wg, wu, wd), outs = refs[:blocks], refs[blocks : blocks + 3], refs[blocks + 3 : -2]
    rows, acc = refs[-2:]
    step, steps = pl.program_id(0), pl.num_programs(0)
    width = rows.shape[1]
    piece = xs[0].shape[0]

    @pl.when(step == 0)
    def _():
        for b in range(blocks):
            rows[b * piece : (b + 1) * piece, :] = xs[b][:, :width]

    x = rows[...]
    gate = jnp.dot(x, wg[0], preferred_element_type=jnp.float32)
    up = jnp.dot(x, wu[0], preferred_element_type=jnp.float32)
    hidden = (gate / (1.0 + jnp.exp(-gate)) * up).astype(jnp.bfloat16)
    part = jnp.dot(hidden, wd[0], preferred_element_type=jnp.float32)

    @pl.when(step == 0)
    def _():
        acc[...] = part

    @pl.when((step > 0) & (step < steps - 1))
    def _():
        acc[...] += part

    @pl.when(step == steps - 1)
    def _():
        for b in range(blocks):
            meta = xs[b][:, width : width + LANES]
            lane = lax.broadcasted_iota(jnp.int32, meta.shape, 1)
            weight = jnp.where(lane == local_ref[0], meta.astype(jnp.float32), 0.0)
            weight = jnp.sum(weight, axis=1, keepdims=True)
            own = slice(b * piece, (b + 1) * piece)
            outs[b][:, :width] = ((acc[own, :] + part[own, :]) * weight).astype(jnp.bfloat16)
            if outs[b].shape[1] > width:
                outs[b][:, width:] = meta


def experts(xs, marked, local, w_gate, w_up, w_down, tile=256):
    blocks = len(xs)
    piece, wide = xs[0].shape
    width, hidden = w_gate.shape[1:]
    wides = [wide if b in marked else width for b in range(blocks)]
    return pl.pallas_call(
        functools.partial(expert_kernel, blocks),
        grid=(hidden // tile,),
        in_specs=[pl.BlockSpec(memory_space=pltpu.SMEM)]
        + [pl.BlockSpec((piece, wide), lambda i: (0, 0))] * blocks
        + [
            pl.BlockSpec((1, width, tile), lambda i: (0, 0, i)),
            pl.BlockSpec((1, width, tile), lambda i: (0, 0, i)),
            pl.BlockSpec((1, tile, width), lambda i: (0, i, 0)),
        ],
        out_specs=[pl.BlockSpec((piece, w), lambda i: (0, 0)) for w in wides],
        out_shape=[jax.ShapeDtypeStruct((piece, w), jnp.bfloat16) for w in wides],
        scratch_shapes=[
            pltpu.VMEM((blocks * piece, width), jnp.bfloat16),
            pltpu.VMEM((blocks * piece, width), jnp.float32),
        ],
        compiler_params=pltpu.CompilerParams(
            vmem_limit_bytes=EXPERT_VMEM, dimension_semantics=("arbitrary",)
        ),
        cost_estimate=pl.CostEstimate(
            flops=6 * blocks * piece * width * hidden,
            bytes_accessed=6 * width * hidden,
            transcendentals=blocks * piece * hidden,
        ),
    )(local, *xs, w_gate, w_up, w_down)


def whole(kernel, shapes, *arrays):
    moved = sum(x.size * x.dtype.itemsize for x in arrays)
    return pl.pallas_call(
        kernel,
        out_shape=shapes,
        compiler_params=pltpu.CompilerParams(vmem_limit_bytes=VMEM),
        cost_estimate=pl.CostEstimate(flops=10**8, bytes_accessed=3 * moved, transcendentals=0),
    )(*arrays)


def to_tokens(pick, rows):
    return lax.dot_general(pick, rows, (((0,), (0,)), ((), ())), preferred_element_type=jnp.float32)


def scatter_kernel(locals_, first, second, out):
    count, width = out.shape
    total = None
    for rows in (first, second):
        meta = rows[:, width:].astype(jnp.float32)
        lane = lax.broadcasted_iota(jnp.int32, meta.shape, 1)
        token = jnp.sum(jnp.where(lane == locals_, meta, 0.0), axis=1, keepdims=True)
        lane = lax.broadcasted_iota(jnp.int32, (rows.shape[0], count), 1)
        part = to_tokens((lane.astype(jnp.float32) == token).astype(jnp.bfloat16), rows[:, :width])
        total = part if total is None else total + part
    out[...] = total.astype(jnp.bfloat16)


def collect_kernel(pick, first, second, far, out):
    total = to_tokens(pick[:PIECE, :], first[...]) + to_tokens(pick[PIECE:, :], second[...])
    out[...] = (total + far[...].astype(jnp.float32)).astype(jnp.bfloat16)


def per_device(tokens, gate_scores, expert_ids, w_gate, w_up, w_down):
    groups, locals_ = lax.axis_size("node"), lax.axis_size("local")
    local = lax.axis_index("local").astype(jnp.int32).reshape(1)
    tie = lax.optimization_barrier

    def across(block):
        parts = block.reshape(groups, block.shape[0] // groups, block.shape[1])
        return lax.all_to_all(parts, "node", 0, 0, tiled=True).reshape(block.shape)

    def shift(block, by):
        return lax.ppermute(block, "local", [(i, (i + by) % locals_) for i in range(locals_)])

    def up(block):
        return shift(block, 1)

    def down(block):
        return shift(block, -1)

    def add(*blocks):
        total = blocks[0].astype(jnp.float32)
        for block in blocks[1:]:
            total = total + block.astype(jnp.float32)
        return total.astype(jnp.bfloat16)

    run = functools.partial(experts, local=local, w_gate=w_gate, w_up=w_up, w_down=w_down)

    send_a, send_b, pick = prepare(tokens, gate_scores, expert_ids, groups, locals_)
    own_a = across(send_a)
    below_a, above_a = up(own_a), down(own_a)
    send_b, _ = tie((send_b, own_a))
    own_b = across(send_b)
    [own_pa] = run([own_a], ())
    below_a, above_a, next_b, own_pa = tie((below_a, above_a, own_b, own_pa))
    far_a, above_b = up(below_a), down(next_b)
    kept = pltpu.with_memory_space_constraint(next_b, pltpu.VMEM)
    below_pa, above_pa, own_pb = run([below_a, above_a, kept], ())
    far_a, above_b, last_b, below_pa = tie((far_a, above_b, next_b, below_pa))
    below_b, far_b = up(last_b), down(above_b)
    far_pa, above_pb = run([far_a, above_b], (0,))
    below_pa, above_pa, far_pa = tie((below_pa, above_pa, far_pa))
    below_b, far_b, above_pb = tie((below_b, far_b, above_pb))
    kept = [pltpu.with_memory_space_constraint(x, pltpu.VMEM) for x in (below_b, far_b)]
    below_pb, far_pb = run(kept, (1,))

    home_a = across(far_pa)
    from_above, from_below = down(below_pa), up(above_pa)
    far_pb, home_a = tie((far_pb, home_a))
    above_pb, below_pb, from_above, from_below, home_a = tie(
        (above_pb, below_pb, from_above, from_below, home_a)
    )
    home_b = across(far_pb)
    far = whole(
        functools.partial(scatter_kernel, locals_),
        jax.ShapeDtypeStruct(tokens.shape, jnp.bfloat16), home_a,
        pltpu.with_memory_space_constraint(home_b, pltpu.VMEM),
    )
    last_above, last_below = down(below_pb), up(above_pb)
    total_b, far = tie((add(own_pb, last_above, last_below), far))
    far = shift(far, locals_ // 2)

    final_a = across(add(own_pa, from_above, from_below))
    final_b = across(total_b)
    near = [pltpu.with_memory_space_constraint(x, pltpu.VMEM) for x in (final_a, final_b, far)]
    return whole(collect_kernel, jax.ShapeDtypeStruct(tokens.shape, jnp.bfloat16), pick, *near)


def solution(mesh):
    in_specs = (
        P(("dp", "node", "local"), None),
        P(("dp", "node", "local"), None),
        P(("dp", "node", "local"), None),
        P(("node", "local"), None, None),
        P(("node", "local"), None, None),
        P(("node", "local"), None, None),
    )
    out_specs = P(("dp", "node", "local"), None)
    return jax.shard_map(
        per_device, mesh=mesh, in_specs=in_specs, out_specs=out_specs, check_vma=False
    )
```

```python
import functools

import jax
import jax.numpy as jnp
from jax import lax
from jax.experimental import pallas as pl
from jax.experimental.pallas import tpu as pltpu
from jax.sharding import PartitionSpec as P

LANES = 128
PIECE = 128
VMEM = 60 * 1024 * 1024
PREPARE_VMEM = 34 * 1024 * 1024
EXPERT_VMEM = 48 * 1024 * 1024


def slot_maps(ids_t, groups, per_group):
    slots, tokens = groups * per_group, ids_t.shape[1]
    slot = lax.broadcasted_iota(jnp.int32, (slots, tokens), 0)
    half_rows = per_group // 2
    half = slots // 2
    group = (slot % half) // half_rows
    rank = (slot // half) * half_rows + slot % half_rows
    named = jnp.zeros((slots, tokens), jnp.bool_)
    for k in range(ids_t.shape[0]):
        named = named | (ids_t[k : k + 1, :] // 4 == group)
    before = lax.broadcasted_iota(jnp.int32, (tokens, tokens), 0) < lax.broadcasted_iota(
        jnp.int32, (tokens, tokens), 1
    )
    earlier = jnp.dot(
        named.astype(jnp.bfloat16), before.astype(jnp.bfloat16), preferred_element_type=jnp.float32
    )
    mine = named & (earlier == rank.astype(jnp.float32))
    return mine, group


def prepare_kernel(locals_, groups, per_group, tok, scores_t, ids_t, out_a, out_b, pick):
    ids = ids_t[...]
    mine, group = slot_maps(ids, groups, per_group)
    onehot = mine.astype(jnp.bfloat16)
    pick[...] = onehot
    score = scores_t[...]
    total = score[0:1, :]
    for k in range(1, score.shape[0]):
        total = total + score[k : k + 1, :]
    gates = (2.5 * score / total).astype(jnp.bfloat16).astype(jnp.float32)
    width = tok.shape[1]
    lane = lax.broadcasted_iota(jnp.int32, (mine.shape[0], LANES), 1)
    meta = jnp.zeros((mine.shape[0], LANES), jnp.float32)
    for j in range(locals_):
        value = jnp.zeros(mine.shape, jnp.float32)
        for k in range(ids.shape[0]):
            value = value + jnp.where(
                mine & (ids[k : k + 1, :] == group * locals_ + j), gates[k : k + 1, :], 0.0
            )
        meta = jnp.where(lane == j, jnp.sum(value, axis=1, keepdims=True), meta)
    token = lax.broadcasted_iota(jnp.int32, mine.shape, 1).astype(jnp.float32)
    token = jnp.sum(jnp.where(mine, token, 0.0), axis=1, keepdims=True)
    meta = jnp.where(lane == locals_, token, meta)
    meta = meta.astype(jnp.bfloat16)
    half = mine.shape[0] // 2
    out_a[:, width : width + LANES] = meta[:half]
    out_b[:, width : width + LANES] = meta[half:]
    for start in range(0, width, 4 * LANES):
        restored = []
        for place in range(start, start + 4 * LANES, LANES):
            x = tok[:, place : place + LANES].astype(jnp.float32)
            largest = jnp.max(jnp.abs(x), axis=1, keepdims=True)
            scale = ((largest + 1e-06) / 448.0).astype(jnp.bfloat16).astype(jnp.float32)
            quantized = (x * (1.0 / scale)).astype(jnp.bfloat16).astype(jnp.float32)
            restored.append((quantized * scale).astype(jnp.bfloat16))
        cols = slice(start, start + 4 * LANES)
        restored = jnp.concatenate(restored, axis=1)
        rows = jnp.dot(onehot, restored, preferred_element_type=jnp.float32).astype(jnp.bfloat16)
        out_a[:, cols] = rows[:half]
        out_b[:, cols] = rows[half:]


def prepare(tokens, gate_scores, expert_ids, groups, locals_):
    count, width = tokens.shape
    per_group = 2 * count // groups
    slots = groups * per_group
    return pl.pallas_call(
        functools.partial(prepare_kernel, locals_, groups, per_group),
        out_shape=[
            jax.ShapeDtypeStruct((slots // 2, width + LANES), jnp.bfloat16),
            jax.ShapeDtypeStruct((slots // 2, width + LANES), jnp.bfloat16),
            jax.ShapeDtypeStruct((slots, count), jnp.bfloat16),
        ],
        compiler_params=pltpu.CompilerParams(vmem_limit_bytes=PREPARE_VMEM),
        cost_estimate=pl.CostEstimate(flops=10**9, bytes_accessed=3 * 10**6, transcendentals=0),
    )(tokens, gate_scores.T, expert_ids.T)


def expert_kernel(blocks, local_ref, *refs):
    xs, (wg, wu, wd), outs = refs[:blocks], refs[blocks : blocks + 3], refs[blocks + 3 : -2]
    rows, acc = refs[-2:]
    step, steps = pl.program_id(0), pl.num_programs(0)
    width = rows.shape[1]
    piece = xs[0].shape[0]

    @pl.when(step == 0)
    def _():
        for b in range(blocks):
            rows[b * piece : (b + 1) * piece, :] = xs[b][:, :width]

    x = rows[...]
    gate = jnp.dot(x, wg[0], preferred_element_type=jnp.float32)
    up = jnp.dot(x, wu[0], preferred_element_type=jnp.float32)
    hidden = (gate / (1.0 + jnp.exp(-gate)) * up).astype(jnp.bfloat16)
    part = jnp.dot(hidden, wd[0], preferred_element_type=jnp.float32)

    @pl.when(step == 0)
    def _():
        acc[...] = part

    @pl.when((step > 0) & (step < steps - 1))
    def _():
        acc[...] += part

    @pl.when(step == steps - 1)
    def _():
        for b in range(blocks):
            meta = xs[b][:, width : width + LANES]
            lane = lax.broadcasted_iota(jnp.int32, meta.shape, 1)
            weight = jnp.where(lane == local_ref[0], meta.astype(jnp.float32), 0.0)
            weight = jnp.sum(weight, axis=1, keepdims=True)
            own = slice(b * piece, (b + 1) * piece)
            outs[b][:, :width] = ((acc[own, :] + part[own, :]) * weight).astype(jnp.bfloat16)
            if outs[b].shape[1] > width:
                outs[b][:, width:] = meta


def experts(xs, marked, local, w_gate, w_up, w_down, tile=256):
    blocks = len(xs)
    piece, wide = xs[0].shape
    width, hidden = w_gate.shape[1:]
    wides = [wide if b in marked else width for b in range(blocks)]
    return pl.pallas_call(
        functools.partial(expert_kernel, blocks),
        grid=(hidden // tile,),
        in_specs=[pl.BlockSpec(memory_space=pltpu.SMEM)]
        + [pl.BlockSpec((piece, wide), lambda i: (0, 0))] * blocks
        + [
            pl.BlockSpec((1, width, tile), lambda i: (0, 0, i)),
            pl.BlockSpec((1, width, tile), lambda i: (0, 0, i)),
            pl.BlockSpec((1, tile, width), lambda i: (0, i, 0)),
        ],
        out_specs=[pl.BlockSpec((piece, w), lambda i: (0, 0)) for w in wides],
        out_shape=[jax.ShapeDtypeStruct((piece, w), jnp.bfloat16) for w in wides],
        scratch_shapes=[
            pltpu.VMEM((blocks * piece, width), jnp.bfloat16),
            pltpu.VMEM((blocks * piece, width), jnp.float32),
        ],
        compiler_params=pltpu.CompilerParams(
            vmem_limit_bytes=EXPERT_VMEM, dimension_semantics=("arbitrary",)
        ),
        cost_estimate=pl.CostEstimate(
            flops=6 * blocks * piece * width * hidden,
            bytes_accessed=6 * width * hidden,
            transcendentals=blocks * piece * hidden,
        ),
    )(local, *xs, w_gate, w_up, w_down)


def whole(kernel, shapes, *arrays):
    moved = sum(x.size * x.dtype.itemsize for x in arrays)
    return pl.pallas_call(
        kernel,
        out_shape=shapes,
        compiler_params=pltpu.CompilerParams(vmem_limit_bytes=VMEM),
        cost_estimate=pl.CostEstimate(flops=10**8, bytes_accessed=3 * moved, transcendentals=0),
    )(*arrays)


def to_tokens(pick, rows):
    return lax.dot_general(pick, rows, (((0,), (0,)), ((), ())), preferred_element_type=jnp.float32)


def scatter_kernel(locals_, first, second, out):
    count, width = out.shape
    total = None
    for rows in (first, second):
        meta = rows[:, width:].astype(jnp.float32)
        lane = lax.broadcasted_iota(jnp.int32, meta.shape, 1)
        token = jnp.sum(jnp.where(lane == locals_, meta, 0.0), axis=1, keepdims=True)
        lane = lax.broadcasted_iota(jnp.int32, (rows.shape[0], count), 1)
        part = to_tokens((lane.astype(jnp.float32) == token).astype(jnp.bfloat16), rows[:, :width])
        total = part if total is None else total + part
    out[...] = total.astype(jnp.bfloat16)


def collect_kernel(pick, first, second, far, out):
    total = to_tokens(pick[:PIECE, :], first[...]) + to_tokens(pick[PIECE:, :], second[...])
    out[...] = (total + far[...].astype(jnp.float32)).astype(jnp.bfloat16)


def per_device(tokens, gate_scores, expert_ids, w_gate, w_up, w_down):
    groups, locals_ = lax.axis_size("node"), lax.axis_size("local")
    local = lax.axis_index("local").astype(jnp.int32).reshape(1)
    tie = lax.optimization_barrier

    def across(block):
        parts = block.reshape(groups, block.shape[0] // groups, block.shape[1])
        return lax.all_to_all(parts, "node", 0, 0, tiled=True).reshape(block.shape)

    def shift(block, by):
        return lax.ppermute(block, "local", [(i, (i + by) % locals_) for i in range(locals_)])

    def up(block):
        return shift(block, 1)

    def down(block):
        return shift(block, -1)

    def add(*blocks):
        total = blocks[0].astype(jnp.float32)
        for block in blocks[1:]:
            total = total + block.astype(jnp.float32)
        return total.astype(jnp.bfloat16)

    run = functools.partial(experts, local=local, w_gate=w_gate, w_up=w_up, w_down=w_down)

    send_a, send_b, pick = prepare(tokens, gate_scores, expert_ids, groups, locals_)
    own_a = across(send_a)
    below_a, above_a = up(own_a), down(own_a)
    send_b, _ = tie((send_b, own_a))
    own_b = across(send_b)
    [own_pa] = run([own_a], ())
    below_a, above_a, next_b, own_pa = tie((below_a, above_a, own_b, own_pa))
    far_a, above_b = up(below_a), down(next_b)
    kept = pltpu.with_memory_space_constraint(next_b, pltpu.VMEM)
    below_pa, above_pa, own_pb = run([below_a, above_a, kept], ())
    far_a, above_b, last_b, below_pa = tie((far_a, above_b, next_b, below_pa))
    below_b, far_b = up(last_b), down(above_b)
    far_pa, above_pb = run([far_a, above_b], (0,))
    below_pa, above_pa, far_pa = tie((below_pa, above_pa, far_pa))
    below_b, far_b, above_pb = tie((below_b, far_b, above_pb))
    kept = [pltpu.with_memory_space_constraint(x, pltpu.VMEM) for x in (below_b, far_b)]
    below_pb, far_pb = run(kept, (1,))

    home_a = across(far_pa)
    from_above, from_below = down(below_pa), up(above_pa)
    far_pb, home_a = tie((far_pb, home_a))
    above_pb, below_pb, from_above, from_below, home_a = tie(
        (above_pb, below_pb, from_above, from_below, home_a)
    )
    home_b = across(far_pb)
    far = whole(
        functools.partial(scatter_kernel, locals_),
        jax.ShapeDtypeStruct(tokens.shape, jnp.bfloat16), home_a,
        pltpu.with_memory_space_constraint(home_b, pltpu.VMEM),
    )
    last_above, last_below = down(below_pb), up(above_pb)
    total_b, far = tie((add(own_pb, last_above, last_below), far))
    far = shift(far, locals_ // 2)

    final_a = across(add(own_pa, from_above, from_below))
    final_b = across(total_b)
    near = [pltpu.with_memory_space_constraint(x, pltpu.VMEM) for x in (final_a, final_b, far)]
    return whole(collect_kernel, jax.ShapeDtypeStruct(tokens.shape, jnp.bfloat16), pick, *near)


def solution(mesh):
    in_specs = (
        P(("dp", "node", "local"), None),
        P(("dp", "node", "local"), None),
        P(("dp", "node", "local"), None),
        P(("node", "local"), None, None),
        P(("node", "local"), None, None),
        P(("node", "local"), None, None),
    )
    out_specs = P(("dp", "node", "local"), None)
    return jax.shard_map(
        per_device, mesh=mesh, in_specs=in_specs, out_specs=out_specs, check_vma=False
    )
```
